32 devices in a mesh: rows: 8 (over z, core), heads: 4 (over y, x).
Axes of the slice: x: 2, y: 2, z: 4, core: 2. Of those that a mesh axis runs over, the one named last changes fastest.
Arguments:
- media: bfloat16 [1024, 32, 1536], P('heads', 'rows'), may hold values from -6 to 6
- latents: float32 [32, 64, 1536], P('rows', 'heads'), may hold values from -6 to 6
- frame_count: int32 [32], P('rows'), may hold values from 1 to 8, as said below
- cotangent: float32 [32, 64, 1536], P('rows', 'heads'), may hold values from -96 to 96
- inward: float32 [2, 3, 1536, 1536], P(None, None, 'rows', 'heads'), may hold values from -0.15625 to 0.15625
- inward_first: float32 [2, 3, 1536, 1536], P(None, None, 'rows', 'heads'), may hold values from -0.00048828125 to 0.00048828125
- inward_second: float32 [2, 3, 1536, 1536], P(None, None, 'rows', 'heads'), may hold values from 1.1037897e-09 to 4.415159e-09
- outward: float32 [2, 1536, 1536], P(None, 'heads', 'rows'), may hold values from -3.5 to 3.5
- outward_first: float32 [2, 1536, 1536], P(None, 'heads', 'rows'), may hold values from -0.00048828125 to 0.00048828125
- outward_second: float32 [2, 1536, 1536], P(None, 'heads', 'rows'), may hold values from 1.1037897e-09 to 4.415159e-09
- widen: float32 [2, 1536, 6144], P(None, 'rows', 'heads'), may hold values from -0.15625 to 0.15625
- widen_first: float32 [2, 1536, 6144], P(None, 'rows', 'heads'), may hold values from -0.00048828125 to 0.00048828125
- widen_second: float32 [2, 1536, 6144], P(None, 'rows', 'heads'), may hold values from 1.1037897e-09 to 4.415159e-09
- narrow: float32 [2, 6144, 1536], P(None, 'heads', 'rows'), may hold values from -0.078125 to 0.078125
- narrow_first: float32 [2, 6144, 1536], P(None, 'heads', 'rows'), may hold values from -0.001953125 to 0.001953125
- narrow_second: float32 [2, 6144, 1536], P(None, 'heads', 'rows'), may hold values from 1.7660636e-08 to 7.064254e-08
- norm_gains: float32 [2, 6, 1536], replicated, may hold values from -1 to 2, as said below
- gain_first: float32 [2, 6, 1536], replicated, may hold values from -0.009765625 to 0.009765625
- gain_second: float32 [2, 6, 1536], replicated, may hold values from 4.4151588e-07 to 1.7660635e-06
Outputs:
- latents_next: float32 [32, 64, 1536], P('rows', 'heads')
- latent_gradient: float32 [32, 64, 1536], P('rows', 'heads')
- media_gradient: float32 [1024, 32, 1536], P('heads', 'rows')
- gradient_norm: float32 [], replicated
- inward_mean: float32 [2, 3, 1536, 1536], P(None, None, 'rows', 'heads')
- inward_square: float32 [2, 3, 1536, 1536], P(None, None, 'rows', 'heads')
- inward_next: float32 [2, 3, 1536, 1536], P(None, None, 'rows', 'heads')
- inward_copy: bfloat16 [2, 3, 1536, 1536], P(None, None, 'rows', 'heads')
- outward_mean: float32 [2, 1536, 1536], P(None, 'heads', 'rows')
- outward_square: float32 [2, 1536, 1536], P(None, 'heads', 'rows')
- outward_next: float32 [2, 1536, 1536], P(None, 'heads', 'rows')
- outward_copy: bfloat16 [2, 1536, 1536], P(None, 'heads', 'rows')
- widen_mean: float32 [2, 1536, 6144], P(None, 'rows', 'heads')
- widen_square: float32 [2, 1536, 6144], P(None, 'rows', 'heads')
- widen_next: float32 [2, 1536, 6144], P(None, 'rows', 'heads')
- widen_copy: bfloat16 [2, 1536, 6144], P(None, 'rows', 'heads')
- narrow_mean: float32 [2, 6144, 1536], P(None, 'heads', 'rows')
- narrow_square: float32 [2, 6144, 1536], P(None, 'heads', 'rows')
- narrow_next: float32 [2, 6144, 1536], P(None, 'heads', 'rows')
- narrow_copy: bfloat16 [2, 6144, 1536], P(None, 'heads', 'rows')
- gain_mean: float32 [2, 6, 1536], replicated
- gain_square: float32 [2, 6, 1536], replicated
- gain_next: float32 [2, 6, 1536], replicated
- feed_norm_gradient: float32 [2, 2, 1536], replicated
The draws below stay inside these ranges and needn't reach their ends.
Inputs may be any that keep to these rules, and one draw needn't show every extreme that they name: `frame_count`: in every run of 4 consecutive videos starting at a multiple of 4, at least one video has 8 frames. `norm_gains`: rows 0, 2 and 4 of each layer are gains, rows 1, 3 and 5 biases.
All inputs are finite; a program needn't handle non-finite values.
Results may differ from the reference program's by a relative error of at most 0.014.
Values may be sent and summed in bfloat16 or wider, within the bound.
A program may use at most 384 MiB of HBM per device.

```python
import math
import jax
import jax.numpy as jnp
from jax import lax

D = 1536
HEADS = 16
HD = 96
NLAT = 64
FF = 6144
LAYERS = 2
FRAMES = 8
STEP = 10
PATCHES = 128
VID_GRP = 4
VIDEOS = 32
POS = 1024


def draw_frame_count(key, part):
    first, second = jax.random.split(key)
    counts = jax.random.randint(first, (VIDEOS,), 1, FRAMES + 1, jnp.int32)
    chosen = jax.random.randint(second, (VIDEOS // VID_GRP,), 0, VID_GRP, jnp.int32)
    place = jnp.arange(VIDEOS, dtype=jnp.int32)
    full = place % VID_GRP == jnp.repeat(chosen, VID_GRP)
    return jnp.where(full, FRAMES, counts).astype(jnp.int32)


def draw_norm_gains(key, part):
    first, second = jax.random.split(key)
    place = jnp.arange(D, dtype=jnp.float32) / (D - 1)
    ramp = 0.6 + 0.5 * place
    rough = jax.random.uniform(first, (LAYERS, 3, D), jnp.float32, 0.7, 1.4)
    shift = jnp.clip(0.3 * jax.random.normal(second, (LAYERS, 3, D), jnp.float32), -1.0, 1.0)
    gain = ramp * rough
    return jnp.stack((gain[:, 0], shift[:, 0], gain[:, 1], shift[:, 1], gain[:, 2], shift[:, 2]), axis=1).astype(jnp.float32)


def draw_cotangent(key, part):
    video_place = jnp.arange(VIDEOS, dtype=jnp.float32) / (VIDEOS - 1)
    slot_place = jnp.arange(NLAT, dtype=jnp.float32) / (NLAT - 1)
    level = video_place[:, None] * slot_place[None, :]
    factor = 1.0 + 15.0 * level * level * level * level
    base = jnp.clip(jax.random.normal(key, (VIDEOS, NLAT, D), jnp.float32), -6.0, 6.0)
    return (base * factor[:, :, None]).astype(jnp.float32)


def steps_of(own_key, extent, pieces, low, top_value):
    level, own = 1.0, jax.random.fold_in(own_key, 6)
    for axis_at, blocks in pieces:
        steps = jnp.exp(jax.random.uniform(jax.random.fold_in(own, axis_at), (blocks,), jnp.float32, low / len(pieces), top_value / len(pieces)))
        level = level * jnp.repeat(steps, extent[axis_at] // blocks).reshape([-1 if axis == axis_at else 1 for axis in range(len(extent))])
    return level


def gaussian(own_key, extent, scale, most, shards=(), kind=jnp.bfloat16):
    factor_of = steps_of(own_key, extent, shards, -0.22, 0.18) if shards else 1.0
    values = jax.random.normal(own_key, extent, jnp.float32) * scale * factor_of
    return jnp.minimum(jnp.maximum(values, -most), most).astype(kind)


def setup_inputs(seed: int = 0) -> dict:
    key_of = jax.random.split(jax.random.key(seed), 20)
    media = gaussian(key_of[0], (POS, VIDEOS, D), 1.0, 6.0, ((0, 4), (1, 8)))
    latents = gaussian(key_of[1], (VIDEOS, NLAT, D), 1.0, 6.0, ((0, 8), (1, 4)), jnp.float32)
    frame_count = draw_frame_count(jax.random.fold_in(key_of[19], 71), 0)
    cotangent = draw_cotangent(jax.random.fold_in(key_of[19], 71), 0)
    inward = gaussian(key_of[4], (LAYERS, 3, D, D), D ** -0.5, 0.15625, ((2, 8), (3, 4)), jnp.float32)
    inward_first = gaussian(key_of[5], (LAYERS, 3, D, D), ((16 * LAYERS * (4 * D * D + 2 * D * FF)) ** -0.5), 0.00048828125, ((2, 8), (3, 4)), jnp.float32)
    inward_second = jnp.clip(jnp.exp(math.log(4.4151589051466544e-09) - 1.3862944 * jax.random.uniform(key_of[6], (LAYERS, 3, D, D), jnp.float32) ** steps_of(key_of[6], (LAYERS, 3, D, D), ((2, 8), (3, 4)), -0.2, 0.2)), 1.1037897262866636e-09, 4.4151589051466544e-09)
    outward = gaussian(key_of[7], (LAYERS, D, D), (max(1, 2 * D // (FRAMES * PATCHES))) ** -0.5, 3.5, ((1, 4), (2, 8)), jnp.float32)
    outward_first = gaussian(key_of[8], (LAYERS, D, D), ((16 * LAYERS * (4 * D * D + 2 * D * FF)) ** -0.5), 0.00048828125, ((1, 4), (2, 8)), jnp.float32)
    outward_second = jnp.clip(jnp.exp(math.log(4.4151589051466544e-09) - 1.3862944 * jax.random.uniform(key_of[9], (LAYERS, D, D), jnp.float32) ** steps_of(key_of[9], (LAYERS, D, D), ((1, 4), (2, 8)), -0.2, 0.2)), 1.1037897262866636e-09, 4.4151589051466544e-09)
    widen = gaussian(key_of[10], (LAYERS, D, FF), D ** -0.5, 0.15625, ((1, 8), (2, 4)), jnp.float32)
    widen_first = gaussian(key_of[11], (LAYERS, D, FF), ((16 * LAYERS * (4 * D * D + 2 * D * FF)) ** -0.5), 0.00048828125, ((1, 8), (2, 4)), jnp.float32)
    widen_second = jnp.clip(jnp.exp(math.log(4.4151589051466544e-09) - 1.3862944 * jax.random.uniform(key_of[12], (LAYERS, D, FF), jnp.float32) ** steps_of(key_of[12], (LAYERS, D, FF), ((1, 8), (2, 4)), -0.2, 0.2)), 1.1037897262866636e-09, 4.4151589051466544e-09)
    narrow = gaussian(key_of[13], (LAYERS, FF, D), FF ** -0.5, 0.078125, ((1, 4), (2, 8)), jnp.float32)
    narrow_first = gaussian(key_of[14], (LAYERS, FF, D), ((LAYERS * (4 * D * D + 2 * D * FF)) ** -0.5), 0.001953125, ((1, 4), (2, 8)), jnp.float32)
    narrow_second = jnp.clip(jnp.exp(math.log(7.064254248234647e-08) - 1.3862944 * jax.random.uniform(key_of[15], (LAYERS, FF, D), jnp.float32) ** steps_of(key_of[15], (LAYERS, FF, D), ((1, 4), (2, 8)), -0.2, 0.2)), 1.7660635620586618e-08, 7.064254248234647e-08)
    norm_gains = draw_norm_gains(jax.random.fold_in(key_of[19], 71), 0)
    gain_first = gaussian(key_of[17], (LAYERS, 6, D), (5 * (LAYERS * (4 * D * D + 2 * D * FF)) ** -0.5), 0.009765625, (), jnp.float32)
    gain_second = jnp.clip(jnp.exp(jax.random.uniform(key_of[18], (LAYERS, 6, D), jnp.float32, math.log(4.415158798565244e-07), math.log(1.7660635194260976e-06))), 4.415158798565244e-07, 1.7660635194260976e-06)
    return {"media": media, "latents": latents, "frame_count": frame_count, "cotangent": cotangent, "inward": inward, "inward_first": inward_first, "inward_second": inward_second, "outward": outward, "outward_first": outward_first, "outward_second": outward_second, "widen": widen, "widen_first": widen_first, "widen_second": widen_second, "narrow": narrow, "narrow_first": narrow_first, "narrow_second": narrow_second, "norm_gains": norm_gains, "gain_first": gain_first, "gain_second": gain_second}


@jax.custom_vjp
def low(v):
    return lax.optimization_barrier(v.astype(jnp.bfloat16)).astype(jnp.float32)

@jax.custom_vjp
def low_back(v):
    return v

def low_keep(v):
    return (low(v), None)

def low_pass(kept, grad):
    return (grad,)

def back_keep(v):
    return (v, None)

def back_low(kept, grad):
    return (low(grad),)
low.defvjp(low_keep, low_pass)
low_back.defvjp(back_keep, back_low)
EPS_NORM = 1e-05
BETA_ONE = 0.5
BETA_TWO = 0.5
ADAM_EPS = 1e-08
WEIGHT_DECAY = 0.1
CLIP_LEVEL = 1.0
MASKED_SCORE = -1e+30
RATE_INWARD = 0.02
RATE_OUTWARD = 0.5
RATE_WIDEN = 0.02
RATE_NARROW = 0.01
RATE_GAINS = 0.1

def layer_norm(rows, gain, shift):
    middle = lax.optimization_barrier(jnp.mean(rows, axis=-1, keepdims=True))
    centred = rows - middle
    spread = lax.optimization_barrier(jnp.mean(centred * centred, axis=-1, keepdims=True))
    return centred * lax.rsqrt(spread + EPS_NORM) * gain + shift

def product(form, left, right):
    return jnp.einsum(form, left, right, precision=lax.Precision.HIGHEST)

def forward_block(params, media_block, latent_block, count_block):
    inward, outward, widen, narrow, norm_gains = params
    inward = low(inward)
    outward = low(outward)
    widen = low(widen)
    narrow = low(narrow)
    batch = media_block.shape[0]
    frame_of = jnp.arange(POS, dtype=jnp.int32) // PATCHES
    live = frame_of[None, :] < count_block[:, None]
    keep_keys = jnp.concatenate((live, jnp.ones((batch, NLAT), dtype=jnp.bool_)), axis=1)[:, None, None, :]
    scale = HD ** (-0.5)
    latent = latent_block
    for layer in range(LAYERS):
        gains = norm_gains[layer]
        media_norm = low(layer_norm(media_block, gains[0], gains[1]))
        latent_norm = low(layer_norm(latent, gains[2], gains[3]))
        query = low_back(low(product('bnd,de->bne', latent_norm, inward[layer, 0])))
        key_media = low_back(low(product('bpd,de->bpe', media_norm, inward[layer, 1])))
        value_media = low_back(low(product('bpd,de->bpe', media_norm, inward[layer, 2])))
        key_latent = low_back(low(product('bnd,de->bne', latent_norm, inward[layer, 1])))
        value_latent = low_back(low(product('bnd,de->bne', latent_norm, inward[layer, 2])))
        keys = jnp.concatenate((key_media, key_latent), axis=1).reshape(batch, POS + NLAT, HEADS, HD)
        values = jnp.concatenate((value_media, value_latent), axis=1).reshape(batch, POS + NLAT, HEADS, HD)
        heads_query = query.reshape(batch, NLAT, HEADS, HD)
        scores = low_back(product('bnhe,bkhe->bhnk', heads_query, keys) * scale)
        scores = jnp.where(keep_keys, scores, MASKED_SCORE)
        top = lax.optimization_barrier(jnp.max(scores, axis=-1, keepdims=True))
        exponent = jnp.exp(scores - top)
        probs = low(exponent / lax.optimization_barrier(jnp.sum(exponent, axis=-1, keepdims=True)))
        mixed = low_back(low(product('bhnk,bkhe->bnhe', probs, values))).reshape(batch, NLAT, D)
        middle = latent + low_back(product('bnd,de->bne', mixed, outward[layer]))
        feed_norm = low(layer_norm(middle, gains[4], gains[5]))
        hidden_pre = low_back(product('bnd,df->bnf', feed_norm, widen[layer]))
        hidden = low(jax.nn.gelu(hidden_pre))
        latent = middle + low_back(product('bnf,fd->bnd', hidden, narrow[layer]))
    return latent

def adam_step(weight, first, second, gradient, rate, decay):
    mean_new = BETA_ONE * first + (1.0 - BETA_ONE) * gradient
    square_new = BETA_TWO * second + (1.0 - BETA_TWO) * gradient * gradient
    mean_hat = mean_new / (1.0 - BETA_ONE ** STEP)
    square_hat = square_new / (1.0 - BETA_TWO ** STEP)
    weight_new = weight - rate * (mean_hat / (jnp.sqrt(square_hat) + ADAM_EPS) + decay * weight)
    return (mean_new, square_new, weight_new)

def reference(media, latents, frame_count, cotangent, inward, inward_first, inward_second, outward, outward_first, outward_second, widen, widen_first, widen_second, narrow, narrow_first, narrow_second, norm_gains, gain_first, gain_second):
    blocks = VIDEOS // 2
    media_blocks = jnp.swapaxes(media.astype(jnp.float32), 0, 1).reshape(blocks, 2, POS, D)
    latent_blocks = latents.reshape(blocks, 2, NLAT, D)
    count_blocks = frame_count.reshape(blocks, 2)

    def whole(params, media_all, latent_all):

        def one_block(parts):
            return forward_block(params, parts[0], parts[1], parts[2])
        return lax.map(jax.checkpoint(one_block), (media_all, latent_all, count_blocks))
    params = (inward, outward, widen, narrow, norm_gains)
    outputs, pullback = jax.vjp(whole, params, media_blocks, latent_blocks)
    grads, media_grads, latent_grads = pullback(cotangent.reshape(blocks, 2, NLAT, D))
    total = jnp.sum(grads[0] * grads[0]) + jnp.sum(grads[1] * grads[1]) + jnp.sum(grads[2] * grads[2])
    total = total + jnp.sum(grads[3] * grads[3]) + jnp.sum(grads[4] * grads[4])
    gradient_norm = jnp.sqrt(total)
    factor = CLIP_LEVEL / jnp.maximum(gradient_norm, CLIP_LEVEL)
    table = ((inward, inward_first, inward_second, RATE_INWARD, WEIGHT_DECAY), (outward, outward_first, outward_second, RATE_OUTWARD, WEIGHT_DECAY), (widen, widen_first, widen_second, RATE_WIDEN, WEIGHT_DECAY), (narrow, narrow_first, narrow_second, RATE_NARROW, WEIGHT_DECAY))
    results = [outputs.reshape(VIDEOS, NLAT, D), latent_grads.reshape(VIDEOS, NLAT, D), jnp.swapaxes(media_grads.reshape(VIDEOS, POS, D), 0, 1), gradient_norm]
    for index in range(4):
        weight, first, second, rate, decay = table[index]
        mean_new, square_new, weight_new = adam_step(weight, first, second, grads[index] * factor, rate, decay)
        results = results + [mean_new, square_new, weight_new, weight_new.astype(jnp.bfloat16)]
    mean_new, square_new, weight_new = adam_step(norm_gains, gain_first, gain_second, grads[4] * factor, RATE_GAINS, 0.0)
    results = results + [mean_new, square_new, weight_new, grads[4][:, 4:6]]
    return tuple(results)
```

```python
import functools

import jax
import jax.numpy as jnp
from jax import lax
from jax.experimental import pallas as pl
from jax.experimental.pallas import tpu as pltpu
from jax.sharding import PartitionSpec as P

HD = 96
STEP = 10
PATCHES = 128


EPS_NORM = 1e-05
BETA_ONE = 0.5
BETA_TWO = 0.5
ADAM_EPS = 1e-08
WEIGHT_DECAY = 0.1
CLIP_LEVEL = 1.0
MASKED_SCORE = -1e30
RATE_INWARD = 0.02
RATE_OUTWARD = 0.5
RATE_WIDEN = 0.02
RATE_NARROW = 0.01
RATE_GAINS = 0.1


def layer_norm(rows, gain, shift):
    middle = jnp.mean(rows, axis=-1, keepdims=True)
    centred = rows - middle
    spread = jnp.mean(centred * centred, axis=-1, keepdims=True)
    return centred * lax.rsqrt(spread + EPS_NORM) * gain + shift


def norm_back(rows, gain, shift, slope):
    _, pullback = jax.vjp(layer_norm, rows, gain, shift)
    return pullback(slope)


def adam_step(weight, first, second, gradient, rate, decay):
    mean_new = BETA_ONE * first + (1.0 - BETA_ONE) * gradient
    square_new = BETA_TWO * second + (1.0 - BETA_TWO) * gradient * gradient
    mean_hat = mean_new / (1.0 - BETA_ONE**STEP)
    square_hat = square_new / (1.0 - BETA_TWO**STEP)
    weight_new = weight - rate * (mean_hat / (jnp.sqrt(square_hat) + ADAM_EPS) + decay * weight)
    return (mean_new, square_new, weight_new)


def gather_slots(rows):
    return lax.all_gather(rows, "heads", axis=1, tiled=True)


def scatter_slots(terms):
    return lax.psum_scatter(terms, "heads", scatter_dimension=1, tiled=True)


def gather_slopes(rows):
    return lax.all_gather(rows, "heads", axis=1, tiled=True)


def scatter_slopes(terms):
    return lax.psum_scatter(terms, "heads", scatter_dimension=1, tiled=True)


def both_scores(query, media_pair, latent_pair, live, scale):
    score_media = (
        jnp.einsum("vnhe,pvhe->vhnp", query, media_pair[0], preferred_element_type=jnp.float32)
        * scale
    )
    score_media = jnp.where(live[:, None, None, :], score_media, MASKED_SCORE)
    score_latent = (
        jnp.einsum("vnhe,vmhe->vhnm", query, latent_pair[0], preferred_element_type=jnp.float32)
        * scale
    )
    return (score_media, score_latent)


def attend(query, media_pair, latent_pair, live, scale):
    score_media, score_latent = both_scores(query, media_pair, latent_pair, live, scale)
    top = jnp.maximum(
        jnp.max(score_media, axis=-1, keepdims=True), jnp.max(score_latent, axis=-1, keepdims=True)
    )
    exponent_media = jnp.exp(score_media - top)
    exponent_latent = jnp.exp(score_latent - top)
    total = jnp.sum(exponent_media, axis=-1, keepdims=True) + jnp.sum(
        exponent_latent, axis=-1, keepdims=True
    )
    share_media = (exponent_media / total).astype(jnp.bfloat16)
    share_latent = (exponent_latent / total).astype(jnp.bfloat16)
    mixed = jnp.einsum(
        "vhnp,pvhe->vnhe", share_media, media_pair[1], preferred_element_type=jnp.float32
    )
    mixed = mixed + jnp.einsum(
        "vhnm,vmhe->vnhe", share_latent, latent_pair[1], preferred_element_type=jnp.float32
    )
    return (mixed.astype(jnp.bfloat16), top + jnp.log(total))


def attend_back(query, media_pair, latent_pair, live, log_total, mixed_slope, scale):
    score_media, score_latent = both_scores(query, media_pair, latent_pair, live, scale)
    share_media = jnp.exp(score_media - log_total)
    share_latent = jnp.exp(score_latent - log_total)
    share_slope_media = jnp.einsum(
        "vnhe,pvhe->vhnp", mixed_slope, media_pair[1], preferred_element_type=jnp.float32
    )
    share_slope_latent = jnp.einsum(
        "vnhe,vmhe->vhnm", mixed_slope, latent_pair[1], preferred_element_type=jnp.float32
    )
    row_total = jnp.sum(share_media * share_slope_media, axis=-1, keepdims=True)
    row_total = row_total + jnp.sum(share_latent * share_slope_latent, axis=-1, keepdims=True)
    score_slope_media = (share_media * (share_slope_media - row_total)).astype(jnp.bfloat16)
    score_slope_latent = (share_latent * (share_slope_latent - row_total)).astype(jnp.bfloat16)
    query_slope = jnp.einsum(
        "vhnp,pvhe->vnhe", score_slope_media, media_pair[0], preferred_element_type=jnp.float32
    )
    query_slope = query_slope + jnp.einsum(
        "vhnm,vmhe->vnhe", score_slope_latent, latent_pair[0], preferred_element_type=jnp.float32
    )
    query_slope = (query_slope * scale).astype(jnp.bfloat16)
    key_media = (
        jnp.einsum("vhnp,vnhe->pvhe", score_slope_media, query, preferred_element_type=jnp.float32)
        * scale
    ).astype(jnp.bfloat16)
    value_media = jnp.einsum(
        "vhnp,vnhe->pvhe",
        share_media.astype(jnp.bfloat16),
        mixed_slope,
        preferred_element_type=jnp.float32,
    ).astype(jnp.bfloat16)
    key_latent = (
        jnp.einsum("vhnm,vnhe->vmhe", score_slope_latent, query, preferred_element_type=jnp.float32)
        * scale
    ).astype(jnp.bfloat16)
    value_latent = jnp.einsum(
        "vhnm,vnhe->vmhe",
        share_latent.astype(jnp.bfloat16),
        mixed_slope,
        preferred_element_type=jnp.float32,
    ).astype(jnp.bfloat16)
    return (query_slope, jnp.stack((key_media, value_media)), jnp.stack((key_latent, value_latent)))


def local_plain(
    media,
    latents,
    frame_count,
    cotangent,
    inward,
    inward_first,
    inward_second,
    outward,
    outward_first,
    outward_second,
    widen,
    widen_first,
    widen_second,
    narrow,
    narrow_first,
    narrow_second,
    norm_gains,
    gain_first,
    gain_second,
):
    heads_count = lax.axis_size("heads")
    layers, _, row_share, head_columns = inward.shape
    local_positions, videos, width = media.shape
    positions = local_positions * heads_count
    latent_count = latents.shape[1] * heads_count
    local_heads = head_columns // HD
    scale = HD ** (-0.5)
    live = (jnp.arange(positions, dtype=jnp.int32) // PATCHES)[None, :] < frame_count[:, None]
    inward_columns, outward_rows, widen_columns, narrow_rows = (
        lax.all_gather(inward.astype(jnp.bfloat16), "rows", axis=2, tiled=True),
        lax.all_gather(outward.astype(jnp.bfloat16), "rows", axis=2, tiled=True),
        lax.all_gather(widen.astype(jnp.bfloat16), "rows", axis=1, tiled=True),
        lax.all_gather(narrow.astype(jnp.bfloat16), "rows", axis=2, tiled=True),
    )
    media_rows = media.astype(jnp.float32)
    latent = latents
    kept = []
    for layer in range(layers):
        gains = norm_gains[layer]
        media_norm = layer_norm(media_rows, gains[0], gains[1]).astype(jnp.bfloat16)
        latent_norm = gather_slots(layer_norm(latent, gains[2], gains[3]).astype(jnp.bfloat16))
        triple = jnp.einsum(
            "vnd,tdc->tvnc", latent_norm, inward_columns[layer], preferred_element_type=jnp.float32
        ).astype(jnp.bfloat16)
        pair_columns = inward_columns[layer, 1:3]
        media_pair = jnp.einsum(
            "pvd,tdc->tpvc",
            lax.all_gather(media_norm, "heads", axis=0, tiled=True),
            pair_columns,
            preferred_element_type=jnp.float32,
        ).astype(jnp.bfloat16)
        query = triple[0].reshape(videos, latent_count, local_heads, HD)
        latent_pair = triple[1:3].reshape(2, videos, latent_count, local_heads, HD)
        heads_pair = media_pair.reshape(2, positions, videos, local_heads, HD)
        mixed, log_total = attend(query, heads_pair, latent_pair, live, scale)
        mixed = mixed.reshape(videos, latent_count, head_columns)
        middle = latent + scatter_slots(
            jnp.einsum(
                "vnc,cd->vnd", mixed, outward_rows[layer], preferred_element_type=jnp.float32
            )
        )
        feed_norm = gather_slots(layer_norm(middle, gains[4], gains[5]).astype(jnp.bfloat16))
        hidden_pre = jnp.einsum(
            "vnd,df->vnf", feed_norm, widen_columns[layer], preferred_element_type=jnp.float32
        )
        hidden = jax.nn.gelu(hidden_pre).astype(jnp.bfloat16)
        kept.append(
            (
                latent,
                middle,
                media_norm,
                latent_norm,
                query,
                heads_pair,
                latent_pair,
                mixed,
                log_total,
                feed_norm,
                hidden_pre,
                hidden,
            )
        )
        latent = middle + scatter_slots(
            jnp.einsum(
                "vnf,fd->vnd", hidden, narrow_rows[layer], preferred_element_type=jnp.float32
            )
        )
    slope = cotangent
    media_slope = jnp.zeros(media_rows.shape, jnp.float32)
    inward_parts, outward_parts, widen_parts, narrow_parts, gain_parts = ([], [], [], [], [])
    for layer in reversed(range(layers)):
        (
            latent_in,
            middle,
            media_norm,
            latent_norm,
            query,
            heads_pair,
            latent_pair,
            mixed,
            log_total,
            feed_norm,
            hidden_pre,
            hidden,
        ) = kept[layer]
        gains = norm_gains[layer]
        feed_slope = gather_slopes(slope.astype(jnp.bfloat16))
        narrow_grad = jnp.einsum(
            "vnf,vnd->fd", hidden, feed_slope, preferred_element_type=jnp.float32
        )
        hidden_slope = jnp.einsum(
            "vnd,fd->vnf", feed_slope, narrow_rows[layer], preferred_element_type=jnp.float32
        )
        _, gelu_back = jax.vjp(jax.nn.gelu, hidden_pre)
        pre_slope = gelu_back(hidden_slope)[0].astype(jnp.bfloat16)
        widen_grad = jnp.einsum(
            "vnd,vnf->df", feed_norm, pre_slope, preferred_element_type=jnp.float32
        )
        norm_slope = scatter_slopes(
            jnp.einsum(
                "vnf,df->vnd", pre_slope, widen_columns[layer], preferred_element_type=jnp.float32
            )
        )
        middle_part, gain_feed, shift_feed = norm_back(middle, gains[4], gains[5], norm_slope)
        middle_slope = slope + middle_part
        branch_slope = gather_slopes(middle_slope.astype(jnp.bfloat16))
        outward_grad = jnp.einsum(
            "vnc,vnd->cd", mixed, branch_slope, preferred_element_type=jnp.float32
        )
        mixed_slope = jnp.einsum(
            "vnd,cd->vnc", branch_slope, outward_rows[layer], preferred_element_type=jnp.float32
        ).astype(jnp.bfloat16)
        mixed_slope = mixed_slope.reshape(videos, latent_count, local_heads, HD)
        query_slope, media_slopes, latent_slopes = attend_back(
            query, heads_pair, latent_pair, live, log_total, mixed_slope, scale
        )
        triple_slope = jnp.concatenate(
            (
                query_slope.reshape(1, videos, latent_count, head_columns),
                latent_slopes.reshape(2, videos, latent_count, head_columns),
            ),
            axis=0,
        )
        inward_grad = jnp.einsum(
            "vnd,tvnc->tdc", latent_norm, triple_slope, preferred_element_type=jnp.float32
        )
        norm_slope = scatter_slopes(
            jnp.einsum(
                "tvnc,tdc->vnd",
                triple_slope,
                inward_columns[layer],
                preferred_element_type=jnp.float32,
            )
        )
        latent_part, gain_latent, shift_latent = norm_back(
            latent_in, gains[2], gains[3], norm_slope
        )
        slope = middle_slope + latent_part
        pair_slope = media_slopes.reshape(2, positions, videos, head_columns)
        media_columns = jnp.einsum(
            "pvd,tpvc->tdc",
            lax.all_gather(media_norm, "heads", axis=0, tiled=True),
            pair_slope,
            preferred_element_type=jnp.float32,
        )
        inward_grad = jnp.concatenate((inward_grad[:1], inward_grad[1:] + media_columns), axis=0)
        pair_columns = inward_columns[layer, 1:3]
        media_norm_slope = lax.psum_scatter(
            jnp.einsum(
                "tpvc,tdc->pvd", pair_slope, pair_columns, preferred_element_type=jnp.float32
            ),
            "heads",
            scatter_dimension=0,
            tiled=True,
        )
        media_part, gain_media, shift_media = norm_back(
            media_rows, gains[0], gains[1], media_norm_slope
        )
        media_slope = media_slope + media_part
        inward_parts.append(inward_grad)
        outward_parts.append(outward_grad)
        widen_parts.append(widen_grad)
        narrow_parts.append(narrow_grad)
        gain_parts.append(
            jnp.stack((gain_media, shift_media, gain_latent, shift_latent, gain_feed, shift_feed))
        )
    inward_grad, outward_grad, widen_grad, narrow_grad = (
        lax.psum_scatter(jnp.stack(inward_parts[::-1]), "rows", scatter_dimension=2, tiled=True),
        lax.psum_scatter(jnp.stack(outward_parts[::-1]), "rows", scatter_dimension=2, tiled=True),
        lax.psum_scatter(jnp.stack(widen_parts[::-1]), "rows", scatter_dimension=1, tiled=True),
        lax.psum_scatter(jnp.stack(narrow_parts[::-1]), "rows", scatter_dimension=2, tiled=True),
    )
    squares = jnp.sum(inward_grad * inward_grad) + jnp.sum(outward_grad * outward_grad)
    squares = squares + jnp.sum(widen_grad * widen_grad) + jnp.sum(narrow_grad * narrow_grad)
    gain_total, square_total = lax.psum((jnp.stack(gain_parts[::-1]), squares), ("rows", "heads"))
    gradient_norm = jnp.sqrt(square_total + jnp.sum(gain_total * gain_total))
    factor = CLIP_LEVEL / jnp.maximum(gradient_norm, CLIP_LEVEL)
    table = (
        (inward, inward_first, inward_second, inward_grad, RATE_INWARD, WEIGHT_DECAY),
        (outward, outward_first, outward_second, outward_grad, RATE_OUTWARD, WEIGHT_DECAY),
        (widen, widen_first, widen_second, widen_grad, RATE_WIDEN, WEIGHT_DECAY),
        (narrow, narrow_first, narrow_second, narrow_grad, RATE_NARROW, WEIGHT_DECAY),
    )
    results = [latent, slope, media_slope, gradient_norm]
    for weight, first, second, gradient, rate, decay in table:
        mean_new, square_new, weight_new = adam_step(
            weight, first, second, gradient * factor, rate, decay
        )
        results = results + [mean_new, square_new, weight_new, weight_new.astype(jnp.bfloat16)]
    mean_new, square_new, weight_new = adam_step(
        norm_gains, gain_first, gain_second, gain_total * factor, RATE_GAINS, 0.0
    )
    results = results + [mean_new, square_new, weight_new, gain_total[:, 4:6]]
    return tuple(results)


BF = jnp.bfloat16
F32 = jnp.float32
VMEM_LIMIT = 60 * 1024 * 1024
NT = (((1,), (1,)), ((), ()))
TN = (((0,), (0,)), ((), ()))
X_SWAP = ((0, 1), (1, 0), (2, 3), (3, 2))
Y_SWAP = ((0, 2), (2, 0), (1, 3), (3, 1))


def vmem_spec():
    return pl.BlockSpec(memory_space=pltpu.VMEM)


def mm(left, right, dims=None, out=BF):
    dims = dims or (((1,), (0,)), ((), ()))
    return lax.dot_general(left, right, dims, preferred_element_type=F32).astype(out)


def media_kernel(first_ref, second_ref, gain_ref, weight_ref, *rest):
    keys_ref, hat_ref, rows_ref = rest[-3:]
    half, layer = pl.program_id(0), pl.program_id(1)

    @pl.when(layer == 0)
    def _():
        @pl.when(half == 0)
        def _():
            rows_ref[...] = first_ref[...].astype(F32).reshape(rows_ref.shape)

        @pl.when(half == 1)
        def _():
            rows_ref[...] = second_ref[...].astype(F32).reshape(rows_ref.shape)

        rows = rows_ref[...]
        centred = rows - jnp.mean(rows, axis=-1, keepdims=True)
        spread = jnp.mean(centred * centred, axis=-1, keepdims=True)
        hat = centred * lax.rsqrt(spread + EPS_NORM)
        rows_ref[...] = hat
        hat_ref[...] = hat.astype(BF).reshape(hat_ref.shape)

    gain = gain_ref[pl.ds(layer, 1), 0]
    shift = gain_ref[pl.ds(layer, 1), 1]
    normed = (rows_ref[...] * gain + shift).astype(BF)
    keys_ref[...] = jnp.dot(normed, weight_ref[...], preferred_element_type=F32).astype(BF).reshape(keys_ref.shape)


def media_part(first, second, gains, weight, group, earlier):
    videos, patches, width = first.shape
    columns = weight.shape[1]
    kinds = (
        jax.ShapeDtypeStruct((8, videos, patches, columns), BF),
        jax.ShapeDtypeStruct((8, videos, patches, width), BF),
    )
    whole = pl.BlockSpec((videos, patches, width), lambda i, j: (0, 0, 0))
    in_specs = [
        whole,
        whole,
        pl.BlockSpec(gains.shape, lambda i, j: (0, 0, 0)),
        pl.BlockSpec((width, columns // 2), lambda i, j: (0, j)),
    ]
    aliases = {}
    if earlier:
        in_specs += [pl.BlockSpec(memory_space=pl.ANY)] * 2
        aliases = {4: 0, 5: 1}
    rows = videos * patches
    return pl.pallas_call(
        media_kernel,
        grid=(2, 2),
        out_shape=kinds,
        in_specs=in_specs,
        out_specs=(
            pl.BlockSpec((1, videos, patches, columns // 2), lambda i, j: (2 * group + i, 0, 0, j)),
            pl.BlockSpec((1, videos, patches, width), lambda i, j: (2 * group + i, 0, 0, 0)),
        ),
        scratch_shapes=[pltpu.VMEM((rows, width), F32)],
        input_output_aliases=aliases,
        compiler_params=pltpu.CompilerParams(vmem_limit_bytes=VMEM_LIMIT),
        cost_estimate=pl.CostEstimate(
            flops=4 * rows * width * columns, bytes_accessed=8 * rows * width, transcendentals=0
        ),
        name="media_part",
    )(first, second, gains, weight, *earlier)


def head_mask(rows, columns, head):
    place = lax.broadcasted_iota(jnp.int32, (rows, columns), 1)
    return (place >= head * HD) & (place < (head + 1) * HD)


def spread_heads(rows):
    heads = rows.shape[1] // HD
    zero = jnp.zeros_like(rows)
    return jnp.concatenate(
        [jnp.where(head_mask(*rows.shape, head), rows, zero) for head in range(heads)], axis=0
    )


def gather_heads(rows, count):
    heads = rows.shape[1] // HD
    total = jnp.zeros((count, rows.shape[1]), F32)
    for head in range(heads):
        part = rows[head * count : (head + 1) * count]
        total = total + jnp.where(head_mask(*part.shape, head), part, 0.0)
    return total


def attend_kernel(live_ref, query_ref, latent_key_ref, latent_value_ref, key_ref, value_ref, mixed_ref, *, scale):
    video = pl.program_id(0)
    slots, patches = key_ref.shape[0], key_ref.shape[2]
    query = spread_heads(query_ref[...])
    rows, columns = query.shape
    place = lax.broadcasted_iota(jnp.int32, (rows, 2 * patches), 1)
    scores = []
    for pair in range(slots // 2):
        keys = key_ref[2 * pair : 2 * pair + 2, 0].reshape(2 * patches, columns)
        score = lax.dot_general(query, keys, NT, preferred_element_type=F32) * scale
        live = jnp.where(place < patches, live_ref[video, 2 * pair], live_ref[video, 2 * pair + 1])
        scores.append(jnp.where(live > 0, score, MASKED_SCORE))
    scores.append(lax.dot_general(query, latent_key_ref[...], NT, preferred_element_type=F32) * scale)
    top = functools.reduce(jnp.maximum, [jnp.max(score, axis=-1, keepdims=True) for score in scores])
    exponents = [jnp.exp(score - top) for score in scores]
    total = functools.reduce(jnp.add, [jnp.sum(e, axis=-1, keepdims=True) for e in exponents])
    mixed = jnp.zeros((rows, columns), F32)
    for pair in range(slots // 2):
        values = value_ref[2 * pair : 2 * pair + 2, 0].reshape(2 * patches, columns)
        mixed = mixed + jnp.dot((exponents[pair] / total).astype(BF), values, preferred_element_type=F32)
    mixed = mixed + jnp.dot(
        (exponents[-1] / total).astype(BF), latent_value_ref[...], preferred_element_type=F32
    )
    mixed_ref[...] = gather_heads(mixed, query_ref.shape[0]).astype(BF)


def attend_fast(live, query, latent_pair, keys, layer, scale):
    slots, videos, patches, _ = keys.shape
    count, columns = query.shape[0] // videos, query.shape[1]
    row_block = pl.BlockSpec((count, columns), lambda v: (v, 0))
    return pl.pallas_call(
        functools.partial(attend_kernel, scale=scale),
        grid=(videos,),
        out_shape=jax.ShapeDtypeStruct(query.shape, BF),
        in_specs=[
            pl.BlockSpec(memory_space=pltpu.SMEM),
            row_block,
            row_block,
            pl.BlockSpec((count, columns), lambda v: (v, 1)),
            pl.BlockSpec((slots, 1, patches, columns), lambda v: (0, v, 0, 2 * layer)),
            pl.BlockSpec((slots, 1, patches, columns), lambda v: (0, v, 0, 2 * layer + 1)),
        ],
        out_specs=row_block,
        compiler_params=pltpu.CompilerParams(vmem_limit_bytes=VMEM_LIMIT),
        cost_estimate=pl.CostEstimate(
            flops=8 * slots * patches * videos * count * 2 * columns,
            bytes_accessed=4 * slots * videos * patches * columns,
            transcendentals=slots * patches * videos * count * 4,
        ),
        name="attend",
    )(live, query, latent_pair, latent_pair, keys, keys)


def attend_back_kernel(
    live_ref, query_ref, latent_key_ref, latent_value_ref, key_ref, value_ref, slope_ref, *rest, scale
):
    query_slope_ref, latent_slope_ref, media_slope_ref = rest[-3:]
    video = pl.program_id(0)
    slots, patches = key_ref.shape[0], key_ref.shape[2]
    pairs = slots // 2
    count = query_ref.shape[0]
    query, slope = spread_heads(query_ref[...]), spread_heads(slope_ref[...])
    rows, columns = query.shape
    place = lax.broadcasted_iota(jnp.int32, (2 * patches, rows), 0)

    def keys_of(ref, pair):
        return ref[2 * pair : 2 * pair + 2, 0].reshape(2 * patches, columns)

    scores = []
    for pair in range(pairs):
        score = lax.dot_general(keys_of(key_ref, pair), query, NT, preferred_element_type=F32) * scale
        live = jnp.where(place < patches, live_ref[video, 2 * pair], live_ref[video, 2 * pair + 1])
        scores.append(jnp.where(live > 0, score, MASKED_SCORE))
    scores.append(lax.dot_general(latent_key_ref[...], query, NT, preferred_element_type=F32) * scale)
    top = functools.reduce(jnp.maximum, [jnp.max(score, axis=0, keepdims=True) for score in scores])
    exponents = [jnp.exp(score - top) for score in scores]
    total = functools.reduce(jnp.add, [jnp.sum(e, axis=0, keepdims=True) for e in exponents])
    shares = [e / total for e in exponents]
    share_slopes = [
        lax.dot_general(keys_of(value_ref, pair), slope, NT, preferred_element_type=F32)
        for pair in range(pairs)
    ]
    share_slopes.append(
        lax.dot_general(latent_value_ref[...], slope, NT, preferred_element_type=F32)
    )
    row_total = functools.reduce(
        jnp.add,
        [jnp.sum(a * b, axis=0, keepdims=True) for a, b in zip(shares, share_slopes)],
    )
    query_slope = jnp.zeros((rows, columns), F32)
    for at in range(pairs + 1):
        keys = keys_of(key_ref, at) if at < pairs else latent_key_ref[...]
        score_slope = (shares[at] * (share_slopes[at] - row_total)).astype(BF)
        key_slope = (jnp.dot(score_slope, query, preferred_element_type=F32) * scale).astype(BF)
        value_slope = jnp.dot(shares[at].astype(BF), slope, preferred_element_type=F32).astype(BF)
        query_slope = query_slope + lax.dot_general(
            score_slope, keys, TN, preferred_element_type=F32
        )
        if at < pairs:
            media_slope_ref[2 * at : 2 * at + 2, 0, :, :columns] = key_slope.reshape(2, patches, columns)
            media_slope_ref[2 * at : 2 * at + 2, 0, :, columns:] = value_slope.reshape(2, patches, columns)
        else:
            latent_slope_ref[:, :columns] = key_slope
            latent_slope_ref[:, columns:] = value_slope
    query_slope_ref[...] = (gather_heads(query_slope, count) * scale).astype(BF)


def attend_back_fast(live, query, latent_pair, keys, slope, layer, scale, earlier):
    slots, videos, patches, _ = keys.shape
    count, columns = query.shape[0] // videos, query.shape[1]
    row_block = pl.BlockSpec((count, columns), lambda v: (v, 0))
    in_specs = [
        pl.BlockSpec(memory_space=pltpu.SMEM),
        row_block,
        row_block,
        pl.BlockSpec((count, columns), lambda v: (v, 1)),
        pl.BlockSpec((slots, 1, patches, columns), lambda v: (0, v, 0, 2 * layer)),
        pl.BlockSpec((slots, 1, patches, columns), lambda v: (0, v, 0, 2 * layer + 1)),
        row_block,
    ]
    aliases = {}
    if earlier:
        in_specs += [pl.BlockSpec(memory_space=pl.ANY)]
        aliases = {7: 2}
    return pl.pallas_call(
        functools.partial(attend_back_kernel, scale=scale),
        grid=(videos,),
        out_shape=(
            jax.ShapeDtypeStruct(query.shape, BF),
            jax.ShapeDtypeStruct(latent_pair.shape, BF),
            jax.ShapeDtypeStruct(keys.shape, BF),
        ),
        in_specs=in_specs,
        out_specs=(
            row_block,
            pl.BlockSpec((count, 2 * columns), lambda v: (v, 0)),
            pl.BlockSpec((slots, 1, patches, 2 * columns), lambda v: (0, v, 0, layer)),
        ),
        input_output_aliases=aliases,
        compiler_params=pltpu.CompilerParams(vmem_limit_bytes=VMEM_LIMIT),
        cost_estimate=pl.CostEstimate(
            flops=20 * slots * patches * videos * count * 2 * columns,
            bytes_accessed=8 * slots * videos * patches * columns,
            transcendentals=slots * patches * videos * count * 4,
        ),
        name="attend_back",
    )(live, query, latent_pair, latent_pair, keys, keys, slope, *earlier)


def greet(count):
    me = lax.axis_index("heads")
    barrier = pltpu.get_barrier_semaphore()
    for step in range(1, count):
        pl.semaphore_signal(barrier, inc=1, device_id={"heads": (me + step) % count})
    pl.semaphore_wait(barrier, count - 1)
    return me


def own_rows(ref, place, share):
    return ref.at[:, pl.ds(pl.multiple_of(place * share, share), share), :]


def start_gather(me, count, share, own_ref, full_ref, send_sem, recv_sem):
    copies = []
    for step in range(1, count):
        copy = pltpu.make_async_remote_copy(
            src_ref=own_ref,
            dst_ref=own_rows(full_ref, me, share),
            send_sem=send_sem.at[step - 1],
            recv_sem=recv_sem.at[step - 1],
            device_id={"heads": (me + step) % count},
        )
        copy.start()
        copies.append(copy)
    return copies


def start_scatter(me, count, share, part_ref, landed_ref, send_sem, recv_sem):
    copies = []
    for step in range(1, count):
        peer = (me + step) % count
        copy = pltpu.make_async_remote_copy(
            src_ref=own_rows(part_ref, peer, share),
            dst_ref=landed_ref.at[step - 1],
            send_sem=send_sem.at[step - 1],
            recv_sem=recv_sem.at[step - 1],
            device_id={"heads": peer},
        )
        copy.start()
        copies.append(copy)
    return copies


def gather_kernel(count, arrays, *refs):
    own, full = refs[:arrays], refs[arrays : 2 * arrays]
    sems = refs[2 * arrays :]
    me = greet(count)
    share = own[0].shape[1]
    copies = []
    for at in range(arrays):
        copies += start_gather(me, count, share, own[at], full[at], sems[2 * at], sems[2 * at + 1])
        full[at][:, pl.ds(pl.multiple_of(me * share, share), share), :] = own[at][...]
    for copy in copies:
        copy.wait()


def gather_fast(arrays, count):
    videos, share, width = arrays[0].shape
    kind = jax.ShapeDtypeStruct((videos, share * count, width), arrays[0].dtype)
    number = len(arrays)
    return pl.pallas_call(
        functools.partial(gather_kernel, count, number),
        out_shape=(kind,) * number,
        in_specs=[vmem_spec()] * number,
        out_specs=(vmem_spec(),) * number,
        scratch_shapes=[pltpu.SemaphoreType.DMA((count - 1,))] * (2 * number),
        compiler_params=pltpu.CompilerParams(
            collective_id=1, has_side_effects=True, vmem_limit_bytes=VMEM_LIMIT
        ),
        cost_estimate=pl.CostEstimate(flops=0, bytes_accessed=30 * 1000 * 1000, transcendentals=0),
        name="gather_latents",
    )(*arrays)


def forward_kernel(
    count, last, part_ref, rest_ref, gain_ref, new_ref, *refs
):
    refs = list(refs)
    full_ref = None if last else refs.pop(0)
    landed_ref, own_ref, send_sem, recv_sem, send_more, recv_more = refs
    me = greet(count)
    share = rest_ref.shape[1]
    copies = start_scatter(me, count, share, part_ref, landed_ref, send_sem, recv_sem)
    mine = pl.ds(pl.multiple_of(me * share, share), share)
    total = rest_ref[...] + part_ref[:, mine, :].astype(F32)
    for step, copy in enumerate(copies):
        copy.wait_recv()
        total = total + landed_ref[step].astype(F32)
    new_ref[...] = total
    if not last:
        own_ref[...] = layer_norm(total, gain_ref[0], gain_ref[1]).astype(BF)
        more = start_gather(me, count, share, own_ref, full_ref, send_more, recv_more)
        full_ref[:, mine, :] = own_ref[...]
        for copy in more:
            copy.wait()
    for copy in copies:
        copy.wait_send()


def forward_exchange(part, rest, gain, count, last=False):
    videos, share, width = rest.shape
    outs = [jax.ShapeDtypeStruct(rest.shape, F32)]
    if not last:
        outs.append(jax.ShapeDtypeStruct(part.shape, BF))
    got = pl.pallas_call(
        functools.partial(forward_kernel, count, last),
        out_shape=tuple(outs),
        in_specs=[vmem_spec()] * 3,
        out_specs=(vmem_spec(),) * len(outs),
        scratch_shapes=[
            pltpu.VMEM((count - 1, videos, share, width), BF),
            pltpu.VMEM((videos, share, width), BF),
        ]
        + [pltpu.SemaphoreType.DMA((count - 1,))] * 4,
        compiler_params=pltpu.CompilerParams(
            collective_id=3 if last else 2, has_side_effects=True, vmem_limit_bytes=VMEM_LIMIT
        ),
        cost_estimate=pl.CostEstimate(flops=0, bytes_accessed=50 * 1000 * 1000, transcendentals=0),
        name="forward_exchange",
    )(part, rest, gain)
    return got if not last else (got[0], None)


def backward_kernel(
    count, last, part_ref, rows_ref, rest_ref, gain_ref, new_ref, sums_ref, *refs
):
    refs = list(refs)
    full_ref = None if last else refs.pop(0)
    landed_ref, own_ref, send_sem, recv_sem, send_more, recv_more = refs
    me = greet(count)
    share = rest_ref.shape[1]
    copies = start_scatter(me, count, share, part_ref, landed_ref, send_sem, recv_sem)
    mine = pl.ds(pl.multiple_of(me * share, share), share)
    rows = rows_ref[...]
    centred = rows - jnp.mean(rows, axis=-1, keepdims=True)
    scale = lax.rsqrt(jnp.mean(centred * centred, axis=-1, keepdims=True) + EPS_NORM)
    hat = centred * scale
    slope = part_ref[:, mine, :].astype(F32)
    for step, copy in enumerate(copies):
        copy.wait_recv()
        slope = slope + landed_ref[step].astype(F32)
    hat_slope = slope * gain_ref[0]
    back = hat_slope - jnp.mean(hat_slope, axis=-1, keepdims=True)
    back = back - hat * jnp.mean(hat_slope * hat, axis=-1, keepdims=True)
    new = rest_ref[...] + back * scale
    new_ref[...] = new
    if not last:
        own_ref[...] = new.astype(BF)
        more = start_gather(me, count, share, own_ref, full_ref, send_more, recv_more)
        full_ref[:, mine, :] = own_ref[...]
    sums_ref[0:1] = jnp.sum(jnp.sum(slope * hat, axis=0), axis=0, keepdims=True)
    sums_ref[1:2] = jnp.sum(jnp.sum(slope, axis=0), axis=0, keepdims=True)
    if not last:
        for copy in more:
            copy.wait()
    for copy in copies:
        copy.wait_send()


def backward_exchange(part, rows, rest, gain, count, last=False):
    videos, share, width = rest.shape
    outs = [jax.ShapeDtypeStruct(rest.shape, F32), jax.ShapeDtypeStruct((2, width), F32)]
    if not last:
        outs.append(jax.ShapeDtypeStruct(part.shape, BF))
    got = pl.pallas_call(
        functools.partial(backward_kernel, count, last),
        out_shape=tuple(outs),
        in_specs=[vmem_spec()] * 4,
        out_specs=(vmem_spec(),) * len(outs),
        scratch_shapes=[
            pltpu.VMEM((count - 1, videos, share, width), BF),
            pltpu.VMEM((videos, share, width), BF),
        ]
        + [pltpu.SemaphoreType.DMA((count - 1,))] * 4,
        compiler_params=pltpu.CompilerParams(
            collective_id=5 if last else 4, has_side_effects=True, vmem_limit_bytes=VMEM_LIMIT
        ),
        cost_estimate=pl.CostEstimate(flops=0, bytes_accessed=50 * 1000 * 1000, transcendentals=0),
        name="backward_exchange",
    )(part, rows, rest, gain)
    return got if not last else (*got, None)


def sum_kernel(heads, rows, term_ref, out_ref, plane_ref, line_ref, send_sem, recv_sem, send_more, recv_more):
    me_head, me_row = lax.axis_index("heads"), lax.axis_index("rows")
    barrier = pltpu.get_barrier_semaphore()
    for step in range(1, heads):
        pl.semaphore_signal(barrier, inc=1, device_id={"heads": (me_head + step) % heads})
    for step in range(1, rows):
        pl.semaphore_signal(barrier, inc=1, device_id={"rows": (me_row + step) % rows})
    pl.semaphore_wait(barrier, heads - 1 + rows - 1)

    def spread(axis, me, count, source, slots_ref, send, recv):
        copies = []
        for step in range(1, count):
            copy = pltpu.make_async_remote_copy(
                src_ref=source,
                dst_ref=slots_ref.at[me],
                send_sem=send.at[step - 1],
                recv_sem=recv.at[step - 1],
                device_id={axis: (me + step) % count},
            )
            copy.start()
            copies.append(copy)
        slots_ref[pl.ds(me, 1)] = source[...][None]
        for copy in copies:
            copy.wait()
        total = slots_ref[0]
        for at in range(1, count):
            total = total + slots_ref[at]
        return total

    out_ref[...] = spread("heads", me_head, heads, term_ref, plane_ref, send_sem, recv_sem)
    total = spread("rows", me_row, rows, out_ref, line_ref, send_more, recv_more)
    out_ref[...] = total


def sum_fast(term, heads, rows, identity):
    return pl.pallas_call(
        functools.partial(sum_kernel, heads, rows),
        out_shape=jax.ShapeDtypeStruct(term.shape, F32),
        in_specs=[vmem_spec()],
        out_specs=vmem_spec(),
        scratch_shapes=[
            pltpu.VMEM((heads, *term.shape), F32),
            pltpu.VMEM((rows, *term.shape), F32),
            pltpu.SemaphoreType.DMA((heads - 1,)),
            pltpu.SemaphoreType.DMA((heads - 1,)),
            pltpu.SemaphoreType.DMA((rows - 1,)),
            pltpu.SemaphoreType.DMA((rows - 1,)),
        ],
        compiler_params=pltpu.CompilerParams(
            collective_id=identity, has_side_effects=True, vmem_limit_bytes=VMEM_LIMIT
        ),
        cost_estimate=pl.CostEstimate(flops=0, bytes_accessed=20 * 1000 * 1000, transcendentals=0),
        name="sum_over_all",
    )(term)


def flat(rows):
    return rows.reshape(-1, rows.shape[-1])


def local_fast(
    media,
    latents,
    frame_count,
    cotangent,
    inward,
    inward_first,
    inward_second,
    outward,
    outward_first,
    outward_second,
    widen,
    widen_first,
    widen_second,
    narrow,
    narrow_first,
    narrow_second,
    norm_gains,
    gain_first,
    gain_second,
):
    heads_count, rows_count = lax.axis_size("heads"), lax.axis_size("rows")
    me = lax.axis_index("heads")
    layers, _, row_share, head_columns = inward.shape
    local_positions, videos, width = media.shape
    latent_count = latents.shape[1] * heads_count
    scale = HD ** (-0.5)

    def swap_x(rows):
        return lax.ppermute(rows, "heads", X_SWAP)

    def swap_y(rows):
        return lax.ppermute(rows, "heads", Y_SWAP)

    def gather_rows(rows):
        return lax.all_gather(rows, "rows", axis=0, tiled=True)

    outward_t, narrow_t = (jnp.swapaxes(outward, 1, 2), jnp.swapaxes(narrow, 1, 2))
    pair_weights = gather_rows(
        jnp.concatenate([inward[l, t].astype(BF) for l in range(layers) for t in (1, 2)], axis=1)
    )
    query_out, widen_full, narrow_full = [], [], []
    for layer in range(layers):
        query_out.append(
            gather_rows(jnp.concatenate((inward[layer, 0], outward_t[layer]), axis=1).astype(BF))
        )
        widen_full.append(gather_rows(widen[layer].astype(BF)))
        narrow_full.append(gather_rows(narrow_t[layer].astype(BF)))

    own = jnp.swapaxes(media, 0, 1).reshape(videos, 2, local_positions // 2, width)
    own = (own[:, 0], own[:, 1])
    from_x = (swap_x(own[0]), swap_x(own[1]))
    from_y = (swap_y(own[0]), swap_y(own[1]))
    from_far = (swap_x(from_y[0]), swap_y(from_x[1]))
    frames = jnp.stack([2 * (me ^ group) + half for group in range(4) for half in range(2)])
    live = (frames[None, :] < frame_count[:, None]).astype(jnp.int32)
    made = ()
    media_gains = norm_gains[:, 0:2]
    for group, parts in enumerate((own, from_x, from_y, from_far)):
        made = media_part(parts[0], parts[1], media_gains, pair_weights, group, made)
    keys, media_hat = made

    latent = latents
    normed = layer_norm(latent, norm_gains[0, 2], norm_gains[0, 3]).astype(BF)
    latent_norm, feed_slope = gather_fast((normed, cotangent.astype(BF)), heads_count)
    kept = []
    for layer in range(layers):
        query_weight, out_weight = query_out[layer][:, :head_columns], query_out[layer][:, head_columns:]
        pair_weight = pair_weights[:, 2 * layer * head_columns : 2 * (layer + 1) * head_columns]
        query = mm(flat(latent_norm), query_weight)
        latent_pair = mm(flat(latent_norm), pair_weight)
        mixed = attend_fast(live, query, latent_pair, keys, layer, scale)
        part = mm(mixed, out_weight, NT).reshape(videos, latent_count, width)
        middle, feed_norm = forward_exchange(part, latent, norm_gains[layer, 4:6], heads_count)
        hidden_pre = mm(flat(feed_norm), widen_full[layer], None, F32)
        hidden = jax.nn.gelu(hidden_pre).astype(BF)
        part = mm(hidden, narrow_full[layer], NT).reshape(videos, latent_count, width)
        last = layer == layers - 1
        gain = norm_gains[0 if last else layer + 1, 2:4]
        kept.append((latent, middle, latent_norm, query, latent_pair, mixed, feed_norm, hidden_pre, hidden))
        latent, latent_norm = forward_exchange(part, middle, gain, heads_count, last)

    slope = cotangent
    gain_parts = [None] * layers
    shares = [None] * layers
    media_slopes = ()

    def scatter_rows(gradient):
        return lax.psum_scatter(gradient, "rows", scatter_dimension=0, tiled=True)

    for layer in reversed(range(layers)):
        latent_in, middle, latent_norm, query, latent_pair, mixed, feed_norm, hidden_pre, hidden = kept[layer]
        query_weight, out_weight = query_out[layer][:, :head_columns], query_out[layer][:, head_columns:]
        pair_weight = pair_weights[:, 2 * layer * head_columns : 2 * (layer + 1) * head_columns]
        feed_slope = flat(feed_slope)
        narrow_grad = scatter_rows(mm(feed_slope, hidden, TN))
        hidden_slope = mm(feed_slope, narrow_full[layer], None, F32)
        _, gelu_back = jax.vjp(jax.nn.gelu, hidden_pre)
        pre_slope = gelu_back(hidden_slope)[0].astype(BF)
        part = mm(pre_slope, widen_full[layer], NT).reshape(videos, latent_count, width)
        middle_slope, feed_sums, branch_slope = backward_exchange(
            part, middle, slope, norm_gains[layer, 4:6], heads_count
        )
        widen_grad = scatter_rows(mm(flat(feed_norm), pre_slope, TN))
        branch_slope = flat(branch_slope)
        mixed_slope = mm(branch_slope, out_weight)
        out_grad = mm(branch_slope, mixed, TN)
        query_slope, latent_slopes, media_slopes = attend_back_fast(
            live, query, latent_pair, keys, mixed_slope, layer, scale, (media_slopes,) if layer < layers - 1 else ()
        )
        part = (mm(query_slope, query_weight, NT, F32) + mm(latent_slopes, pair_weight, NT, F32)).astype(BF)
        part = part.reshape(videos, latent_count, width)
        last = layer == 0
        slope, latent_sums, feed_slope = backward_exchange(
            part, latent_in, middle_slope, norm_gains[layer, 2:4], heads_count, last
        )
        query_grad = mm(flat(latent_norm), query_slope, TN)
        pair_slope = flat(media_slopes[..., 2 * layer * head_columns : 2 * (layer + 1) * head_columns])
        hat_grad = mm(flat(media_hat), pair_slope, TN, F32)
        slope_sum = jnp.sum(pair_slope.astype(F32), axis=0)
        gain, shift = norm_gains[layer, 0], norm_gains[layer, 1]
        pair_grad = (
            mm(flat(latent_norm), latent_slopes, TN, F32)
            + gain[:, None] * hat_grad
            + shift[:, None] * slope_sum[None, :]
        ).astype(BF)
        wide = pair_weight.astype(F32)
        media_sums = jnp.stack(
            (jnp.sum(wide * hat_grad, axis=1), jnp.sum(wide * slope_sum[None, :], axis=1))
        )
        inward_grad = scatter_rows(jnp.concatenate((out_grad, query_grad, pair_grad), axis=1))
        shares[layer] = (narrow_grad, widen_grad, inward_grad)
        gain_parts[layer] = jnp.concatenate((media_sums, latent_sums, feed_sums), axis=0)

    scaled = jnp.concatenate(
        [
            (
                pair_weights[:, 2 * l * head_columns : 2 * (l + 1) * head_columns].astype(F32)
                * norm_gains[l, 0][:, None]
            ).astype(BF)
            for l in range(layers)
        ],
        axis=1,
    )

    def hat_slope(group, half):
        return mm(flat(media_slopes[2 * group + half]), scaled, NT).reshape(videos, -1, width)

    over_x = swap_x(hat_slope(3, 0))
    over_y = swap_y(hat_slope(3, 1))
    back = [hat_slope(0, 0).astype(F32), hat_slope(0, 1).astype(F32)]
    in_x = [swap_x(hat_slope(1, 0)), None]
    in_y = [None, swap_y(hat_slope(2, 1))]
    in_x[1] = swap_x(hat_slope(1, 1) + over_y)
    in_y[0] = swap_y(hat_slope(2, 0) + over_x)
    pieces = []
    for half in range(2):
        total = back[half] + in_x[half].astype(F32) + in_y[half].astype(F32)
        rows = own[half].astype(F32)
        centred = rows - jnp.mean(rows, axis=-1, keepdims=True)
        spread = lax.rsqrt(jnp.mean(centred * centred, axis=-1, keepdims=True) + EPS_NORM)
        hat = centred * spread
        total = total - jnp.mean(total, axis=-1, keepdims=True) - hat * jnp.mean(total * hat, axis=-1, keepdims=True)
        pieces.append(jnp.swapaxes(total * spread, 0, 1))
    media_slope = jnp.concatenate(pieces, axis=0)

    gain_total = sum_fast(jnp.concatenate(gain_parts, axis=0), heads_count, rows_count, 6)
    gain_total = gain_total.reshape(layers, 6, width)
    squares = jnp.zeros((), F32)
    for share in shares:
        for piece in share:
            wide = piece.astype(F32)
            squares = squares + jnp.sum(wide * wide)
    square_total = sum_fast(jnp.full((8, 128), squares, F32), heads_count, rows_count, 7)[0, 0]
    gradient_norm = jnp.sqrt(square_total + jnp.sum(gain_total * gain_total))
    factor = CLIP_LEVEL / jnp.maximum(gradient_norm, CLIP_LEVEL)

    def wide_part(index, begin, end):
        return jnp.stack([share[index][:, begin:end] for share in shares]).astype(F32)

    columns = head_columns
    inward_grad = jnp.stack(
        [
            jnp.stack([share[2][:, (1 + t) * columns : (2 + t) * columns] for t in range(3)])
            for share in shares
        ]
    ).astype(F32)
    table = (
        (inward, inward_first, inward_second, inward_grad, RATE_INWARD),
        (outward, outward_first, outward_second, jnp.swapaxes(wide_part(2, 0, columns), 1, 2), RATE_OUTWARD),
        (widen, widen_first, widen_second, wide_part(1, 0, None), RATE_WIDEN),
        (narrow, narrow_first, narrow_second, jnp.swapaxes(wide_part(0, 0, None), 1, 2), RATE_NARROW),
    )
    results = [latent, slope, media_slope, gradient_norm]
    for weight, first, second, gradient, rate in table:
        mean_new, square_new, weight_new = adam_step(
            weight, first, second, gradient * factor, rate, WEIGHT_DECAY
        )
        results = results + [mean_new, square_new, weight_new, weight_new.astype(BF)]
    mean_new, square_new, weight_new = adam_step(
        norm_gains, gain_first, gain_second, gain_total * factor, RATE_GAINS, 0.0
    )
    results = results + [mean_new, square_new, weight_new, gain_total[:, 4:6]]
    return tuple(results)


def solution(mesh):
    placed = (
        P("heads", "rows", None),
        P("rows", "heads", None),
        P("rows"),
        P("rows", "heads", None),
        P(None, None, "rows", "heads"),
        P(None, None, "rows", "heads"),
        P(None, None, "rows", "heads"),
        P(None, "heads", "rows"),
        P(None, "heads", "rows"),
        P(None, "heads", "rows"),
        P(None, "rows", "heads"),
        P(None, "rows", "heads"),
        P(None, "rows", "heads"),
        P(None, "heads", "rows"),
        P(None, "heads", "rows"),
        P(None, "heads", "rows"),
        P(),
        P(),
        P(),
    )
    local = local_fast if (mesh.shape["rows"], mesh.shape["heads"]) == (8, 4) else local_plain
    return jax.shard_map(
        local,
        mesh=mesh,
        in_specs=placed,
        out_specs=(
            P("rows", "heads", None),
            P("rows", "heads", None),
            P("heads", "rows", None),
            P(),
            P(None, None, "rows", "heads"),
            P(None, None, "rows", "heads"),
            P(None, None, "rows", "heads"),
            P(None, None, "rows", "heads"),
            P(None, "heads", "rows"),
            P(None, "heads", "rows"),
            P(None, "heads", "rows"),
            P(None, "heads", "rows"),
            P(None, "rows", "heads"),
            P(None, "rows", "heads"),
            P(None, "rows", "heads"),
            P(None, "rows", "heads"),
            P(None, "heads", "rows"),
            P(None, "heads", "rows"),
            P(None, "heads", "rows"),
            P(None, "heads", "rows"),
            P(),
            P(),
            P(),
            P(),
        ),
        check_vma=False,
    )
```

```python
import functools

import jax
import jax.numpy as jnp
from jax import lax
from jax.experimental import pallas as pl
from jax.experimental.pallas import tpu as pltpu
from jax.sharding import PartitionSpec as P

HD = 96
STEP = 10
PATCHES = 128


EPS_NORM = 1e-05
BETA_ONE = 0.5
BETA_TWO = 0.5
ADAM_EPS = 1e-08
WEIGHT_DECAY = 0.1
CLIP_LEVEL = 1.0
MASKED_SCORE = -1e30
RATE_INWARD = 0.02
RATE_OUTWARD = 0.5
RATE_WIDEN = 0.02
RATE_NARROW = 0.01
RATE_GAINS = 0.1


def layer_norm(rows, gain, shift):
    middle = jnp.mean(rows, axis=-1, keepdims=True)
    centred = rows - middle
    spread = jnp.mean(centred * centred, axis=-1, keepdims=True)
    return centred * lax.rsqrt(spread + EPS_NORM) * gain + shift


def norm_back(rows, gain, shift, slope):
    _, pullback = jax.vjp(layer_norm, rows, gain, shift)
    return pullback(slope)


def adam_step(weight, first, second, gradient, rate, decay):
    mean_new = BETA_ONE * first + (1.0 - BETA_ONE) * gradient
    square_new = BETA_TWO * second + (1.0 - BETA_TWO) * gradient * gradient
    mean_hat = mean_new / (1.0 - BETA_ONE**STEP)
    square_hat = square_new / (1.0 - BETA_TWO**STEP)
    weight_new = weight - rate * (mean_hat / (jnp.sqrt(square_hat) + ADAM_EPS) + decay * weight)
    return (mean_new, square_new, weight_new)


def gather_slots(rows):
    return lax.all_gather(rows, "heads", axis=1, tiled=True)


def scatter_slots(terms):
    return lax.psum_scatter(terms, "heads", scatter_dimension=1, tiled=True)


def gather_slopes(rows):
    return lax.all_gather(rows, "heads", axis=1, tiled=True)


def scatter_slopes(terms):
    return lax.psum_scatter(terms, "heads", scatter_dimension=1, tiled=True)


def both_scores(query, media_pair, latent_pair, live, scale):
    score_media = (
        jnp.einsum("vnhe,pvhe->vhnp", query, media_pair[0], preferred_element_type=jnp.float32)
        * scale
    )
    score_media = jnp.where(live[:, None, None, :], score_media, MASKED_SCORE)
    score_latent = (
        jnp.einsum("vnhe,vmhe->vhnm", query, latent_pair[0], preferred_element_type=jnp.float32)
        * scale
    )
    return (score_media, score_latent)


def attend(query, media_pair, latent_pair, live, scale):
    score_media, score_latent = both_scores(query, media_pair, latent_pair, live, scale)
    top = jnp.maximum(
        jnp.max(score_media, axis=-1, keepdims=True), jnp.max(score_latent, axis=-1, keepdims=True)
    )
    exponent_media = jnp.exp(score_media - top)
    exponent_latent = jnp.exp(score_latent - top)
    total = jnp.sum(exponent_media, axis=-1, keepdims=True) + jnp.sum(
        exponent_latent, axis=-1, keepdims=True
    )
    share_media = (exponent_media / total).astype(jnp.bfloat16)
    share_latent = (exponent_latent / total).astype(jnp.bfloat16)
    mixed = jnp.einsum(
        "vhnp,pvhe->vnhe", share_media, media_pair[1], preferred_element_type=jnp.float32
    )
    mixed = mixed + jnp.einsum(
        "vhnm,vmhe->vnhe", share_latent, latent_pair[1], preferred_element_type=jnp.float32
    )
    return (mixed.astype(jnp.bfloat16), top + jnp.log(total))


def attend_back(query, media_pair, latent_pair, live, log_total, mixed_slope, scale):
    score_media, score_latent = both_scores(query, media_pair, latent_pair, live, scale)
    share_media = jnp.exp(score_media - log_total)
    share_latent = jnp.exp(score_latent - log_total)
    share_slope_media = jnp.einsum(
        "vnhe,pvhe->vhnp", mixed_slope, media_pair[1], preferred_element_type=jnp.float32
    )
    share_slope_latent = jnp.einsum(
        "vnhe,vmhe->vhnm", mixed_slope, latent_pair[1], preferred_element_type=jnp.float32
    )
    row_total = jnp.sum(share_media * share_slope_media, axis=-1, keepdims=True)
    row_total = row_total + jnp.sum(share_latent * share_slope_latent, axis=-1, keepdims=True)
    score_slope_media = (share_media * (share_slope_media - row_total)).astype(jnp.bfloat16)
    score_slope_latent = (share_latent * (share_slope_latent - row_total)).astype(jnp.bfloat16)
    query_slope = jnp.einsum(
        "vhnp,pvhe->vnhe", score_slope_media, media_pair[0], preferred_element_type=jnp.float32
    )
    query_slope = query_slope + jnp.einsum(
        "vhnm,vmhe->vnhe", score_slope_latent, latent_pair[0], preferred_element_type=jnp.float32
    )
    query_slope = (query_slope * scale).astype(jnp.bfloat16)
    key_media = (
        jnp.einsum("vhnp,vnhe->pvhe", score_slope_media, query, preferred_element_type=jnp.float32)
        * scale
    ).astype(jnp.bfloat16)
    value_media = jnp.einsum(
        "vhnp,vnhe->pvhe",
        share_media.astype(jnp.bfloat16),
        mixed_slope,
        preferred_element_type=jnp.float32,
    ).astype(jnp.bfloat16)
    key_latent = (
        jnp.einsum("vhnm,vnhe->vmhe", score_slope_latent, query, preferred_element_type=jnp.float32)
        * scale
    ).astype(jnp.bfloat16)
    value_latent = jnp.einsum(
        "vhnm,vnhe->vmhe",
        share_latent.astype(jnp.bfloat16),
        mixed_slope,
        preferred_element_type=jnp.float32,
    ).astype(jnp.bfloat16)
    return (query_slope, jnp.stack((key_media, value_media)), jnp.stack((key_latent, value_latent)))


def local_plain(
    media,
    latents,
    frame_count,
    cotangent,
    inward,
    inward_first,
    inward_second,
    outward,
    outward_first,
    outward_second,
    widen,
    widen_first,
    widen_second,
    narrow,
    narrow_first,
    narrow_second,
    norm_gains,
    gain_first,
    gain_second,
):
    heads_count = lax.axis_size("heads")
    layers, _, row_share, head_columns = inward.shape
    local_positions, videos, width = media.shape
    positions = local_positions * heads_count
    latent_count = latents.shape[1] * heads_count
    local_heads = head_columns // HD
    scale = HD ** (-0.5)
    live = (jnp.arange(positions, dtype=jnp.int32) // PATCHES)[None, :] < frame_count[:, None]
    inward_columns, outward_rows, widen_columns, narrow_rows = (
        lax.all_gather(inward.astype(jnp.bfloat16), "rows", axis=2, tiled=True),
        lax.all_gather(outward.astype(jnp.bfloat16), "rows", axis=2, tiled=True),
        lax.all_gather(widen.astype(jnp.bfloat16), "rows", axis=1, tiled=True),
        lax.all_gather(narrow.astype(jnp.bfloat16), "rows", axis=2, tiled=True),
    )
    media_rows = media.astype(jnp.float32)
    latent = latents
    kept = []
    for layer in range(layers):
        gains = norm_gains[layer]
        media_norm = layer_norm(media_rows, gains[0], gains[1]).astype(jnp.bfloat16)
        latent_norm = gather_slots(layer_norm(latent, gains[2], gains[3]).astype(jnp.bfloat16))
        triple = jnp.einsum(
            "vnd,tdc->tvnc", latent_norm, inward_columns[layer], preferred_element_type=jnp.float32
        ).astype(jnp.bfloat16)
        pair_columns = inward_columns[layer, 1:3]
        media_pair = jnp.einsum(
            "pvd,tdc->tpvc",
            lax.all_gather(media_norm, "heads", axis=0, tiled=True),
            pair_columns,
            preferred_element_type=jnp.float32,
        ).astype(jnp.bfloat16)
        query = triple[0].reshape(videos, latent_count, local_heads, HD)
        latent_pair = triple[1:3].reshape(2, videos, latent_count, local_heads, HD)
        heads_pair = media_pair.reshape(2, positions, videos, local_heads, HD)
        mixed, log_total = attend(query, heads_pair, latent_pair, live, scale)
        mixed = mixed.reshape(videos, latent_count, head_columns)
        middle = latent + scatter_slots(
            jnp.einsum(
                "vnc,cd->vnd", mixed, outward_rows[layer], preferred_element_type=jnp.float32
            )
        )
        feed_norm = gather_slots(layer_norm(middle, gains[4], gains[5]).astype(jnp.bfloat16))
        hidden_pre = jnp.einsum(
            "vnd,df->vnf", feed_norm, widen_columns[layer], preferred_element_type=jnp.float32
        )
        hidden = jax.nn.gelu(hidden_pre).astype(jnp.bfloat16)
        kept.append(
            (
                latent,
                middle,
                media_norm,
                latent_norm,
                query,
                heads_pair,
                latent_pair,
                mixed,
                log_total,
                feed_norm,
                hidden_pre,
                hidden,
            )
        )
        latent = middle + scatter_slots(
            jnp.einsum(
                "vnf,fd->vnd", hidden, narrow_rows[layer], preferred_element_type=jnp.float32
            )
        )
    slope = cotangent
    media_slope = jnp.zeros(media_rows.shape, jnp.float32)
    inward_parts, outward_parts, widen_parts, narrow_parts, gain_parts = ([], [], [], [], [])
    for layer in reversed(range(layers)):
        (
            latent_in,
            middle,
            media_norm,
            latent_norm,
            query,
            heads_pair,
            latent_pair,
            mixed,
            log_total,
            feed_norm,
            hidden_pre,
            hidden,
        ) = kept[layer]
        gains = norm_gains[layer]
        feed_slope = gather_slopes(slope.astype(jnp.bfloat16))
        narrow_grad = jnp.einsum(
            "vnf,vnd->fd", hidden, feed_slope, preferred_element_type=jnp.float32
        )
        hidden_slope = jnp.einsum(
            "vnd,fd->vnf", feed_slope, narrow_rows[layer], preferred_element_type=jnp.float32
        )
        _, gelu_back = jax.vjp(jax.nn.gelu, hidden_pre)
        pre_slope = gelu_back(hidden_slope)[0].astype(jnp.bfloat16)
        widen_grad = jnp.einsum(
            "vnd,vnf->df", feed_norm, pre_slope, preferred_element_type=jnp.float32
        )
        norm_slope = scatter_slopes(
            jnp.einsum(
                "vnf,df->vnd", pre_slope, widen_columns[layer], preferred_element_type=jnp.float32
            )
        )
        middle_part, gain_feed, shift_feed = norm_back(middle, gains[4], gains[5], norm_slope)
        middle_slope = slope + middle_part
        branch_slope = gather_slopes(middle_slope.astype(jnp.bfloat16))
        outward_grad = jnp.einsum(
            "vnc,vnd->cd", mixed, branch_slope, preferred_element_type=jnp.float32
        )
        mixed_slope = jnp.einsum(
            "vnd,cd->vnc", branch_slope, outward_rows[layer], preferred_element_type=jnp.float32
        ).astype(jnp.bfloat16)
        mixed_slope = mixed_slope.reshape(videos, latent_count, local_heads, HD)
        query_slope, media_slopes, latent_slopes = attend_back(
            query, heads_pair, latent_pair, live, log_total, mixed_slope, scale
        )
        triple_slope = jnp.concatenate(
            (
                query_slope.reshape(1, videos, latent_count, head_columns),
                latent_slopes.reshape(2, videos, latent_count, head_columns),
            ),
            axis=0,
        )
        inward_grad = jnp.einsum(
            "vnd,tvnc->tdc", latent_norm, triple_slope, preferred_element_type=jnp.float32
        )
        norm_slope = scatter_slopes(
            jnp.einsum(
                "tvnc,tdc->vnd",
                triple_slope,
                inward_columns[layer],
                preferred_element_type=jnp.float32,
            )
        )
        latent_part, gain_latent, shift_latent = norm_back(
            latent_in, gains[2], gains[3], norm_slope
        )
        slope = middle_slope + latent_part
        pair_slope = media_slopes.reshape(2, positions, videos, head_columns)
        media_columns = jnp.einsum(
            "pvd,tpvc->tdc",
            lax.all_gather(media_norm, "heads", axis=0, tiled=True),
            pair_slope,
            preferred_element_type=jnp.float32,
        )
        inward_grad = jnp.concatenate((inward_grad[:1], inward_grad[1:] + media_columns), axis=0)
        pair_columns = inward_columns[layer, 1:3]
        media_norm_slope = lax.psum_scatter(
            jnp.einsum(
                "tpvc,tdc->pvd", pair_slope, pair_columns, preferred_element_type=jnp.float32
            ),
            "heads",
            scatter_dimension=0,
            tiled=True,
        )
        media_part, gain_media, shift_media = norm_back(
            media_rows, gains[0], gains[1], media_norm_slope
        )
        media_slope = media_slope + media_part
        inward_parts.append(inward_grad)
        outward_parts.append(outward_grad)
        widen_parts.append(widen_grad)
        narrow_parts.append(narrow_grad)
        gain_parts.append(
            jnp.stack((gain_media, shift_media, gain_latent, shift_latent, gain_feed, shift_feed))
        )
    inward_grad, outward_grad, widen_grad, narrow_grad = (
        lax.psum_scatter(jnp.stack(inward_parts[::-1]), "rows", scatter_dimension=2, tiled=True),
        lax.psum_scatter(jnp.stack(outward_parts[::-1]), "rows", scatter_dimension=2, tiled=True),
        lax.psum_scatter(jnp.stack(widen_parts[::-1]), "rows", scatter_dimension=1, tiled=True),
        lax.psum_scatter(jnp.stack(narrow_parts[::-1]), "rows", scatter_dimension=2, tiled=True),
    )
    squares = jnp.sum(inward_grad * inward_grad) + jnp.sum(outward_grad * outward_grad)
    squares = squares + jnp.sum(widen_grad * widen_grad) + jnp.sum(narrow_grad * narrow_grad)
    gain_total, square_total = lax.psum((jnp.stack(gain_parts[::-1]), squares), ("rows", "heads"))
    gradient_norm = jnp.sqrt(square_total + jnp.sum(gain_total * gain_total))
    factor = CLIP_LEVEL / jnp.maximum(gradient_norm, CLIP_LEVEL)
    table = (
        (inward, inward_first, inward_second, inward_grad, RATE_INWARD, WEIGHT_DECAY),
        (outward, outward_first, outward_second, outward_grad, RATE_OUTWARD, WEIGHT_DECAY),
        (widen, widen_first, widen_second, widen_grad, RATE_WIDEN, WEIGHT_DECAY),
        (narrow, narrow_first, narrow_second, narrow_grad, RATE_NARROW, WEIGHT_DECAY),
    )
    results = [latent, slope, media_slope, gradient_norm]
    for weight, first, second, gradient, rate, decay in table:
        mean_new, square_new, weight_new = adam_step(
            weight, first, second, gradient * factor, rate, decay
        )
        results = results + [mean_new, square_new, weight_new, weight_new.astype(jnp.bfloat16)]
    mean_new, square_new, weight_new = adam_step(
        norm_gains, gain_first, gain_second, gain_total * factor, RATE_GAINS, 0.0
    )
    results = results + [mean_new, square_new, weight_new, gain_total[:, 4:6]]
    return tuple(results)


BF = jnp.bfloat16
F32 = jnp.float32
VMEM_LIMIT = 60 * 1024 * 1024
NT = (((1,), (1,)), ((), ()))
TN = (((0,), (0,)), ((), ()))
X_SWAP = ((0, 1), (1, 0), (2, 3), (3, 2))
Y_SWAP = ((0, 2), (2, 0), (1, 3), (3, 1))
FAR_SWAP = ((0, 3), (3, 0), (1, 2), (2, 1))


def vmem_spec():
    return pl.BlockSpec(memory_space=pltpu.VMEM)


def mm(left, right, dims=None, out=BF):
    dims = dims or (((1,), (0,)), ((), ()))
    return lax.dot_general(left, right, dims, preferred_element_type=F32).astype(out)


def media_kernel(first_ref, second_ref, gain_ref, weight_ref, *rest):
    keys_ref, hat_ref, rows_ref = rest[-3:]
    half, layer = pl.program_id(0), pl.program_id(1)

    @pl.when(layer == 0)
    def _():
        @pl.when(half == 0)
        def _():
            rows_ref[...] = first_ref[...].astype(F32).reshape(rows_ref.shape)

        @pl.when(half == 1)
        def _():
            rows_ref[...] = second_ref[...].astype(F32).reshape(rows_ref.shape)

        rows = rows_ref[...]
        centred = rows - jnp.mean(rows, axis=-1, keepdims=True)
        spread = jnp.mean(centred * centred, axis=-1, keepdims=True)
        hat = centred * lax.rsqrt(spread + EPS_NORM)
        rows_ref[...] = hat
        hat_ref[...] = hat.astype(BF).reshape(hat_ref.shape)

    gain = gain_ref[pl.ds(layer, 1), 0]
    shift = gain_ref[pl.ds(layer, 1), 1]
    normed = (rows_ref[...] * gain + shift).astype(BF)
    keys_ref[...] = jnp.dot(normed, weight_ref[...], preferred_element_type=F32).astype(BF).reshape(keys_ref.shape)


def media_part(first, second, gains, weight, group, earlier):
    videos, patches, width = first.shape
    columns = weight.shape[1]
    kinds = (
        jax.ShapeDtypeStruct((8, videos, patches, columns), BF),
        jax.ShapeDtypeStruct((8, videos, patches, width), BF),
    )
    whole = pl.BlockSpec((videos, patches, width), lambda i, j: (0, 0, 0))
    in_specs = [
        whole,
        whole,
        pl.BlockSpec(gains.shape, lambda i, j: (0, 0, 0)),
        pl.BlockSpec((width, columns // 2), lambda i, j: (0, j)),
    ]
    aliases = {}
    if earlier:
        in_specs += [pl.BlockSpec(memory_space=pl.ANY)] * 2
        aliases = {4: 0, 5: 1}
    rows = videos * patches
    return pl.pallas_call(
        media_kernel,
        grid=(2, 2),
        out_shape=kinds,
        in_specs=in_specs,
        out_specs=(
            pl.BlockSpec((1, videos, patches, columns // 2), lambda i, j: (2 * group + i, 0, 0, j)),
            pl.BlockSpec((1, videos, patches, width), lambda i, j: (2 * group + i, 0, 0, 0)),
        ),
        scratch_shapes=[pltpu.VMEM((rows, width), F32)],
        input_output_aliases=aliases,
        compiler_params=pltpu.CompilerParams(vmem_limit_bytes=VMEM_LIMIT),
        cost_estimate=pl.CostEstimate(
            flops=4 * rows * width * columns, bytes_accessed=8 * rows * width, transcendentals=0
        ),
        name="media_part",
    )(first, second, gains, weight, *earlier)


def head_mask(rows, columns, head):
    place = lax.broadcasted_iota(jnp.int32, (rows, columns), 1)
    return (place >= head * HD) & (place < (head + 1) * HD)


def spread_heads(rows):
    heads = rows.shape[1] // HD
    zero = jnp.zeros_like(rows)
    return jnp.concatenate(
        [jnp.where(head_mask(*rows.shape, head), rows, zero) for head in range(heads)], axis=0
    )


def gather_heads(rows, count):
    heads = rows.shape[1] // HD
    total = jnp.zeros((count, rows.shape[1]), F32)
    for head in range(heads):
        part = rows[head * count : (head + 1) * count]
        total = total + jnp.where(head_mask(*part.shape, head), part, 0.0)
    return total


def attend_kernel(live_ref, query_ref, latent_key_ref, latent_value_ref, key_ref, value_ref, mixed_ref, *, scale):
    video = pl.program_id(0)
    slots, patches = key_ref.shape[0], key_ref.shape[2]
    query = spread_heads(query_ref[...])
    rows, columns = query.shape
    place = lax.broadcasted_iota(jnp.int32, (rows, 2 * patches), 1)
    scores = []
    for pair in range(slots // 2):
        keys = key_ref[2 * pair : 2 * pair + 2, 0].reshape(2 * patches, columns)
        score = lax.dot_general(query, keys, NT, preferred_element_type=F32) * scale
        live = jnp.where(place < patches, live_ref[video, 2 * pair], live_ref[video, 2 * pair + 1])
        scores.append(jnp.where(live > 0, score, MASKED_SCORE))
    scores.append(lax.dot_general(query, latent_key_ref[...], NT, preferred_element_type=F32) * scale)
    top = functools.reduce(jnp.maximum, [jnp.max(score, axis=-1, keepdims=True) for score in scores])
    exponents = [jnp.exp(score - top) for score in scores]
    total = functools.reduce(jnp.add, [jnp.sum(e, axis=-1, keepdims=True) for e in exponents])
    mixed = jnp.zeros((rows, columns), F32)
    for pair in range(slots // 2):
        values = value_ref[2 * pair : 2 * pair + 2, 0].reshape(2 * patches, columns)
        mixed = mixed + jnp.dot((exponents[pair] / total).astype(BF), values, preferred_element_type=F32)
    mixed = mixed + jnp.dot(
        (exponents[-1] / total).astype(BF), latent_value_ref[...], preferred_element_type=F32
    )
    mixed_ref[...] = gather_heads(mixed, query_ref.shape[0]).astype(BF)


def attend_fast(live, query, latent_pair, keys, layer, scale):
    slots, videos, patches, _ = keys.shape
    count, columns = query.shape[0] // videos, query.shape[1]
    row_block = pl.BlockSpec((count, columns), lambda v: (v, 0))
    return pl.pallas_call(
        functools.partial(attend_kernel, scale=scale),
        grid=(videos,),
        out_shape=jax.ShapeDtypeStruct(query.shape, BF),
        in_specs=[
            pl.BlockSpec(memory_space=pltpu.SMEM),
            row_block,
            row_block,
            pl.BlockSpec((count, columns), lambda v: (v, 1)),
            pl.BlockSpec((slots, 1, patches, columns), lambda v: (0, v, 0, 2 * layer)),
            pl.BlockSpec((slots, 1, patches, columns), lambda v: (0, v, 0, 2 * layer + 1)),
        ],
        out_specs=row_block,
        compiler_params=pltpu.CompilerParams(vmem_limit_bytes=VMEM_LIMIT),
        cost_estimate=pl.CostEstimate(
            flops=8 * slots * patches * videos * count * 2 * columns,
            bytes_accessed=4 * slots * videos * patches * columns,
            transcendentals=slots * patches * videos * count * 4,
        ),
        name="attend",
    )(live, query, latent_pair, latent_pair, keys, keys)


def attend_back_kernel(
    live_ref, query_ref, latent_key_ref, latent_value_ref, key_ref, value_ref, slope_ref, *rest, scale
):
    query_slope_ref, latent_slope_ref, media_slope_ref = rest[-3:]
    video = pl.program_id(0)
    slots, patches = key_ref.shape[0], key_ref.shape[2]
    pairs = slots // 2
    count = query_ref.shape[0]
    query, slope = spread_heads(query_ref[...]), spread_heads(slope_ref[...])
    rows, columns = query.shape
    place = lax.broadcasted_iota(jnp.int32, (2 * patches, rows), 0)

    def keys_of(ref, pair):
        return ref[2 * pair : 2 * pair + 2, 0].reshape(2 * patches, columns)

    scores = []
    for pair in range(pairs):
        score = lax.dot_general(keys_of(key_ref, pair), query, NT, preferred_element_type=F32) * scale
        live = jnp.where(place < patches, live_ref[video, 2 * pair], live_ref[video, 2 * pair + 1])
        scores.append(jnp.where(live > 0, score, MASKED_SCORE))
    scores.append(lax.dot_general(latent_key_ref[...], query, NT, preferred_element_type=F32) * scale)
    top = functools.reduce(jnp.maximum, [jnp.max(score, axis=0, keepdims=True) for score in scores])
    exponents = [jnp.exp(score - top) for score in scores]
    total = functools.reduce(jnp.add, [jnp.sum(e, axis=0, keepdims=True) for e in exponents])
    shares = [e / total for e in exponents]
    share_slopes = [
        lax.dot_general(keys_of(value_ref, pair), slope, NT, preferred_element_type=F32)
        for pair in range(pairs)
    ]
    share_slopes.append(
        lax.dot_general(latent_value_ref[...], slope, NT, preferred_element_type=F32)
    )
    row_total = functools.reduce(
        jnp.add,
        [jnp.sum(a * b, axis=0, keepdims=True) for a, b in zip(shares, share_slopes)],
    )
    query_slope = jnp.zeros((rows, columns), F32)
    for at in range(pairs + 1):
        keys = keys_of(key_ref, at) if at < pairs else latent_key_ref[...]
        score_slope = (shares[at] * (share_slopes[at] - row_total)).astype(BF)
        key_slope = (jnp.dot(score_slope, query, preferred_element_type=F32) * scale).astype(BF)
        value_slope = jnp.dot(shares[at].astype(BF), slope, preferred_element_type=F32).astype(BF)
        query_slope = query_slope + lax.dot_general(
            score_slope, keys, TN, preferred_element_type=F32
        )
        if at < pairs:
            media_slope_ref[2 * at : 2 * at + 2, 0, :, :columns] = key_slope.reshape(2, patches, columns)
            media_slope_ref[2 * at : 2 * at + 2, 0, :, columns:] = value_slope.reshape(2, patches, columns)
        else:
            latent_slope_ref[:, :columns] = key_slope
            latent_slope_ref[:, columns:] = value_slope
    query_slope_ref[...] = (gather_heads(query_slope, count) * scale).astype(BF)


def attend_back_fast(live, query, latent_pair, keys, slope, layer, scale, earlier):
    slots, videos, patches, _ = keys.shape
    count, columns = query.shape[0] // videos, query.shape[1]
    row_block = pl.BlockSpec((count, columns), lambda v: (v, 0))
    in_specs = [
        pl.BlockSpec(memory_space=pltpu.SMEM),
        row_block,
        row_block,
        pl.BlockSpec((count, columns), lambda v: (v, 1)),
        pl.BlockSpec((slots, 1, patches, columns), lambda v: (0, v, 0, 2 * layer)),
        pl.BlockSpec((slots, 1, patches, columns), lambda v: (0, v, 0, 2 * layer + 1)),
        row_block,
    ]
    aliases = {}
    if earlier:
        in_specs += [pl.BlockSpec(memory_space=pl.ANY)]
        aliases = {7: 2}
    return pl.pallas_call(
        functools.partial(attend_back_kernel, scale=scale),
        grid=(videos,),
        out_shape=(
            jax.ShapeDtypeStruct(query.shape, BF),
            jax.ShapeDtypeStruct(latent_pair.shape, BF),
            jax.ShapeDtypeStruct(keys.shape, BF),
        ),
        in_specs=in_specs,
        out_specs=(
            row_block,
            pl.BlockSpec((count, 2 * columns), lambda v: (v, 0)),
            pl.BlockSpec((slots, 1, patches, 2 * columns), lambda v: (0, v, 0, layer)),
        ),
        input_output_aliases=aliases,
        compiler_params=pltpu.CompilerParams(vmem_limit_bytes=VMEM_LIMIT),
        cost_estimate=pl.CostEstimate(
            flops=20 * slots * patches * videos * count * 2 * columns,
            bytes_accessed=8 * slots * videos * patches * columns,
            transcendentals=slots * patches * videos * count * 4,
        ),
        name="attend_back",
    )(live, query, latent_pair, latent_pair, keys, keys, slope, *earlier)


def product_pair_kernel(first_ref, second_ref, third_ref, fourth_ref, *rest):
    out_ref = rest[-1]

    @pl.when(pl.program_id(0) == 0)
    def _():
        out_ref[...] = mm(first_ref[...], second_ref[...], TN)

    @pl.when(pl.program_id(0) == 1)
    def _():
        out_ref[...] = mm(third_ref[...], fourth_ref[...], TN)

    if len(rest) > 1:
        @pl.when(pl.program_id(0) == 2)
        def _():
            out_ref[...] = rest[0][...]


def product_pair(first, second, third, fourth, *extra):
    rows, width, columns = first.shape[0], first.shape[1], second.shape[1]
    cut = columns // 3
    left = pl.BlockSpec((rows, width), lambda i, j: (0, 0))
    return pl.pallas_call(
        product_pair_kernel,
        grid=(2 + len(extra), 3),
        out_shape=jax.ShapeDtypeStruct((width, (2 + len(extra)) * columns), BF),
        in_specs=[
            left,
            pl.BlockSpec((rows, cut), lambda i, j: (0, jnp.where(i == 0, j, 2))),
            left,
            pl.BlockSpec((rows, cut), lambda i, j: (0, jnp.where(i == 0, 0, jnp.where(i == 1, j, 2)))),
        ]
        + [pl.BlockSpec((width, cut), lambda i, j: (0, jnp.where(i == 2, j, 0)))] * len(extra),
        out_specs=pl.BlockSpec((width, cut), lambda i, j: (0, 3 * i + j)),
        compiler_params=pltpu.CompilerParams(vmem_limit_bytes=VMEM_LIMIT),
        cost_estimate=pl.CostEstimate(
            flops=4 * rows * width * columns, bytes_accessed=8 * width * columns, transcendentals=0
        ),
        name="feed_gradients",
    )(first, second, third, fourth, *extra)


def greet(count):
    me = lax.axis_index("heads")
    barrier = pltpu.get_barrier_semaphore()
    for step in range(1, count):
        pl.semaphore_signal(barrier, inc=1, device_id={"heads": (me + step) % count})
    pl.semaphore_wait(barrier, count - 1)
    return me


def own_rows(ref, place, share):
    return ref.at[:, pl.ds(pl.multiple_of(place * share, share), share), :]


def start_gather(me, count, share, own_ref, full_ref, send_sem, recv_sem):
    copies = []
    for step in range(1, count):
        copy = pltpu.make_async_remote_copy(
            src_ref=own_ref,
            dst_ref=own_rows(full_ref, me, share),
            send_sem=send_sem.at[step - 1],
            recv_sem=recv_sem.at[step - 1],
            device_id={"heads": (me + step) % count},
        )
        copy.start()
        copies.append(copy)
    return copies


def start_scatter(me, count, share, part_ref, landed_ref, send_sem, recv_sem):
    copies = []
    for step in range(1, count):
        peer = (me + step) % count
        copy = pltpu.make_async_remote_copy(
            src_ref=own_rows(part_ref, peer, share),
            dst_ref=landed_ref.at[step - 1],
            send_sem=send_sem.at[step - 1],
            recv_sem=recv_sem.at[step - 1],
            device_id={"heads": peer},
        )
        copy.start()
        copies.append(copy)
    return copies


def forward_kernel(
    count, last, part_ref, rest_ref, gain_ref, new_ref, *refs
):
    refs = list(refs)
    full_ref = None if last else refs.pop(0)
    landed_ref, own_ref, send_sem, recv_sem, send_more, recv_more = refs
    me = greet(count)
    share = rest_ref.shape[1]
    copies = start_scatter(me, count, share, part_ref, landed_ref, send_sem, recv_sem)
    mine = pl.ds(pl.multiple_of(me * share, share), share)
    total = rest_ref[...] + part_ref[:, mine, :].astype(F32)
    for step, copy in enumerate(copies):
        copy.wait_recv()
        total = total + landed_ref[step].astype(F32)
    new_ref[...] = total
    if not last:
        own_ref[...] = layer_norm(total, gain_ref[0], gain_ref[1]).astype(BF)
        more = start_gather(me, count, share, own_ref, full_ref, send_more, recv_more)
        full_ref[:, mine, :] = own_ref[...]
        for copy in more:
            copy.wait()
    for copy in copies:
        copy.wait_send()


def forward_exchange(part, rest, gain, count, last=False):
    videos, share, width = rest.shape
    outs = [jax.ShapeDtypeStruct(rest.shape, F32)]
    if not last:
        outs.append(jax.ShapeDtypeStruct(part.shape, BF))
    got = pl.pallas_call(
        functools.partial(forward_kernel, count, last),
        out_shape=tuple(outs),
        in_specs=[vmem_spec()] * 3,
        out_specs=(vmem_spec(),) * len(outs),
        scratch_shapes=[
            pltpu.VMEM((count - 1, videos, share, width), BF),
            pltpu.VMEM((videos, share, width), BF),
        ]
        + [pltpu.SemaphoreType.DMA((count - 1,))] * 4,
        compiler_params=pltpu.CompilerParams(
            collective_id=3 if last else 2, has_side_effects=True, vmem_limit_bytes=VMEM_LIMIT
        ),
        cost_estimate=pl.CostEstimate(flops=0, bytes_accessed=75 * 1000 * 1000, transcendentals=0),
        name="forward_exchange",
    )(part, rest, gain)
    return got if not last else (got[0], None)


def backward_kernel(
    count, last, part_ref, rows_ref, rest_ref, gain_ref, new_ref, sums_ref, *refs
):
    refs = list(refs)
    full_ref = None if last else refs.pop(0)
    landed_ref, own_ref, send_sem, recv_sem, send_more, recv_more = refs
    me = greet(count)
    share = rest_ref.shape[1]
    copies = start_scatter(me, count, share, part_ref, landed_ref, send_sem, recv_sem)
    mine = pl.ds(pl.multiple_of(me * share, share), share)
    rows = rows_ref[...]
    centred = rows - jnp.mean(rows, axis=-1, keepdims=True)
    scale = lax.rsqrt(jnp.mean(centred * centred, axis=-1, keepdims=True) + EPS_NORM)
    hat = centred * scale
    slope = part_ref[:, mine, :].astype(F32)
    for step, copy in enumerate(copies):
        copy.wait_recv()
        slope = slope + landed_ref[step].astype(F32)
    hat_slope = slope * gain_ref[0]
    back = hat_slope - jnp.mean(hat_slope, axis=-1, keepdims=True)
    back = back - hat * jnp.mean(hat_slope * hat, axis=-1, keepdims=True)
    new = rest_ref[...] + back * scale
    new_ref[...] = new
    if not last:
        own_ref[...] = new.astype(BF)
        more = start_gather(me, count, share, own_ref, full_ref, send_more, recv_more)
        full_ref[:, mine, :] = own_ref[...]
    sums_ref[0:1] = jnp.sum(jnp.sum(slope * hat, axis=0), axis=0, keepdims=True)
    sums_ref[1:2] = jnp.sum(jnp.sum(slope, axis=0), axis=0, keepdims=True)
    if not last:
        for copy in more:
            copy.wait()
    for copy in copies:
        copy.wait_send()


def backward_exchange(part, rows, rest, gain, count, last=False):
    videos, share, width = rest.shape
    outs = [jax.ShapeDtypeStruct(rest.shape, F32), jax.ShapeDtypeStruct((2, width), F32)]
    if not last:
        outs.append(jax.ShapeDtypeStruct(part.shape, BF))
    got = pl.pallas_call(
        functools.partial(backward_kernel, count, last),
        out_shape=tuple(outs),
        in_specs=[vmem_spec()] * 4,
        out_specs=(vmem_spec(),) * len(outs),
        scratch_shapes=[
            pltpu.VMEM((count - 1, videos, share, width), BF),
            pltpu.VMEM((videos, share, width), BF),
        ]
        + [pltpu.SemaphoreType.DMA((count - 1,))] * 4,
        compiler_params=pltpu.CompilerParams(
            collective_id=5 if last else 4, has_side_effects=True, vmem_limit_bytes=VMEM_LIMIT
        ),
        cost_estimate=pl.CostEstimate(flops=0, bytes_accessed=75 * 1000 * 1000, transcendentals=0),
        name="backward_exchange",
    )(part, rows, rest, gain)
    return got if not last else (*got, None)


def sum_kernel(heads, rows, term_ref, out_ref, plane_ref, line_ref, part_ref, *sems):
    me_head, me_row = lax.axis_index("heads"), lax.axis_index("rows")
    barrier = pltpu.get_barrier_semaphore()
    for step in range(1, heads):
        pl.semaphore_signal(barrier, inc=1, device_id={"heads": (me_head + step) % heads})
    for step in range(1, rows):
        pl.semaphore_signal(barrier, inc=1, device_id={"rows": (me_row + step) % rows})
    pl.semaphore_wait(barrier, heads - 1 + rows - 1)

    def spread(axis, me, count, source_of, slots_ref, own, send, recv):
        copies = []
        for step in range(1, count):
            peer = (me + step) % count
            copy = pltpu.make_async_remote_copy(
                src_ref=source_of(peer),
                dst_ref=slots_ref.at[me],
                send_sem=send.at[step - 1],
                recv_sem=recv.at[step - 1],
                device_id={axis: peer},
            )
            copy.start()
            copies.append(copy)
        slots_ref[pl.ds(me, 1)] = own[None]
        for copy in copies:
            copy.wait()

    def added(slots_ref, count):
        total = slots_ref[0]
        for at in range(1, count):
            total = total + slots_ref[at]
        return total

    mine = term_ref[pl.ds(me_head, 1)][0]
    spread("heads", me_head, heads, lambda peer: term_ref.at[peer], plane_ref, mine, *sems[0:2])
    part_ref[0] = added(plane_ref, heads)
    spread("rows", me_row, rows, lambda peer: part_ref.at[0], line_ref, part_ref[0], *sems[2:4])
    part_ref[1] = added(line_ref, rows)
    spread("heads", me_head, heads, lambda peer: part_ref.at[1], out_ref, part_ref[1], *sems[4:6])


def sum_fast(term, heads, rows, identity):
    block = term.shape[1:]
    return pl.pallas_call(
        functools.partial(sum_kernel, heads, rows),
        out_shape=jax.ShapeDtypeStruct(term.shape, F32),
        in_specs=[vmem_spec()],
        out_specs=vmem_spec(),
        scratch_shapes=[
            pltpu.VMEM((heads, *block), F32),
            pltpu.VMEM((rows, *block), F32),
            pltpu.VMEM((2, *block), F32),
            pltpu.SemaphoreType.DMA((heads - 1,)),
            pltpu.SemaphoreType.DMA((heads - 1,)),
            pltpu.SemaphoreType.DMA((rows - 1,)),
            pltpu.SemaphoreType.DMA((rows - 1,)),
            pltpu.SemaphoreType.DMA((heads - 1,)),
            pltpu.SemaphoreType.DMA((heads - 1,)),
        ],
        compiler_params=pltpu.CompilerParams(
            collective_id=identity, has_side_effects=True, vmem_limit_bytes=VMEM_LIMIT
        ),
        cost_estimate=pl.CostEstimate(flops=0, bytes_accessed=40 * 1000 * 1000, transcendentals=0),
        name="sum_over_all",
    )(term)


def flat(rows):
    return rows.reshape(-1, rows.shape[-1])


def local_fast(
    media,
    latents,
    frame_count,
    cotangent,
    inward,
    inward_first,
    inward_second,
    outward,
    outward_first,
    outward_second,
    widen,
    widen_first,
    widen_second,
    narrow,
    narrow_first,
    narrow_second,
    norm_gains,
    gain_first,
    gain_second,
):
    heads_count, rows_count = lax.axis_size("heads"), lax.axis_size("rows")
    me = lax.axis_index("heads")
    layers, _, row_share, head_columns = inward.shape
    local_positions, videos, width = media.shape
    latent_count = latents.shape[1] * heads_count
    scale = HD ** (-0.5)

    def swap_x(rows):
        return lax.ppermute(rows, "heads", X_SWAP)

    def swap_y(rows):
        return lax.ppermute(rows, "heads", Y_SWAP)

    def gather_rows(rows):
        return lax.all_gather(rows, "rows", axis=0, tiled=True)

    outward_t, narrow_t = (jnp.swapaxes(outward, 1, 2), jnp.swapaxes(narrow, 1, 2))
    columns, units = head_columns, widen.shape[2]
    first_set = [inward[l, t] for l in range(layers) for t in (1, 2)]
    first_set = first_set + [inward[l, 0] for l in range(layers)] + [outward_t[l] for l in range(layers)]
    first_set = jnp.concatenate([piece.astype(BF) for piece in first_set], axis=1)

    latent = latents
    normed = layer_norm(latent, norm_gains[0, 2], norm_gains[0, 3]).astype(BF)
    slope_rows = cotangent.astype(BF)
    first_set = gather_rows(first_set)
    pair_weights = first_set[:, : 2 * layers * columns]
    begin = 2 * layers * columns
    query_full = [first_set[:, begin + l * columns : begin + (l + 1) * columns] for l in range(layers)]
    begin = begin + layers * columns
    out_full = [first_set[:, begin + l * columns : begin + (l + 1) * columns] for l in range(layers)]
    widen_full, narrow_full = [], []
    for layer in range(layers):
        later = gather_rows(jnp.concatenate((widen[layer].astype(BF), narrow_t[layer].astype(BF)), axis=1))
        widen_full.append(later[:, :units])
        narrow_full.append(later[:, units:])
    share = latents.shape[1]
    moved = [(normed, slope_rows)]
    for swap in (X_SWAP, Y_SWAP, FAR_SWAP):
        moved.append(tuple(lax.ppermute(rows, "heads", swap) for rows in (normed, slope_rows)))
    gathered = []
    for at in range(2):
        full = jnp.zeros((videos, latent_count, width), BF)
        for group in range(heads_count):
            full = lax.dynamic_update_slice(full, moved[group][at], (0, (me ^ group) * share, 0))
        gathered.append(full)
    latent_norm, feed_slope = gathered

    own = jnp.swapaxes(media, 0, 1).reshape(videos, 2, local_positions // 2, width)
    own = (own[:, 0], own[:, 1])
    from_x = (swap_x(own[0]), swap_x(own[1]))
    from_y = (swap_y(own[0]), swap_y(own[1]))
    from_far = (swap_x(from_y[0]), swap_y(from_x[1]))
    frames = jnp.stack([2 * (me ^ group) + half for group in range(4) for half in range(2)])
    live = (frames[None, :] < frame_count[:, None]).astype(jnp.int32)
    made = ()
    media_gains = norm_gains[:, 0:2]
    for group, parts in enumerate((own, from_x, from_y, from_far)):
        made = media_part(parts[0], parts[1], media_gains, pair_weights, group, made)
    keys, media_hat = made

    kept = []
    for layer in range(layers):
        query_weight, out_weight = query_full[layer], out_full[layer]
        pair_weight = pair_weights[:, 2 * layer * head_columns : 2 * (layer + 1) * head_columns]
        query = mm(flat(latent_norm), query_weight)
        latent_pair = mm(flat(latent_norm), pair_weight)
        mixed = attend_fast(live, query, latent_pair, keys, layer, scale)
        part = mm(mixed, out_weight, NT).reshape(videos, latent_count, width)
        middle, feed_norm = forward_exchange(part, latent, norm_gains[layer, 4:6], heads_count)
        hidden_pre = mm(flat(feed_norm), widen_full[layer], None, F32)
        hidden = jax.nn.gelu(hidden_pre).astype(BF)
        part = mm(hidden, narrow_full[layer], NT).reshape(videos, latent_count, width)
        last = layer == layers - 1
        gain = norm_gains[0 if last else layer + 1, 2:4]
        kept.append((latent, middle, latent_norm, query, latent_pair, mixed, feed_norm, hidden_pre, hidden))
        if last:
            latent = middle
            for group, swap in enumerate((None, X_SWAP, Y_SWAP, FAR_SWAP)):
                term = lax.dynamic_slice_in_dim(part, (me ^ group) * share, share, axis=1)
                latent = latent + (lax.ppermute(term, "heads", swap) if swap else term).astype(F32)
        else:
            latent, latent_norm = forward_exchange(part, middle, gain, heads_count)

    slope = cotangent
    gain_parts = [None] * layers
    shares, waiting = [], []
    media_slopes = ()

    scaled = jnp.concatenate(
        [
            (
                pair_weights[:, 2 * l * head_columns : 2 * (l + 1) * head_columns].astype(F32)
                * norm_gains[l, 0][:, None]
            ).astype(BF)
            for l in range(layers)
        ],
        axis=1,
    )

    def hat_slope(slopes, group, half):
        return mm(flat(slopes[2 * group + half]), scaled, NT).reshape(videos, -1, width)

    summed = []

    def scatter_rows(gradient):
        if summed:
            gradient, _ = lax.optimization_barrier((gradient, summed[-1]))
        summed.append(lax.psum_scatter(gradient, "rows", scatter_dimension=0, tiled=True))
        return summed[-1]

    for layer in reversed(range(layers)):
        latent_in, middle, latent_norm, query, latent_pair, mixed, feed_norm, hidden_pre, hidden = kept[layer]
        query_weight, out_weight = query_full[layer], out_full[layer]
        pair_weight = pair_weights[:, 2 * layer * head_columns : 2 * (layer + 1) * head_columns]
        feed_slope = flat(feed_slope)
        hidden_slope = mm(feed_slope, narrow_full[layer], None, F32)
        _, gelu_back = jax.vjp(jax.nn.gelu, hidden_pre)
        pre_slope = gelu_back(hidden_slope)[0].astype(BF)
        part = mm(pre_slope, widen_full[layer], NT).reshape(videos, latent_count, width)
        feed_grad = product_pair(feed_slope, hidden, flat(feed_norm), pre_slope, *waiting)
        part, feed_grad = lax.optimization_barrier((part, feed_grad))
        shares.append(scatter_rows(feed_grad))
        middle_slope, feed_sums, branch_slope = backward_exchange(
            part, middle, slope, norm_gains[layer, 4:6], heads_count
        )
        branch_slope = flat(branch_slope)
        mixed_slope = mm(branch_slope, out_weight)
        out_grad = mm(branch_slope, mixed, TN)
        query_slope, latent_slopes, media_slopes = attend_back_fast(
            live, query, latent_pair, keys, mixed_slope, layer, scale, (media_slopes,) if layer < layers - 1 else ()
        )
        part = (mm(query_slope, query_weight, NT, F32) + mm(latent_slopes, pair_weight, NT, F32)).astype(BF)
        part = part.reshape(videos, latent_count, width)
        last = layer == 0
        slope, latent_sums, feed_slope = backward_exchange(
            part, latent_in, middle_slope, norm_gains[layer, 2:4], heads_count, last
        )
        if last:
            media_slopes, slope = lax.optimization_barrier((media_slopes, slope))
            far = [hat_slope(media_slopes, 3, half) for half in range(2)]
            media_slopes, *far = lax.optimization_barrier((media_slopes, *far))
            over_x, over_y = swap_x(far[0]), swap_y(far[1])
            near = [hat_slope(media_slopes, 1, 0), hat_slope(media_slopes, 2, 1)]
            media_slopes, *near = lax.optimization_barrier((media_slopes, *near))
            in_x, in_y = [swap_x(near[0]), None], [None, swap_y(near[1])]
            near = [hat_slope(media_slopes, 1, 1), hat_slope(media_slopes, 2, 0)]
            media_slopes, *near = lax.optimization_barrier((media_slopes, *near))
        query_grad = mm(flat(latent_norm), query_slope, TN)
        pair_slope = flat(media_slopes[..., 2 * layer * head_columns : 2 * (layer + 1) * head_columns])
        hat_grad = mm(flat(media_hat), pair_slope, TN, F32)
        slope_sum = jnp.sum(pair_slope.astype(F32), axis=0)
        gain, shift = norm_gains[layer, 0], norm_gains[layer, 1]
        pair_grad = (
            mm(flat(latent_norm), latent_slopes, TN, F32)
            + gain[:, None] * hat_grad
            + shift[:, None] * slope_sum[None, :]
        ).astype(BF)
        wide = pair_weight.astype(F32)
        media_sums = jnp.stack(
            (jnp.sum(wide * hat_grad, axis=1), jnp.sum(wide * slope_sum[None, :], axis=1))
        )
        inward_grad = jnp.concatenate((out_grad, query_grad, pair_grad), axis=1)
        if last:
            inward_grad, over_x, over_y, in_x[0], in_y[1] = lax.optimization_barrier(
                (inward_grad, over_x, over_y, in_x[0], in_y[1])
            )
            shares.append(scatter_rows(inward_grad))
        else:
            inward_grad, latent = lax.optimization_barrier((inward_grad, latent))
            waiting = [inward_grad]
        gain_parts[layer] = jnp.concatenate((media_sums, latent_sums, feed_sums), axis=0)

    back = [hat_slope(media_slopes, 0, half).astype(F32) for half in range(2)]
    in_x[1] = swap_x(near[0] + over_y)
    in_y[0] = swap_y(near[1] + over_x)

    def square_sum(rows):
        wide = rows.astype(F32)
        return jnp.sum(wide * wide)

    early = sum(square_sum(piece) for piece in shares[:-1])
    in_x[1], in_y[0], early = lax.optimization_barrier((in_x[1], in_y[0], early))
    rows = jnp.stack(own, axis=1).astype(F32)
    total = jnp.stack(back, axis=1) + jnp.stack(in_x, axis=1).astype(F32) + jnp.stack(in_y, axis=1).astype(F32)
    centred = rows - jnp.mean(rows, axis=-1, keepdims=True)
    spread = lax.rsqrt(jnp.mean(centred * centred, axis=-1, keepdims=True) + EPS_NORM)
    hat = centred * spread
    total = total - jnp.mean(total, axis=-1, keepdims=True) - hat * jnp.mean(total * hat, axis=-1, keepdims=True)
    media_slope = (total * spread).reshape(videos, local_positions, width)
    media_slope = jnp.swapaxes(media_slope, 0, 1)

    media_slope, shares[-1] = lax.optimization_barrier((media_slope, shares[-1]))
    gain_term = jnp.concatenate(gain_parts, axis=0).reshape(heads_count, -1, 128)
    lines = gain_term.shape[1]
    squares = jnp.full((heads_count, 8 - lines % 8, 128), early + square_sum(shares[-1]), F32)
    totals = sum_fast(jnp.concatenate((gain_term, squares), axis=1), heads_count, rows_count, 6)
    gain_total = totals[:, :lines].reshape(layers, 6, width)
    square_total = totals[0, lines, 0]
    feed_parts = [piece[:, : 2 * units] for piece in shares[-2::-1]]
    inward_parts = [shares[-1]] + [piece[:, 2 * units :] for piece in shares[-2:0:-1]]
    gradient_norm = jnp.sqrt(square_total + jnp.sum(gain_total * gain_total))
    factor = CLIP_LEVEL / jnp.maximum(gradient_norm, CLIP_LEVEL)

    def wide_part(parts, begin, end):
        return jnp.stack([piece[:, begin:end] for piece in parts]).astype(F32)

    inward_grad = jnp.stack(
        [wide_part(inward_parts, (1 + t) * columns, (2 + t) * columns) for t in range(3)], axis=1
    )
    table = (
        (inward, inward_first, inward_second, inward_grad, RATE_INWARD),
        (outward, outward_first, outward_second, jnp.swapaxes(wide_part(inward_parts, 0, columns), 1, 2), RATE_OUTWARD),
        (widen, widen_first, widen_second, wide_part(feed_parts, units, None), RATE_WIDEN),
        (narrow, narrow_first, narrow_second, jnp.swapaxes(wide_part(feed_parts, 0, units), 1, 2), RATE_NARROW),
    )
    results = [latent, slope, media_slope, gradient_norm]
    for weight, first, second, gradient, rate in table:
        mean_new, square_new, weight_new = adam_step(
            weight, first, second, gradient * factor, rate, WEIGHT_DECAY
        )
        results = results + [mean_new, square_new, weight_new, weight_new.astype(BF)]
    mean_new, square_new, weight_new = adam_step(
        norm_gains, gain_first, gain_second, gain_total * factor, RATE_GAINS, 0.0
    )
    results = results + [mean_new, square_new, weight_new, gain_total[:, 4:6]]
    return tuple(results)


def solution(mesh):
    placed = (
        P("heads", "rows", None),
        P("rows", "heads", None),
        P("rows"),
        P("rows", "heads", None),
        P(None, None, "rows", "heads"),
        P(None, None, "rows", "heads"),
        P(None, None, "rows", "heads"),
        P(None, "heads", "rows"),
        P(None, "heads", "rows"),
        P(None, "heads", "rows"),
        P(None, "rows", "heads"),
        P(None, "rows", "heads"),
        P(None, "rows", "heads"),
        P(None, "heads", "rows"),
        P(None, "heads", "rows"),
        P(None, "heads", "rows"),
        P(),
        P(),
        P(),
    )
    local = local_fast if (mesh.shape["rows"], mesh.shape["heads"]) == (8, 4) else local_plain
    return jax.shard_map(
        local,
        mesh=mesh,
        in_specs=placed,
        out_specs=(
            P("rows", "heads", None),
            P("rows", "heads", None),
            P("heads", "rows", None),
            P(),
            P(None, None, "rows", "heads"),
            P(None, None, "rows", "heads"),
            P(None, None, "rows", "heads"),
            P(None, None, "rows", "heads"),
            P(None, "heads", "rows"),
            P(None, "heads", "rows"),
            P(None, "heads", "rows"),
            P(None, "heads", "rows"),
            P(None, "rows", "heads"),
            P(None, "rows", "heads"),
            P(None, "rows", "heads"),
            P(None, "rows", "heads"),
            P(None, "heads", "rows"),
            P(None, "heads", "rows"),
            P(None, "heads", "rows"),
            P(None, "heads", "rows"),
            P(),
            P(),
            P(),
            P(),
        ),
        check_vma=False,
    )
```

```python
import functools

import jax
import jax.numpy as jnp
from jax import lax
from jax.experimental import pallas as pl
from jax.experimental.pallas import tpu as pltpu
from jax.sharding import PartitionSpec as P

HD = 96
STEP = 10
PATCHES = 128


EPS_NORM = 1e-05
BETA_ONE = 0.5
BETA_TWO = 0.5
ADAM_EPS = 1e-08
WEIGHT_DECAY = 0.1
CLIP_LEVEL = 1.0
MASKED_SCORE = -1e30
RATE_INWARD = 0.02
RATE_OUTWARD = 0.5
RATE_WIDEN = 0.02
RATE_NARROW = 0.01
RATE_GAINS = 0.1


def layer_norm(rows, gain, shift):
    middle = jnp.mean(rows, axis=-1, keepdims=True)
    centred = rows - middle
    spread = jnp.mean(centred * centred, axis=-1, keepdims=True)
    return centred * lax.rsqrt(spread + EPS_NORM) * gain + shift


def norm_back(rows, gain, shift, slope):
    _, pullback = jax.vjp(layer_norm, rows, gain, shift)
    return pullback(slope)


def adam_step(weight, first, second, gradient, rate, decay):
    mean_new = BETA_ONE * first + (1.0 - BETA_ONE) * gradient
    square_new = BETA_TWO * second + (1.0 - BETA_TWO) * gradient * gradient
    mean_hat = mean_new / (1.0 - BETA_ONE**STEP)
    square_hat = square_new / (1.0 - BETA_TWO**STEP)
    weight_new = weight - rate * (mean_hat / (jnp.sqrt(square_hat) + ADAM_EPS) + decay * weight)
    return (mean_new, square_new, weight_new)


def gather_slots(rows):
    return lax.all_gather(rows, HEADS, axis=1, tiled=True)


def scatter_slots(terms):
    return lax.psum_scatter(terms, HEADS, scatter_dimension=1, tiled=True)


def gather_slopes(rows):
    return lax.all_gather(rows, HEADS, axis=1, tiled=True)


def scatter_slopes(terms):
    return lax.psum_scatter(terms, HEADS, scatter_dimension=1, tiled=True)


def both_scores(query, media_pair, latent_pair, live, scale):
    score_media = (
        jnp.einsum("vnhe,pvhe->vhnp", query, media_pair[0], preferred_element_type=jnp.float32)
        * scale
    )
    score_media = jnp.where(live[:, None, None, :], score_media, MASKED_SCORE)
    score_latent = (
        jnp.einsum("vnhe,vmhe->vhnm", query, latent_pair[0], preferred_element_type=jnp.float32)
        * scale
    )
    return (score_media, score_latent)


def attend(query, media_pair, latent_pair, live, scale):
    score_media, score_latent = both_scores(query, media_pair, latent_pair, live, scale)
    top = jnp.maximum(
        jnp.max(score_media, axis=-1, keepdims=True), jnp.max(score_latent, axis=-1, keepdims=True)
    )
    exponent_media = jnp.exp(score_media - top)
    exponent_latent = jnp.exp(score_latent - top)
    total = jnp.sum(exponent_media, axis=-1, keepdims=True) + jnp.sum(
        exponent_latent, axis=-1, keepdims=True
    )
    share_media = (exponent_media / total).astype(jnp.bfloat16)
    share_latent = (exponent_latent / total).astype(jnp.bfloat16)
    mixed = jnp.einsum(
        "vhnp,pvhe->vnhe", share_media, media_pair[1], preferred_element_type=jnp.float32
    )
    mixed = mixed + jnp.einsum(
        "vhnm,vmhe->vnhe", share_latent, latent_pair[1], preferred_element_type=jnp.float32
    )
    return (mixed.astype(jnp.bfloat16), top + jnp.log(total))


def attend_back(query, media_pair, latent_pair, live, log_total, mixed_slope, scale):
    score_media, score_latent = both_scores(query, media_pair, latent_pair, live, scale)
    share_media = jnp.exp(score_media - log_total)
    share_latent = jnp.exp(score_latent - log_total)
    share_slope_media = jnp.einsum(
        "vnhe,pvhe->vhnp", mixed_slope, media_pair[1], preferred_element_type=jnp.float32
    )
    share_slope_latent = jnp.einsum(
        "vnhe,vmhe->vhnm", mixed_slope, latent_pair[1], preferred_element_type=jnp.float32
    )
    row_total = jnp.sum(share_media * share_slope_media, axis=-1, keepdims=True)
    row_total = row_total + jnp.sum(share_latent * share_slope_latent, axis=-1, keepdims=True)
    score_slope_media = (share_media * (share_slope_media - row_total)).astype(jnp.bfloat16)
    score_slope_latent = (share_latent * (share_slope_latent - row_total)).astype(jnp.bfloat16)
    query_slope = jnp.einsum(
        "vhnp,pvhe->vnhe", score_slope_media, media_pair[0], preferred_element_type=jnp.float32
    )
    query_slope = query_slope + jnp.einsum(
        "vhnm,vmhe->vnhe", score_slope_latent, latent_pair[0], preferred_element_type=jnp.float32
    )
    query_slope = (query_slope * scale).astype(jnp.bfloat16)
    key_media = (
        jnp.einsum("vhnp,vnhe->pvhe", score_slope_media, query, preferred_element_type=jnp.float32)
        * scale
    ).astype(jnp.bfloat16)
    value_media = jnp.einsum(
        "vhnp,vnhe->pvhe",
        share_media.astype(jnp.bfloat16),
        mixed_slope,
        preferred_element_type=jnp.float32,
    ).astype(jnp.bfloat16)
    key_latent = (
        jnp.einsum("vhnm,vnhe->vmhe", score_slope_latent, query, preferred_element_type=jnp.float32)
        * scale
    ).astype(jnp.bfloat16)
    value_latent = jnp.einsum(
        "vhnm,vnhe->vmhe",
        share_latent.astype(jnp.bfloat16),
        mixed_slope,
        preferred_element_type=jnp.float32,
    ).astype(jnp.bfloat16)
    return (query_slope, jnp.stack((key_media, value_media)), jnp.stack((key_latent, value_latent)))


def local_plain(
    media,
    latents,
    frame_count,
    cotangent,
    inward,
    inward_first,
    inward_second,
    outward,
    outward_first,
    outward_second,
    widen,
    widen_first,
    widen_second,
    narrow,
    narrow_first,
    narrow_second,
    norm_gains,
    gain_first,
    gain_second,
):
    heads_count = lax.axis_size(HEADS)
    layers, _, row_share, head_columns = inward.shape
    local_positions, videos, width = media.shape
    positions = local_positions * heads_count
    latent_count = latents.shape[1] * heads_count
    local_heads = head_columns // HD
    scale = HD ** (-0.5)
    live = (jnp.arange(positions, dtype=jnp.int32) // PATCHES)[None, :] < frame_count[:, None]
    inward_columns, outward_rows, widen_columns, narrow_rows = (
        lax.all_gather(inward.astype(jnp.bfloat16), ROWS, axis=2, tiled=True),
        lax.all_gather(outward.astype(jnp.bfloat16), ROWS, axis=2, tiled=True),
        lax.all_gather(widen.astype(jnp.bfloat16), ROWS, axis=1, tiled=True),
        lax.all_gather(narrow.astype(jnp.bfloat16), ROWS, axis=2, tiled=True),
    )
    media_rows = media.astype(jnp.float32)
    latent = latents
    kept = []
    for layer in range(layers):
        gains = norm_gains[layer]
        media_norm = layer_norm(media_rows, gains[0], gains[1]).astype(jnp.bfloat16)
        latent_norm = gather_slots(layer_norm(latent, gains[2], gains[3]).astype(jnp.bfloat16))
        triple = jnp.einsum(
            "vnd,tdc->tvnc", latent_norm, inward_columns[layer], preferred_element_type=jnp.float32
        ).astype(jnp.bfloat16)
        pair_columns = inward_columns[layer, 1:3]
        media_pair = jnp.einsum(
            "pvd,tdc->tpvc",
            lax.all_gather(media_norm, HEADS, axis=0, tiled=True),
            pair_columns,
            preferred_element_type=jnp.float32,
        ).astype(jnp.bfloat16)
        query = triple[0].reshape(videos, latent_count, local_heads, HD)
        latent_pair = triple[1:3].reshape(2, videos, latent_count, local_heads, HD)
        heads_pair = media_pair.reshape(2, positions, videos, local_heads, HD)
        mixed, log_total = attend(query, heads_pair, latent_pair, live, scale)
        mixed = mixed.reshape(videos, latent_count, head_columns)
        middle = latent + scatter_slots(
            jnp.einsum(
                "vnc,cd->vnd", mixed, outward_rows[layer], preferred_element_type=jnp.float32
            )
        )
        feed_norm = gather_slots(layer_norm(middle, gains[4], gains[5]).astype(jnp.bfloat16))
        hidden_pre = jnp.einsum(
            "vnd,df->vnf", feed_norm, widen_columns[layer], preferred_element_type=jnp.float32
        )
        hidden = jax.nn.gelu(hidden_pre).astype(jnp.bfloat16)
        kept.append(
            (
                latent,
                middle,
                media_norm,
                latent_norm,
                query,
                heads_pair,
                latent_pair,
                mixed,
                log_total,
                feed_norm,
                hidden_pre,
                hidden,
            )
        )
        latent = middle + scatter_slots(
            jnp.einsum(
                "vnf,fd->vnd", hidden, narrow_rows[layer], preferred_element_type=jnp.float32
            )
        )
    slope = cotangent
    media_slope = jnp.zeros(media_rows.shape, jnp.float32)
    inward_parts, outward_parts, widen_parts, narrow_parts, gain_parts = ([], [], [], [], [])
    for layer in reversed(range(layers)):
        (
            latent_in,
            middle,
            media_norm,
            latent_norm,
            query,
            heads_pair,
            latent_pair,
            mixed,
            log_total,
            feed_norm,
            hidden_pre,
            hidden,
        ) = kept[layer]
        gains = norm_gains[layer]
        feed_slope = gather_slopes(slope.astype(jnp.bfloat16))
        narrow_grad = jnp.einsum(
            "vnf,vnd->fd", hidden, feed_slope, preferred_element_type=jnp.float32
        )
        hidden_slope = jnp.einsum(
            "vnd,fd->vnf", feed_slope, narrow_rows[layer], preferred_element_type=jnp.float32
        )
        _, gelu_back = jax.vjp(jax.nn.gelu, hidden_pre)
        pre_slope = gelu_back(hidden_slope)[0].astype(jnp.bfloat16)
        widen_grad = jnp.einsum(
            "vnd,vnf->df", feed_norm, pre_slope, preferred_element_type=jnp.float32
        )
        norm_slope = scatter_slopes(
            jnp.einsum(
                "vnf,df->vnd", pre_slope, widen_columns[layer], preferred_element_type=jnp.float32
            )
        )
        middle_part, gain_feed, shift_feed = norm_back(middle, gains[4], gains[5], norm_slope)
        middle_slope = slope + middle_part
        branch_slope = gather_slopes(middle_slope.astype(jnp.bfloat16))
        outward_grad = jnp.einsum(
            "vnc,vnd->cd", mixed, branch_slope, preferred_element_type=jnp.float32
        )
        mixed_slope = jnp.einsum(
            "vnd,cd->vnc", branch_slope, outward_rows[layer], preferred_element_type=jnp.float32
        ).astype(jnp.bfloat16)
        mixed_slope = mixed_slope.reshape(videos, latent_count, local_heads, HD)
        query_slope, media_slopes, latent_slopes = attend_back(
            query, heads_pair, latent_pair, live, log_total, mixed_slope, scale
        )
        triple_slope = jnp.concatenate(
            (
                query_slope.reshape(1, videos, latent_count, head_columns),
                latent_slopes.reshape(2, videos, latent_count, head_columns),
            ),
            axis=0,
        )
        inward_grad = jnp.einsum(
            "vnd,tvnc->tdc", latent_norm, triple_slope, preferred_element_type=jnp.float32
        )
        norm_slope = scatter_slopes(
            jnp.einsum(
                "tvnc,tdc->vnd",
                triple_slope,
                inward_columns[layer],
                preferred_element_type=jnp.float32,
            )
        )
        latent_part, gain_latent, shift_latent = norm_back(
            latent_in, gains[2], gains[3], norm_slope
        )
        slope = middle_slope + latent_part
        pair_slope = media_slopes.reshape(2, positions, videos, head_columns)
        media_columns = jnp.einsum(
            "pvd,tpvc->tdc",
            lax.all_gather(media_norm, HEADS, axis=0, tiled=True),
            pair_slope,
            preferred_element_type=jnp.float32,
        )
        inward_grad = jnp.concatenate((inward_grad[:1], inward_grad[1:] + media_columns), axis=0)
        pair_columns = inward_columns[layer, 1:3]
        media_norm_slope = lax.psum_scatter(
            jnp.einsum(
                "tpvc,tdc->pvd", pair_slope, pair_columns, preferred_element_type=jnp.float32
            ),
            HEADS,
            scatter_dimension=0,
            tiled=True,
        )
        media_part, gain_media, shift_media = norm_back(
            media_rows, gains[0], gains[1], media_norm_slope
        )
        media_slope = media_slope + media_part
        inward_parts.append(inward_grad)
        outward_parts.append(outward_grad)
        widen_parts.append(widen_grad)
        narrow_parts.append(narrow_grad)
        gain_parts.append(
            jnp.stack((gain_media, shift_media, gain_latent, shift_latent, gain_feed, shift_feed))
        )
    inward_grad, outward_grad, widen_grad, narrow_grad = (
        lax.psum_scatter(jnp.stack(inward_parts[::-1]), ROWS, scatter_dimension=2, tiled=True),
        lax.psum_scatter(jnp.stack(outward_parts[::-1]), ROWS, scatter_dimension=2, tiled=True),
        lax.psum_scatter(jnp.stack(widen_parts[::-1]), ROWS, scatter_dimension=1, tiled=True),
        lax.psum_scatter(jnp.stack(narrow_parts[::-1]), ROWS, scatter_dimension=2, tiled=True),
    )
    squares = jnp.sum(inward_grad * inward_grad) + jnp.sum(outward_grad * outward_grad)
    squares = squares + jnp.sum(widen_grad * widen_grad) + jnp.sum(narrow_grad * narrow_grad)
    gain_total, square_total = lax.psum((jnp.stack(gain_parts[::-1]), squares), (ROWS, HEADS))
    gradient_norm = jnp.sqrt(square_total + jnp.sum(gain_total * gain_total))
    factor = CLIP_LEVEL / jnp.maximum(gradient_norm, CLIP_LEVEL)
    table = (
        (inward, inward_first, inward_second, inward_grad, RATE_INWARD, WEIGHT_DECAY),
        (outward, outward_first, outward_second, outward_grad, RATE_OUTWARD, WEIGHT_DECAY),
        (widen, widen_first, widen_second, widen_grad, RATE_WIDEN, WEIGHT_DECAY),
        (narrow, narrow_first, narrow_second, narrow_grad, RATE_NARROW, WEIGHT_DECAY),
    )
    results = [latent, slope, media_slope, gradient_norm]
    for weight, first, second, gradient, rate, decay in table:
        mean_new, square_new, weight_new = adam_step(
            weight, first, second, gradient * factor, rate, decay
        )
        results = results + [mean_new, square_new, weight_new, weight_new.astype(jnp.bfloat16)]
    mean_new, square_new, weight_new = adam_step(
        norm_gains, gain_first, gain_second, gain_total * factor, RATE_GAINS, 0.0
    )
    results = results + [mean_new, square_new, weight_new, gain_total[:, 4:6]]
    return tuple(results)


BF = jnp.bfloat16
F32 = jnp.float32
MIB = 1024 * 1024
HEADS, ROWS = "heads", "rows"
NT = (((1,), (1,)), ((), ()))
TN = (((0,), (0,)), ((), ()))
X_SWAP = ((0, 1), (1, 0), (2, 3), (3, 2))
Y_SWAP = ((0, 2), (2, 0), (1, 3), (3, 1))
FAR_SWAP = ((0, 3), (3, 0), (1, 2), (2, 1))


def vmem_spec():
    return pl.BlockSpec(memory_space=pltpu.VMEM)


def mm(left, right, dims=None, out=BF):
    dims = dims or (((1,), (0,)), ((), ()))
    return lax.dot_general(left, right, dims, preferred_element_type=F32).astype(out)


def greet(count):
    me = lax.axis_index(HEADS)
    barrier = pltpu.get_barrier_semaphore()
    for step in range(1, count):
        pl.semaphore_signal(barrier, inc=1, device_id={HEADS: (me + step) % count})
    pl.semaphore_wait(barrier, count - 1)
    return me


def own_rows(ref, place, share):
    return ref.at[:, pl.ds(pl.multiple_of(place * share, share), share), :]


def start_gather(me, count, share, own_ref, full_ref, send_sem, recv_sem):
    copies = []
    for step in range(1, count):
        copy = pltpu.make_async_remote_copy(
            src_ref=own_ref,
            dst_ref=own_rows(full_ref, me, share),
            send_sem=send_sem.at[step - 1],
            recv_sem=recv_sem.at[step - 1],
            device_id={HEADS: (me + step) % count},
        )
        copy.start()
        copies.append(copy)
    return copies


def beside(me):
    return me + 1 - 2 * (me % 2), me + 2 - 4 * (me // 2)


def gather_kernel(count, own_ref, norm_ref, near_ref, full_ref, send_sem, recv_sem, norm_send, norm_recv):
    me = greet(count)
    beside_x, beside_y = beside(me)
    share = norm_ref.shape[1]
    copies = start_gather(me, count, share, norm_ref, full_ref, norm_send, norm_recv)
    for at, (half, slot, peer) in enumerate(
        ((1, 1, beside_x), (0, 2, beside_y), (0, 0, beside_x), (1, 3, beside_y))
    ):
        copy = pltpu.make_async_remote_copy(
            src_ref=own_ref.at[half],
            dst_ref=near_ref.at[slot],
            send_sem=send_sem.at[at],
            recv_sem=recv_sem.at[at],
            device_id={HEADS: peer},
        )
        copy.start()
        copies.append(copy)
    full_ref[:, pl.ds(pl.multiple_of(me * share, share), share), :] = norm_ref[...]
    for copy in copies:
        copy.wait()


def gather_near(own, norm, count):
    videos, share, width = norm.shape
    any_spec = pl.BlockSpec(memory_space=pl.ANY)
    return pl.pallas_call(
        functools.partial(gather_kernel, count),
        out_shape=(
            jax.ShapeDtypeStruct((4, *own.shape[1:]), BF),
            jax.ShapeDtypeStruct((videos, share * count, width), BF),
        ),
        in_specs=[any_spec, vmem_spec()],
        out_specs=(any_spec, vmem_spec()),
        scratch_shapes=[pltpu.SemaphoreType.DMA((4,))] * 2 + [pltpu.SemaphoreType.DMA((count - 1,))] * 2,
        compiler_params=pltpu.CompilerParams(
            collective_id=1, has_side_effects=True, vmem_limit_bytes=60 * MIB
        ),
        cost_estimate=pl.CostEstimate(flops=0, bytes_accessed=250 * 1000 * 1000, transcendentals=0),
        name="gather_near",
    )(own, norm)


def media_rows(half, layer, chunk_ref, gain_ref, weight_ref, keys_ref, hat_ref, rows_ref, other_ref=None):
    @pl.when(layer == 0)
    def _():
        if other_ref is None:
            rows_ref[...] = chunk_ref[0].astype(F32).reshape(rows_ref.shape)
        else:

            @pl.when(half < 2)
            def _():
                rows_ref[...] = chunk_ref[0].astype(F32).reshape(rows_ref.shape)

            @pl.when(half >= 2)
            def _():
                rows_ref[...] = other_ref[0].astype(F32).reshape(rows_ref.shape)

        rows = rows_ref[...]
        centred = rows - jnp.mean(rows, axis=-1, keepdims=True)
        spread = jnp.mean(centred * centred, axis=-1, keepdims=True)
        hat = centred * lax.rsqrt(spread + EPS_NORM)
        rows_ref[...] = hat
        hat_ref[...] = hat.astype(BF).reshape(hat_ref.shape)

    gain = gain_ref[pl.ds(layer, 1), 0]
    shift = gain_ref[pl.ds(layer, 1), 1]
    normed = (rows_ref[...] * gain + shift).astype(BF)
    keys_ref[...] = jnp.dot(normed, weight_ref[...], preferred_element_type=F32).astype(BF).reshape(keys_ref.shape)


def near_kernel(
    count, own_ref, near_ref, gain_ref, weight_ref, source_ref, keys_ref, hat_ref, far_ref, rows_ref, send_sem, recv_sem
):
    half, layer = pl.program_id(0), pl.program_id(1)
    me = lax.axis_index(HEADS)
    beside_x, beside_y = beside(me)

    def relays():
        return [
            pltpu.make_async_remote_copy(
                src_ref=source_ref.at[slot],
                dst_ref=far_ref.at[at],
                send_sem=send_sem.at[at],
                recv_sem=recv_sem.at[at],
                device_id={HEADS: peer},
            )
            for at, (slot, peer) in enumerate(((2, beside_x), (1, beside_y)))
        ]

    @pl.when((half == 0) & (layer == 0))
    def _():
        barrier = pltpu.get_barrier_semaphore()
        for peer in (beside_x, beside_y):
            pl.semaphore_signal(barrier, inc=1, device_id={HEADS: peer})
        pl.semaphore_wait(barrier, 2)
        for copy in relays():
            copy.start()

    media_rows(half, layer, own_ref, gain_ref, weight_ref, keys_ref, hat_ref, rows_ref, near_ref)

    @pl.when((half == 5) & (layer == 1))
    def _():
        for copy in relays():
            copy.wait()


def media_near(own, near, gains, weight, columns, count):
    _, videos, patches, width = own.shape
    rows = videos * patches
    any_spec = pl.BlockSpec(memory_space=pl.ANY)
    return pl.pallas_call(
        functools.partial(near_kernel, count),
        grid=(6, 2),
        out_shape=(
            jax.ShapeDtypeStruct((8, videos, patches, columns), BF),
            jax.ShapeDtypeStruct((8, videos, patches, width), BF),
            jax.ShapeDtypeStruct(own.shape, BF),
        ),
        in_specs=[
            pl.BlockSpec((1, videos, patches, width), lambda i, j: (jnp.minimum(i, 1), 0, 0, 0)),
            pl.BlockSpec((1, videos, patches, width), lambda i, j: (jnp.maximum(i - 2, 0), 0, 0, 0)),
            pl.BlockSpec(gains.shape, lambda i, j: (0, 0, 0)),
            pl.BlockSpec((width, columns // 2), lambda i, j: (0, j)),
            any_spec,
        ],
        out_specs=(
            pl.BlockSpec((1, videos, patches, columns // 2), lambda i, j: (i, 0, 0, j)),
            pl.BlockSpec((1, videos, patches, width), lambda i, j: (i, 0, 0, 0)),
            any_spec,
        ),
        scratch_shapes=[
            pltpu.VMEM((rows, width), F32),
            pltpu.SemaphoreType.DMA((2,)),
            pltpu.SemaphoreType.DMA((2,)),
        ],
        compiler_params=pltpu.CompilerParams(
            collective_id=6, has_side_effects=True, vmem_limit_bytes=60 * MIB
        ),
        cost_estimate=pl.CostEstimate(
            flops=12 * rows * width * columns, bytes_accessed=24 * rows * width, transcendentals=0
        ),
        name="media_near",
    )(own, near, gains, weight, near)


def far_kernel(
    count, chunk_ref, gain_ref, weight_ref, slope_ref, keys_in, hat_in, keys_ref, hat_ref, full_ref, rows_ref, *sems
):
    half, layer = pl.program_id(0), pl.program_id(1)
    send_sem, recv_sem, own_sem = sems
    me = lax.axis_index(HEADS)
    share = slope_ref.shape[1]

    def copies():
        return [
            pltpu.make_async_remote_copy(
                src_ref=slope_ref,
                dst_ref=own_rows(full_ref, me, share),
                send_sem=send_sem.at[step - 1],
                recv_sem=recv_sem.at[step - 1],
                device_id={HEADS: (me + step) % count},
            )
            for step in range(1, count)
        ] + [pltpu.make_async_copy(slope_ref, own_rows(full_ref, me, share), own_sem)]

    @pl.when((half == 0) & (layer == 0))
    def _():
        greet(count)
        for copy in copies():
            copy.start()

    media_rows(half, layer, chunk_ref, gain_ref, weight_ref, keys_ref, hat_ref, rows_ref)

    @pl.when((half == 1) & (layer == 1))
    def _():
        for copy in copies():
            copy.wait()


def media_far(far, gains, weight, slope, keys, hat, count):
    _, videos, patches, width = far.shape
    columns = keys.shape[3]
    rows = videos * patches
    share = slope.shape[1]
    any_spec = pl.BlockSpec(memory_space=pl.ANY)
    return pl.pallas_call(
        functools.partial(far_kernel, count),
        grid=(2, 2),
        out_shape=(
            jax.ShapeDtypeStruct(keys.shape, BF),
            jax.ShapeDtypeStruct(hat.shape, BF),
            jax.ShapeDtypeStruct((videos, share * count, width), BF),
        ),
        in_specs=[
            pl.BlockSpec((1, videos, patches, width), lambda i, j: (i, 0, 0, 0)),
            pl.BlockSpec(gains.shape, lambda i, j: (0, 0, 0)),
            pl.BlockSpec((width, columns // 2), lambda i, j: (0, j)),
            any_spec,
            any_spec,
            any_spec,
        ],
        out_specs=(
            pl.BlockSpec((1, videos, patches, columns // 2), lambda i, j: (6 + i, 0, 0, j)),
            pl.BlockSpec((1, videos, patches, width), lambda i, j: (6 + i, 0, 0, 0)),
            any_spec,
        ),
        scratch_shapes=[
            pltpu.VMEM((rows, width), F32),
            pltpu.SemaphoreType.DMA((count - 1,)),
            pltpu.SemaphoreType.DMA((count - 1,)),
            pltpu.SemaphoreType.DMA,
        ],
        input_output_aliases={4: 0, 5: 1},
        compiler_params=pltpu.CompilerParams(
            collective_id=8, has_side_effects=True, vmem_limit_bytes=60 * MIB
        ),
        cost_estimate=pl.CostEstimate(
            flops=4 * rows * width * columns, bytes_accessed=8 * rows * width, transcendentals=0
        ),
        name="media_far",
    )(far, gains, weight, slope, keys, hat)


def head_mask(rows, columns, head):
    place = lax.broadcasted_iota(jnp.int32, (rows, columns), 1)
    return (place >= head * HD) & (place < (head + 1) * HD)


def spread_heads(rows):
    heads = rows.shape[1] // HD
    zero = jnp.zeros_like(rows)
    return jnp.concatenate(
        [jnp.where(head_mask(*rows.shape, head), rows, zero) for head in range(heads)], axis=0
    )


def gather_heads(rows, count):
    heads = rows.shape[1] // HD
    total = jnp.zeros((count, rows.shape[1]), F32)
    for head in range(heads):
        part = rows[head * count : (head + 1) * count]
        total = total + jnp.where(head_mask(*part.shape, head), part, 0.0)
    return total


def attend_kernel(live_ref, query_ref, latent_key_ref, latent_value_ref, key_ref, value_ref, mixed_ref, *, scale):
    video = pl.program_id(0)
    slots, patches = key_ref.shape[0], key_ref.shape[2]
    query = spread_heads(query_ref[...])
    rows, columns = query.shape
    place = lax.broadcasted_iota(jnp.int32, (rows, 2 * patches), 1)
    scores = []
    for pair in range(slots // 2):
        keys = key_ref[2 * pair : 2 * pair + 2, 0].reshape(2 * patches, columns)
        score = lax.dot_general(query, keys, NT, preferred_element_type=F32) * scale
        live = jnp.where(place < patches, live_ref[video, 2 * pair], live_ref[video, 2 * pair + 1])
        scores.append(jnp.where(live > 0, score, MASKED_SCORE))
    scores.append(lax.dot_general(query, latent_key_ref[...], NT, preferred_element_type=F32) * scale)
    top = functools.reduce(jnp.maximum, [jnp.max(score, axis=-1, keepdims=True) for score in scores])
    exponents = [jnp.exp(score - top) for score in scores]
    total = functools.reduce(jnp.add, [jnp.sum(e, axis=-1, keepdims=True) for e in exponents])
    mixed = jnp.zeros((rows, columns), F32)
    for pair in range(slots // 2):
        values = value_ref[2 * pair : 2 * pair + 2, 0].reshape(2 * patches, columns)
        mixed = mixed + jnp.dot((exponents[pair] / total).astype(BF), values, preferred_element_type=F32)
    mixed = mixed + jnp.dot(
        (exponents[-1] / total).astype(BF), latent_value_ref[...], preferred_element_type=F32
    )
    mixed_ref[...] = gather_heads(mixed, query_ref.shape[0]).astype(BF)


def attend_fast(live, query, latent_pair, keys, layer, scale):
    slots, videos, patches, _ = keys.shape
    count, columns = query.shape[0] // videos, query.shape[1]
    row_block = pl.BlockSpec((count, columns), lambda v: (v, 0))
    return pl.pallas_call(
        functools.partial(attend_kernel, scale=scale),
        grid=(videos,),
        out_shape=jax.ShapeDtypeStruct(query.shape, BF),
        in_specs=[
            pl.BlockSpec(memory_space=pltpu.SMEM),
            row_block,
            row_block,
            pl.BlockSpec((count, columns), lambda v: (v, 1)),
            pl.BlockSpec((slots, 1, patches, columns), lambda v: (0, v, 0, 2 * layer)),
            pl.BlockSpec((slots, 1, patches, columns), lambda v: (0, v, 0, 2 * layer + 1)),
        ],
        out_specs=row_block,
        compiler_params=pltpu.CompilerParams(vmem_limit_bytes=28 * MIB),
        cost_estimate=pl.CostEstimate(
            flops=8 * slots * patches * videos * count * 2 * columns,
            bytes_accessed=4 * slots * videos * patches * columns,
            transcendentals=slots * patches * videos * count * 4,
        ),
        name="attend",
    )(live, query, latent_pair, latent_pair, keys, keys)


def attend_back_kernel(
    live_ref, query_ref, latent_key_ref, latent_value_ref, key_ref, value_ref, slope_ref, *rest, scale
):
    query_slope_ref, latent_slope_ref, media_slope_ref = rest[-3:]
    video = pl.program_id(0)
    slots, patches = key_ref.shape[0], key_ref.shape[2]
    pairs = slots // 2
    count = query_ref.shape[0]
    query, slope = spread_heads(query_ref[...]), spread_heads(slope_ref[...])
    rows, columns = query.shape
    place = lax.broadcasted_iota(jnp.int32, (2 * patches, rows), 0)

    def keys_of(ref, pair):
        return ref[2 * pair : 2 * pair + 2, 0].reshape(2 * patches, columns)

    scores = []
    for pair in range(pairs):
        score = lax.dot_general(keys_of(key_ref, pair), query, NT, preferred_element_type=F32) * scale
        live = jnp.where(place < patches, live_ref[video, 2 * pair], live_ref[video, 2 * pair + 1])
        scores.append(jnp.where(live > 0, score, MASKED_SCORE))
    scores.append(lax.dot_general(latent_key_ref[...], query, NT, preferred_element_type=F32) * scale)
    top = functools.reduce(jnp.maximum, [jnp.max(score, axis=0, keepdims=True) for score in scores])
    exponents = [jnp.exp(score - top) for score in scores]
    total = functools.reduce(jnp.add, [jnp.sum(e, axis=0, keepdims=True) for e in exponents])
    shares = [e / total for e in exponents]
    share_slopes = [
        lax.dot_general(keys_of(value_ref, pair), slope, NT, preferred_element_type=F32)
        for pair in range(pairs)
    ]
    share_slopes.append(
        lax.dot_general(latent_value_ref[...], slope, NT, preferred_element_type=F32)
    )
    row_total = functools.reduce(
        jnp.add,
        [jnp.sum(a * b, axis=0, keepdims=True) for a, b in zip(shares, share_slopes)],
    )
    query_slope = jnp.zeros((rows, columns), F32)
    for at in range(pairs + 1):
        keys = keys_of(key_ref, at) if at < pairs else latent_key_ref[...]
        score_slope = (shares[at] * (share_slopes[at] - row_total)).astype(BF)
        key_slope = (jnp.dot(score_slope, query, preferred_element_type=F32) * scale).astype(BF)
        value_slope = jnp.dot(shares[at].astype(BF), slope, preferred_element_type=F32).astype(BF)
        query_slope = query_slope + lax.dot_general(
            score_slope, keys, TN, preferred_element_type=F32
        )
        if at < pairs:
            media_slope_ref[2 * at : 2 * at + 2, 0, :, :columns] = key_slope.reshape(2, patches, columns)
            media_slope_ref[2 * at : 2 * at + 2, 0, :, columns:] = value_slope.reshape(2, patches, columns)
        else:
            latent_slope_ref[:, :columns] = key_slope
            latent_slope_ref[:, columns:] = value_slope
    query_slope_ref[...] = (gather_heads(query_slope, count) * scale).astype(BF)


def attend_back_fast(live, query, latent_pair, keys, slope, layer, scale, earlier):
    slots, videos, patches, _ = keys.shape
    count, columns = query.shape[0] // videos, query.shape[1]
    row_block = pl.BlockSpec((count, columns), lambda v: (v, 0))
    in_specs = [
        pl.BlockSpec(memory_space=pltpu.SMEM),
        row_block,
        row_block,
        pl.BlockSpec((count, columns), lambda v: (v, 1)),
        pl.BlockSpec((slots, 1, patches, columns), lambda v: (0, v, 0, 2 * layer)),
        pl.BlockSpec((slots, 1, patches, columns), lambda v: (0, v, 0, 2 * layer + 1)),
        row_block,
    ]
    aliases = {}
    if earlier:
        in_specs += [pl.BlockSpec(memory_space=pl.ANY)]
        aliases = {7: 2}
    return pl.pallas_call(
        functools.partial(attend_back_kernel, scale=scale),
        grid=(videos,),
        out_shape=(
            jax.ShapeDtypeStruct(query.shape, BF),
            jax.ShapeDtypeStruct(latent_pair.shape, BF),
            jax.ShapeDtypeStruct(keys.shape, BF),
        ),
        in_specs=in_specs,
        out_specs=(
            row_block,
            pl.BlockSpec((count, 2 * columns), lambda v: (v, 0)),
            pl.BlockSpec((slots, 1, patches, 2 * columns), lambda v: (0, v, 0, layer)),
        ),
        input_output_aliases=aliases,
        compiler_params=pltpu.CompilerParams(vmem_limit_bytes=60 * MIB),
        cost_estimate=pl.CostEstimate(
            flops=20 * slots * patches * videos * count * 2 * columns,
            bytes_accessed=8 * slots * videos * patches * columns,
            transcendentals=slots * patches * videos * count * 4,
        ),
        name="attend_back",
    )(live, query, latent_pair, latent_pair, keys, keys, slope, *earlier)


def product_pair_kernel(first_ref, second_ref, third_ref, fourth_ref, *rest):
    out_ref = rest[-1]
    kind = pl.program_id(0) - (len(rest) - 1)

    @pl.when(kind == 0)
    def _():
        out_ref[...] = mm(first_ref[...], second_ref[...], TN)

    @pl.when(kind == 1)
    def _():
        out_ref[...] = mm(third_ref[...], fourth_ref[...], TN)

    if len(rest) > 1:
        @pl.when(kind < 0)
        def _():
            out_ref[...] = rest[0][...]


def product_pair(first, second, third, fourth, *extra):
    rows, width, columns = first.shape[0], first.shape[1], second.shape[1]
    cut = columns // 3
    left = pl.BlockSpec((rows, width), lambda i, j: (0, 0))
    first_kind = len(extra)

    def at(i, j, kind):
        return jnp.where(i == kind, j, jnp.where(i < kind, 0, 2))

    return pl.pallas_call(
        product_pair_kernel,
        grid=(2 + len(extra), 3),
        out_shape=jax.ShapeDtypeStruct((width, (2 + len(extra)) * columns), BF),
        in_specs=[
            left,
            pl.BlockSpec((rows, cut), lambda i, j: (0, at(i, j, first_kind))),
            left,
            pl.BlockSpec((rows, cut), lambda i, j: (0, at(i, j, first_kind + 1))),
        ]
        + [pl.BlockSpec((width, cut), lambda i, j: (0, at(i, j, 0)))] * len(extra),
        out_specs=pl.BlockSpec((width, cut), lambda i, j: (0, 3 * i + j)),
        compiler_params=pltpu.CompilerParams(vmem_limit_bytes=60 * MIB),
        cost_estimate=pl.CostEstimate(
            flops=4 * rows * width * columns, bytes_accessed=8 * width * columns, transcendentals=0
        ),
        name="feed_gradients",
    )(first, second, third, fourth, *extra)


def start_scatter(me, count, share, part_ref, landed_ref, send_sem, recv_sem):
    copies = []
    for step in range(1, count):
        peer = (me + step) % count
        copy = pltpu.make_async_remote_copy(
            src_ref=own_rows(part_ref, peer, share),
            dst_ref=landed_ref.at[step - 1],
            send_sem=send_sem.at[step - 1],
            recv_sem=recv_sem.at[step - 1],
            device_id={HEADS: peer},
        )
        copy.start()
        copies.append(copy)
    return copies


def forward_kernel(
    count, last, part_ref, rest_ref, gain_ref, new_ref, *refs
):
    refs = list(refs)
    full_ref = None if last else refs.pop(0)
    landed_ref, own_ref, send_sem, recv_sem, send_more, recv_more = refs
    me = greet(count)
    share = rest_ref.shape[1]
    copies = start_scatter(me, count, share, part_ref, landed_ref, send_sem, recv_sem)
    mine = pl.ds(pl.multiple_of(me * share, share), share)
    total = rest_ref[...] + part_ref[:, mine, :].astype(F32)
    for step, copy in enumerate(copies):
        copy.wait_recv()
        total = total + landed_ref[step].astype(F32)
    new_ref[...] = total
    if not last:
        own_ref[...] = layer_norm(total, gain_ref[0], gain_ref[1]).astype(BF)
        more = start_gather(me, count, share, own_ref, full_ref, send_more, recv_more)
        full_ref[:, mine, :] = own_ref[...]
        for copy in more:
            copy.wait()
    for copy in copies:
        copy.wait_send()


def forward_exchange(part, rest, gain, count, last=False):
    videos, share, width = rest.shape
    outs = [jax.ShapeDtypeStruct(rest.shape, F32)]
    if not last:
        outs.append(jax.ShapeDtypeStruct(part.shape, BF))
    got = pl.pallas_call(
        functools.partial(forward_kernel, count, last),
        out_shape=tuple(outs),
        in_specs=[vmem_spec()] * 3,
        out_specs=(vmem_spec(),) * len(outs),
        scratch_shapes=[
            pltpu.VMEM((count - 1, videos, share, width), BF),
            pltpu.VMEM((videos, share, width), BF),
        ]
        + [pltpu.SemaphoreType.DMA((count - 1,))] * 4,
        compiler_params=pltpu.CompilerParams(
            collective_id=3 if last else 2, has_side_effects=True, vmem_limit_bytes=14 * MIB
        ),
        cost_estimate=pl.CostEstimate(flops=0, bytes_accessed=75 * 1000 * 1000, transcendentals=0),
        name="forward_exchange",
    )(part, rest, gain)
    return got if not last else (got[0], None)


def backward_kernel(
    count, last, part_ref, rows_ref, rest_ref, gain_ref, new_ref, sums_ref, *refs
):
    refs = list(refs)
    full_ref = None if last else refs.pop(0)
    landed_ref, own_ref, send_sem, recv_sem, send_more, recv_more = refs
    me = greet(count)
    share = rest_ref.shape[1]
    copies = start_scatter(me, count, share, part_ref, landed_ref, send_sem, recv_sem)
    mine = pl.ds(pl.multiple_of(me * share, share), share)
    rows = rows_ref[...]
    centred = rows - jnp.mean(rows, axis=-1, keepdims=True)
    scale = lax.rsqrt(jnp.mean(centred * centred, axis=-1, keepdims=True) + EPS_NORM)
    hat = centred * scale
    slope = part_ref[:, mine, :].astype(F32)
    for step, copy in enumerate(copies):
        copy.wait_recv()
        slope = slope + landed_ref[step].astype(F32)
    hat_slope = slope * gain_ref[0]
    back = hat_slope - jnp.mean(hat_slope, axis=-1, keepdims=True)
    back = back - hat * jnp.mean(hat_slope * hat, axis=-1, keepdims=True)
    new = rest_ref[...] + back * scale
    new_ref[...] = new
    if not last:
        own_ref[...] = new.astype(BF)
        more = start_gather(me, count, share, own_ref, full_ref, send_more, recv_more)
        full_ref[:, mine, :] = own_ref[...]
    sums_ref[0:1] = jnp.sum(jnp.sum(slope * hat, axis=0), axis=0, keepdims=True)
    sums_ref[1:2] = jnp.sum(jnp.sum(slope, axis=0), axis=0, keepdims=True)
    if not last:
        for copy in more:
            copy.wait()
    for copy in copies:
        copy.wait_send()


def backward_exchange(part, rows, rest, gain, count, last=False):
    videos, share, width = rest.shape
    outs = [jax.ShapeDtypeStruct(rest.shape, F32), jax.ShapeDtypeStruct((2, width), F32)]
    if not last:
        outs.append(jax.ShapeDtypeStruct(part.shape, BF))
    got = pl.pallas_call(
        functools.partial(backward_kernel, count, last),
        out_shape=tuple(outs),
        in_specs=[vmem_spec()] * 4,
        out_specs=(vmem_spec(),) * len(outs),
        scratch_shapes=[
            pltpu.VMEM((count - 1, videos, share, width), BF),
            pltpu.VMEM((videos, share, width), BF),
        ]
        + [pltpu.SemaphoreType.DMA((count - 1,))] * 4,
        compiler_params=pltpu.CompilerParams(
            collective_id=5 if last else 4, has_side_effects=True, vmem_limit_bytes=14 * MIB
        ),
        cost_estimate=pl.CostEstimate(flops=0, bytes_accessed=75 * 1000 * 1000, transcendentals=0),
        name="backward_exchange",
    )(part, rows, rest, gain)
    return got if not last else (*got, None)


def sum_kernel(heads, rows, term_ref, out_ref, plane_ref, line_ref, part_ref, *sems):
    me_head, me_row = lax.axis_index(HEADS), lax.axis_index(ROWS)
    barrier = pltpu.get_barrier_semaphore()
    for step in range(1, heads):
        pl.semaphore_signal(barrier, inc=1, device_id={HEADS: (me_head + step) % heads})
    for step in range(1, rows):
        pl.semaphore_signal(barrier, inc=1, device_id={ROWS: (me_row + step) % rows})
    pl.semaphore_wait(barrier, heads - 1 + rows - 1)

    def spread(axis, me, count, source_of, slots_ref, own, send, recv):
        copies = []
        for step in range(1, count):
            peer = (me + step) % count
            copy = pltpu.make_async_remote_copy(
                src_ref=source_of(peer),
                dst_ref=slots_ref.at[me],
                send_sem=send.at[step - 1],
                recv_sem=recv.at[step - 1],
                device_id={axis: peer},
            )
            copy.start()
            copies.append(copy)
        slots_ref[pl.ds(me, 1)] = own[None]
        for copy in copies:
            copy.wait()

    def added(slots_ref, count):
        total = slots_ref[0]
        for at in range(1, count):
            total = total + slots_ref[at]
        return total

    mine = term_ref[pl.ds(me_head, 1)][0]
    spread(HEADS, me_head, heads, lambda peer: term_ref.at[peer], plane_ref, mine, *sems[0:2])
    part_ref[0] = added(plane_ref, heads)
    spread(ROWS, me_row, rows, lambda peer: part_ref.at[0], line_ref, part_ref[0], *sems[2:4])
    part_ref[1] = added(line_ref, rows)
    spread(HEADS, me_head, heads, lambda peer: part_ref.at[1], out_ref, part_ref[1], *sems[4:6])


def sum_fast(term, heads, rows, identity):
    block = term.shape[1:]
    return pl.pallas_call(
        functools.partial(sum_kernel, heads, rows),
        out_shape=jax.ShapeDtypeStruct(term.shape, F32),
        in_specs=[vmem_spec()],
        out_specs=vmem_spec(),
        scratch_shapes=[
            pltpu.VMEM((heads, *block), F32),
            pltpu.VMEM((rows, *block), F32),
            pltpu.VMEM((2, *block), F32),
            pltpu.SemaphoreType.DMA((heads - 1,)),
            pltpu.SemaphoreType.DMA((heads - 1,)),
            pltpu.SemaphoreType.DMA((rows - 1,)),
            pltpu.SemaphoreType.DMA((rows - 1,)),
            pltpu.SemaphoreType.DMA((heads - 1,)),
            pltpu.SemaphoreType.DMA((heads - 1,)),
        ],
        compiler_params=pltpu.CompilerParams(
            collective_id=identity, has_side_effects=True, vmem_limit_bytes=8 * MIB
        ),
        cost_estimate=pl.CostEstimate(flops=0, bytes_accessed=40 * 1000 * 1000, transcendentals=0),
        name="sum_over_all",
    )(term)


def last_kernel(
    chips,
    heads,
    part_ref,
    to_x_ref,
    to_y_ref,
    slots_ref,
    final_ref,
    final_rest_ref,
    rows_ref,
    rest_ref,
    gain_ref,
    out_ref,
    from_x_ref,
    from_y_ref,
    new_ref,
    sums_ref,
    final_out_ref,
    mine_ref,
    other_ref,
    down_ref,
    up_ref,
    landed_ref,
    final_landed_ref,
    near_sem,
    slot_send,
    slot_recv,
    final_send,
    final_recv,
    down_send,
    down_recv,
    up_send,
    up_recv,
):
    head, place = lax.axis_index(HEADS), lax.axis_index(ROWS)
    z, core = place // 2, place % 2
    sibling, above, below = place + 1 - 2 * core, place + 2, place - 2
    beside_x, beside_y = head + 1 - 2 * (head % 2), (head + 2) % heads
    has_above, has_below = z < chips - 1, z > 0
    depth = out_ref.shape[0]
    pieces = down_send.shape[1]
    cut = depth // pieces

    barrier = pltpu.get_barrier_semaphore()
    for step in range(1, heads):
        pl.semaphore_signal(barrier, inc=1, device_id={HEADS: (head + step) % heads})
    pl.semaphore_signal(barrier, inc=1, device_id={ROWS: sibling})

    for step in (2, 2 * chips - 2):
        pl.semaphore_signal(barrier, inc=1, device_id={ROWS: (place + step) % (2 * chips)})
    pl.semaphore_wait(barrier, heads + 2)

    share = rest_ref.shape[1]
    slots = start_scatter(head, heads, share, slots_ref, landed_ref, slot_send, slot_recv)
    finals = start_scatter(head, heads, share, final_ref, final_landed_ref, final_send, final_recv)
    over = pltpu.make_async_remote_copy(
        src_ref=part_ref.at[:, 1 - core],
        dst_ref=other_ref,
        send_sem=near_sem.at[0],
        recv_sem=near_sem.at[1],
        device_id={ROWS: sibling},
    )
    over.start()
    keep = pltpu.make_async_copy(part_ref.at[:, core], mine_ref, near_sem.at[2])
    keep.start()
    media_x = pltpu.make_async_remote_copy(
        src_ref=to_x_ref,
        dst_ref=from_x_ref,
        send_sem=near_sem.at[3],
        recv_sem=near_sem.at[4],
        device_id={HEADS: beside_x},
    )
    media_y = pltpu.make_async_remote_copy(
        src_ref=to_y_ref,
        dst_ref=from_y_ref,
        send_sem=near_sem.at[5],
        recv_sem=near_sem.at[6],
        device_id={HEADS: beside_y},
    )
    media_x.start()
    media_y.start()
    keep.wait()
    over.wait()
    for chip in range(chips):

        def add_rows(at, carry, chip=chip):
            lines = pl.ds(pl.multiple_of(at * 16, 16), 16)
            mine_ref[chip, lines] = (
                mine_ref[chip, lines].astype(F32) + other_ref[chip, lines].astype(F32)
            ).astype(BF)
            return carry

        lax.fori_loop(0, depth // 16, add_rows, 0)

    def chain(step, piece, down):
        landed, send, recv = (down_ref, down_send, down_recv) if down else (up_ref, up_send, up_recv)
        owner = z - chips + step if down else z + chips - step
        lines = pl.ds(piece * cut, cut)
        return pltpu.make_async_remote_copy(
            src_ref=mine_ref.at[owner, lines],
            dst_ref=landed.at[step - 1, lines],
            send_sem=send.at[step - 1, piece],
            recv_sem=recv.at[step - 1, piece],
            device_id={ROWS: below if down else above},
        )

    def take(step, piece, down, owner):
        landed, recv = (down_ref, down_recv) if down else (up_ref, up_recv)
        lines = pl.ds(piece * cut, cut)
        arrival = pltpu.make_async_remote_copy(
            src_ref=mine_ref.at[z, lines],
            dst_ref=landed.at[step - 1, lines],
            send_sem=recv.at[step - 1, piece],
            recv_sem=recv.at[step - 1, piece],
            device_id={ROWS: sibling},
        )
        arrival.wait_recv()
        mine_ref[owner, lines] = (
            mine_ref[owner, lines].astype(F32) + landed[step - 1, lines].astype(F32)
        ).astype(BF)

    for step in range(1, chips):
        for piece in range(pieces):
            for down in (True, False):
                sends = (z >= chips - step) if down else (z <= step - 1)
                takes = sends & (has_above if down else has_below)
                owner = z - chips + step if down else z + chips - step

                if step > 1:

                    @pl.when(takes)
                    def _():
                        take(step - 1, piece, down, owner)

                @pl.when(sends)
                def _():
                    chain(step, piece, down).start()

    rows = rows_ref[...]
    centred = rows - jnp.mean(rows, axis=-1, keepdims=True)
    scale = lax.rsqrt(jnp.mean(centred * centred, axis=-1, keepdims=True) + EPS_NORM)
    hat = centred * scale
    own_slots = pl.ds(pl.multiple_of(head * share, share), share)
    final = final_rest_ref[...] + final_ref[:, own_slots, :].astype(F32)
    for at, copy in enumerate(finals):
        copy.wait_recv()
        final = final + final_landed_ref[at].astype(F32)
    final_out_ref[...] = final
    slope = slots_ref[:, own_slots, :].astype(F32)
    for at, copy in enumerate(slots):
        copy.wait_recv()
        slope = slope + landed_ref[at].astype(F32)
    hat_slope = slope * gain_ref[0]
    back = hat_slope - jnp.mean(hat_slope, axis=-1, keepdims=True)
    back = back - hat * jnp.mean(hat_slope * hat, axis=-1, keepdims=True)
    new_ref[...] = rest_ref[...] + back * scale
    sums_ref[0:1] = jnp.sum(jnp.sum(slope * hat, axis=0), axis=0, keepdims=True)
    sums_ref[1:2] = jnp.sum(jnp.sum(slope, axis=0), axis=0, keepdims=True)

    for piece in range(pieces):

        @pl.when(has_above)
        def _():
            take(chips - 1, piece, True, z)

        @pl.when(has_below)
        def _():
            take(chips - 1, piece, False, z)

    out_ref[...] = mine_ref[z]
    for step in range(1, chips):
        for piece in range(pieces):

            @pl.when(z >= chips - step)
            def _():
                chain(step, piece, True).wait_send()

            @pl.when(z <= step - 1)
            def _():
                chain(step, piece, False).wait_send()

    for copy in slots + finals:
        copy.wait_send()
    media_x.wait()
    media_y.wait()


def last_step(partial, to_x, to_y, slots, final, final_rest, rows, rest, gain, heads, chips):
    depth, columns = partial.shape[0] // (2 * chips), partial.shape[1]
    videos, share, width = rest.shape
    pieces = 4
    any_spec = pl.BlockSpec(memory_space=pl.ANY)
    block = pltpu.VMEM((chips, depth, columns), BF)
    steps = pltpu.VMEM((chips - 1, depth, columns), BF)
    chain_sem = pltpu.SemaphoreType.DMA((chips - 1, pieces))
    slot_sem = pltpu.SemaphoreType.DMA((heads - 1,))
    return pl.pallas_call(
        functools.partial(last_kernel, chips, heads),
        out_shape=(
            jax.ShapeDtypeStruct((depth, columns), BF),
            jax.ShapeDtypeStruct(to_x.shape, BF),
            jax.ShapeDtypeStruct(to_y.shape, BF),
            jax.ShapeDtypeStruct(rest.shape, F32),
            jax.ShapeDtypeStruct((2, width), F32),
            jax.ShapeDtypeStruct(rest.shape, F32),
        ),
        in_specs=[any_spec] * 3 + [vmem_spec()] * 6,
        out_specs=(vmem_spec(), any_spec, any_spec, vmem_spec(), vmem_spec(), vmem_spec()),
        scratch_shapes=[
            block,
            block,
            steps,
            steps,
            pltpu.VMEM((heads - 1, videos, share, width), BF),
            pltpu.VMEM((heads - 1, videos, share, width), BF),
            pltpu.SemaphoreType.DMA((7,)),
            slot_sem,
            slot_sem,
            slot_sem,
            slot_sem,
            chain_sem,
            chain_sem,
            chain_sem,
            chain_sem,
        ],
        compiler_params=pltpu.CompilerParams(
            collective_id=7, has_side_effects=True, vmem_limit_bytes=60 * MIB
        ),
        cost_estimate=pl.CostEstimate(flops=0, bytes_accessed=160 * 1000 * 1000, transcendentals=0),
        name="last_step",
    )(partial.reshape(chips, 2, depth, columns), to_x, to_y, slots, final, final_rest, rows, rest, gain)


def media_back_kernel(*refs):
    first, second, out_ref = refs[:4], refs[4:8], refs[-1]

    def write(own_ref, *terms):
        rows = own_ref[...].astype(F32)
        centred = rows - jnp.mean(rows, axis=-1, keepdims=True)
        spread = lax.rsqrt(jnp.mean(centred * centred, axis=-1, keepdims=True) + EPS_NORM)
        hat = centred * spread
        total = functools.reduce(jnp.add, [term[...].astype(F32) for term in terms])
        total = total - jnp.mean(total, axis=-1, keepdims=True) - hat * jnp.mean(total * hat, axis=-1, keepdims=True)
        total = total * spread
        for video in range(rows.shape[0]):
            out_ref[:, video, :] = total[video]

    @pl.when(pl.program_id(0) == 0)
    def _():
        write(*first)

    @pl.when(pl.program_id(0) == 1)
    def _():
        write(*second)


def media_back(first, second):
    videos, rows, width = first[0].shape
    cut = 32
    steps = rows // cut
    specs = [pl.BlockSpec((videos, cut, width), lambda i, j: (0, jnp.where(i == 0, j, steps - 1), 0))] * 4
    specs += [pl.BlockSpec((videos, cut, width), lambda i, j: (0, jnp.where(i == 1, j, 0), 0))] * 4
    return pl.pallas_call(
        media_back_kernel,
        grid=(2, steps),
        out_shape=jax.ShapeDtypeStruct((2 * rows, videos, width), F32),
        in_specs=specs,
        out_specs=pl.BlockSpec((cut, videos, width), lambda i, j: (steps * i + j, 0, 0)),
        compiler_params=pltpu.CompilerParams(vmem_limit_bytes=60 * MIB),
        cost_estimate=pl.CostEstimate(flops=0, bytes_accessed=30 * 1000 * 1000, transcendentals=0),
        name="media_back",
    )(*first, *second)


def adam_kernel(rates, begins, factor_ref, *refs):
    kinds, step = len(rates), pl.program_id(0)
    layers = (len(refs) // kinds) - 7
    factor = factor_ref[0, 0]
    ins = [refs[at * (3 + layers) : (at + 1) * (3 + layers)] for at in range(kinds)]
    outs = [refs[kinds * (3 + layers) + 4 * at :][:4] for at in range(kinds)]
    for kind in range(kinds):
        steps = (begins[kind + 1] - begins[kind]) // layers
        weight_ref, first_ref, second_ref = ins[kind][:3]
        mean_ref, square_ref, next_ref, copy_ref = outs[kind]
        columns = weight_ref.shape[3]
        for layer in range(layers):
            begin = begins[kind] + layer * steps

            @pl.when((step >= begin) & (step < begin + steps))
            def _():
                for part in range(weight_ref.shape[1]):
                    grad = ins[kind][3 + layer][:, part * columns : (part + 1) * columns]
                    mean, square, weight = adam_step(
                        weight_ref[0, part],
                        first_ref[0, part],
                        second_ref[0, part],
                        grad.astype(F32) * factor,
                        rates[kind],
                        WEIGHT_DECAY,
                    )
                    mean_ref[0, part] = mean
                    square_ref[0, part] = square
                    next_ref[0, part] = weight
                    copy_ref[0, part] = weight.astype(BF)


def adam_fast(kinds, factor):
    layers = kinds[0][0].shape[0]
    begins = [0]
    for weight, _, _, _, cut, _ in kinds:
        begins.append(begins[-1] + layers * (weight.shape[2] // cut))
    operands, in_specs, out_specs, out_shape = [], [], [], []
    for kind, (weight, first, second, grads, cut, _) in enumerate(kinds):
        _, parts, rows, columns = weight.shape
        steps = rows // cut
        begin, end = begins[kind], begins[kind + 1]

        def place(i, begin=begin, end=end, steps=steps):
            at = jnp.clip(i, begin, end - 1) - begin
            return (at // steps, 0, at % steps, 0)

        spec = pl.BlockSpec((1, parts, cut, columns), place)
        operands += [weight, first, second]
        in_specs += [spec] * 3
        for layer, (grad, base) in enumerate(grads):

            def grad_place(i, begin=begin + layer * steps, steps=steps, base=base):
                return (jnp.clip(i, begin, begin + steps - 1) - begin, base)

            operands.append(grad)
            in_specs.append(pl.BlockSpec((cut, parts * columns), grad_place))
        wide = jax.ShapeDtypeStruct(weight.shape, F32)
        out_specs += [spec] * 4
        out_shape += [wide, wide, wide, jax.ShapeDtypeStruct(weight.shape, BF)]
    size = sum(kind[0].size for kind in kinds)
    made = pl.pallas_call(
        functools.partial(adam_kernel, [kind[-1] for kind in kinds], begins),
        grid=(begins[-1],),
        out_shape=tuple(out_shape),
        in_specs=[pl.BlockSpec(memory_space=pltpu.SMEM)] + in_specs,
        out_specs=tuple(out_specs),
        compiler_params=pltpu.CompilerParams(vmem_limit_bytes=60 * MIB),
        cost_estimate=pl.CostEstimate(flops=20 * size, bytes_accessed=28 * size, transcendentals=size),
        name="adam",
    )(factor, *operands)
    return [made[4 * at : 4 * at + 4] for at in range(len(kinds))]


def flat(rows):
    return rows.reshape(-1, rows.shape[-1])


def local_fast(
    media,
    latents,
    frame_count,
    cotangent,
    inward,
    inward_first,
    inward_second,
    outward,
    outward_first,
    outward_second,
    widen,
    widen_first,
    widen_second,
    narrow,
    narrow_first,
    narrow_second,
    norm_gains,
    gain_first,
    gain_second,
):
    heads_count, rows_count = lax.axis_size(HEADS), lax.axis_size(ROWS)
    me = lax.axis_index(HEADS)
    layers, _, row_share, head_columns = inward.shape
    local_positions, videos, width = media.shape
    latent_count = latents.shape[1] * heads_count
    scale = HD ** (-0.5)

    def swap_x(rows):
        return lax.ppermute(rows, HEADS, X_SWAP)

    def swap_y(rows):
        return lax.ppermute(rows, HEADS, Y_SWAP)

    def gather_rows(rows):
        return lax.all_gather(rows, ROWS, axis=0, tiled=True)

    outward_t, narrow_t = (jnp.swapaxes(outward, 1, 2), jnp.swapaxes(narrow, 1, 2))
    columns, units = head_columns, widen.shape[2]
    first_set = [inward[l, t] for l in range(layers) for t in (1, 2)]
    first_set = first_set + [inward[l, 0] for l in range(layers)] + [outward_t[l] for l in range(layers)]
    first_set = jnp.concatenate([piece.astype(BF) for piece in first_set], axis=1)

    latent = latents
    normed = layer_norm(latent, norm_gains[0, 2], norm_gains[0, 3]).astype(BF)
    slope_rows = cotangent.astype(BF)
    first_set = gather_rows(first_set)
    pair_weights = first_set[:, : 2 * layers * columns]
    begin = 2 * layers * columns
    query_full = [first_set[:, begin + l * columns : begin + (l + 1) * columns] for l in range(layers)]
    begin = begin + layers * columns
    out_full = [first_set[:, begin + l * columns : begin + (l + 1) * columns] for l in range(layers)]
    share = latents.shape[1]
    own = jnp.swapaxes(media.reshape(2, local_positions // 2, videos, width), 1, 2)
    later_sets = [
        jnp.concatenate((widen[layer].astype(BF), narrow_t[layer].astype(BF)), axis=1) for layer in range(layers)
    ]
    own, *later_sets = lax.optimization_barrier((own, *later_sets))
    later_sets = [gather_rows(rows) for rows in later_sets]
    widen_full = [rows[:, :units] for rows in later_sets]
    narrow_full = [rows[:, units:] for rows in later_sets]

    frames = jnp.stack([2 * (me ^ group) + half for group in range(4) for half in range(2)])
    live = (frames[None, :] < frame_count[:, None]).astype(jnp.int32)
    media_gains = norm_gains[:, 0:2]
    near, latent_norm = gather_near(own, normed, heads_count)
    keys, media_hat, far = media_near(own, near, media_gains, first_set, 2 * layers * columns, heads_count)
    keys, media_hat, feed_slope = media_far(far, media_gains, first_set, slope_rows, keys, media_hat, heads_count)
    kept = []
    for layer in range(layers):
        query_weight, out_weight = query_full[layer], out_full[layer]
        pair_weight = pair_weights[:, 2 * layer * head_columns : 2 * (layer + 1) * head_columns]
        query = mm(flat(latent_norm), query_weight)
        latent_pair = mm(flat(latent_norm), pair_weight)
        mixed = attend_fast(live, query, latent_pair, keys, layer, scale)
        part = mm(mixed, out_weight, NT).reshape(videos, latent_count, width)
        middle, feed_norm = forward_exchange(part, latent, norm_gains[layer, 4:6], heads_count)
        hidden_pre = mm(flat(feed_norm), widen_full[layer], None, F32)
        hidden = jax.nn.gelu(hidden_pre).astype(BF)
        part = mm(hidden, narrow_full[layer], NT).reshape(videos, latent_count, width)
        last = layer == layers - 1
        gain = norm_gains[0 if last else layer + 1, 2:4]
        kept.append((latent, middle, latent_norm, query, latent_pair, mixed, feed_norm, hidden_pre, hidden))
        if last:
            final_part, final_rest = part, middle
        else:
            latent, latent_norm = forward_exchange(part, middle, gain, heads_count)

    slope = cotangent
    gain_parts = [None] * layers
    shares, waiting = [], []
    media_slopes = ()

    scaled = jnp.concatenate(
        [
            (
                pair_weights[:, 2 * l * head_columns : 2 * (l + 1) * head_columns].astype(F32)
                * norm_gains[l, 0][:, None]
            ).astype(BF)
            for l in range(layers)
        ],
        axis=1,
    )

    def hat_slope(slopes, group, half):
        return mm(flat(slopes[2 * group + half]), scaled, NT).reshape(videos, -1, width)

    summed = []

    def scatter_rows(gradient):
        if summed:
            gradient, _ = lax.optimization_barrier((gradient, summed[-1]))
        summed.append(lax.psum_scatter(gradient, ROWS, scatter_dimension=0, tiled=True))
        return summed[-1]

    for layer in reversed(range(layers)):
        latent_in, middle, latent_norm, query, latent_pair, mixed, feed_norm, hidden_pre, hidden = kept[layer]
        query_weight, out_weight = query_full[layer], out_full[layer]
        pair_weight = pair_weights[:, 2 * layer * head_columns : 2 * (layer + 1) * head_columns]
        feed_slope = flat(feed_slope)
        hidden_slope = mm(feed_slope, narrow_full[layer], None, F32)
        _, gelu_back = jax.vjp(jax.nn.gelu, hidden_pre)
        pre_slope = gelu_back(hidden_slope)[0].astype(BF)
        part = mm(pre_slope, widen_full[layer], NT).reshape(videos, latent_count, width)
        feed_grad = product_pair(feed_slope, hidden, flat(feed_norm), pre_slope, *waiting)
        part, feed_grad = lax.optimization_barrier((part, feed_grad))
        shares.append(scatter_rows(feed_grad))
        middle_slope, feed_sums, branch_slope = backward_exchange(
            part, middle, slope, norm_gains[layer, 4:6], heads_count
        )
        branch_slope = flat(branch_slope)
        mixed_slope = mm(branch_slope, out_weight)
        out_grad = mm(branch_slope, mixed, TN)
        query_slope, latent_slopes, media_slopes = attend_back_fast(
            live, query, latent_pair, keys, mixed_slope, layer, scale, (media_slopes,) if layer < layers - 1 else ()
        )
        part = (mm(query_slope, query_weight, NT, F32) + mm(latent_slopes, pair_weight, NT, F32)).astype(BF)
        part = part.reshape(videos, latent_count, width)
        last = layer == 0
        if not last:
            slope, latent_sums, feed_slope = backward_exchange(
                part, latent_in, middle_slope, norm_gains[layer, 2:4], heads_count
            )
        else:
            last_part = part
            far = [hat_slope(media_slopes, 3, half) for half in range(2)]
            media_slopes, *far = lax.optimization_barrier((media_slopes, *far))
            over_x, over_y = swap_x(far[0]), swap_y(far[1])
            near = [hat_slope(media_slopes, 1, 0), hat_slope(media_slopes, 2, 1)]
            media_slopes, *near = lax.optimization_barrier((media_slopes, *near))
            in_x, in_y = [swap_x(near[0]), None], [None, swap_y(near[1])]
            near = [hat_slope(media_slopes, 1, 1), hat_slope(media_slopes, 2, 0)]
            media_slopes, *near = lax.optimization_barrier((media_slopes, *near))
        query_grad = mm(flat(latent_norm), query_slope, TN)
        pair_slope = flat(media_slopes[..., 2 * layer * head_columns : 2 * (layer + 1) * head_columns])
        hat_grad = mm(flat(media_hat), pair_slope, TN, F32)
        slope_sum = jnp.sum(pair_slope.astype(F32), axis=0)
        gain, shift = norm_gains[layer, 0], norm_gains[layer, 1]
        pair_grad = (
            mm(flat(latent_norm), latent_slopes, TN, F32)
            + gain[:, None] * hat_grad
            + shift[:, None] * slope_sum[None, :]
        ).astype(BF)
        wide = pair_weight.astype(F32)
        media_sums = jnp.stack(
            (jnp.sum(wide * hat_grad, axis=1), jnp.sum(wide * slope_sum[None, :], axis=1))
        )
        inward_grad = jnp.concatenate((query_grad, pair_grad, out_grad), axis=1)
        if last:
            near = [near[0] + over_y, near[1] + over_x]
            last_grad, *near = lax.optimization_barrier((inward_grad, *near))
        else:
            waiting = [inward_grad]
        gain_parts[layer] = [media_sums, None if last else latent_sums, feed_sums]

    back = [hat_slope(media_slopes, 0, half) for half in range(2)]
    last_grad, *back = lax.optimization_barrier((last_grad, *back))
    share_out, in_x[1], in_y[0], slope, gain_parts[0][1], latent = last_step(
        last_grad, *near, last_part, final_part, final_rest, latents, middle_slope, norm_gains[0, 2:4], heads_count, rows_count // 2
    )
    media_slope = media_back(*[(own[half], back[half], in_x[half], in_y[half]) for half in range(2)])

    def square_sum(rows):
        wide = rows.astype(F32)
        return jnp.sum(wide * wide)

    shares.append(share_out)
    early = sum(square_sum(piece) for piece in shares[:-1])
    gain_term = jnp.concatenate([rows for parts in gain_parts for rows in parts], axis=0).reshape(heads_count, -1, 128)
    lines = gain_term.shape[1]
    squares = jnp.full((heads_count, 8 - lines % 8, 128), early + square_sum(shares[-1]), F32)
    totals = sum_fast(jnp.concatenate((gain_term, squares), axis=1), heads_count, rows_count, 9)
    gain_total = totals[:, :lines].reshape(layers, 6, width)
    square_total = totals[0, lines, 0]
    gain_total = totals[:, :lines].reshape(layers, 6, width)
    square_total = totals[0, lines, 0]
    gain_total = totals[:, :lines].reshape(layers, 6, width)
    square_total = totals[0, lines, 0]
    gain_total = totals[:, :lines].reshape(layers, 6, width)
    square_total = totals[0, lines, 0]
    feed_parts = [piece[:, : 2 * units] for piece in shares[-2::-1]]
    inward_parts = [shares[-1]] + [piece[:, 2 * units :] for piece in shares[-2:0:-1]]
    gradient_norm = jnp.sqrt(square_total + jnp.sum(gain_total * gain_total))
    factor = CLIP_LEVEL / jnp.maximum(gradient_norm, CLIP_LEVEL)

    factor_cell = factor.reshape(1, 1)
    early_share, middle_share, late_share = shares
    depth = widen.shape[1]

    def turned(*arrays):
        return [jnp.swapaxes(rows, 1, 2)[:, None] for rows in arrays]

    def turn_back(arrays):
        return [jnp.swapaxes(rows[:, 0], 1, 2) for rows in arrays]

    inward_made, outward_made, widen_made, narrow_made = adam_fast(
        (
            (
                *(inward, inward_first, inward_second),
                [(late_share, 0), (middle_share, 0)],
                *(depth // 2, RATE_INWARD),
            ),
            (
                *turned(outward, outward_first, outward_second),
                [(late_share, 3), (middle_share, 3)],
                *(depth, RATE_OUTWARD),
            ),
            (
                *[rows[:, None] for rows in (widen, widen_first, widen_second)],
                [(middle_share, 1 + 4 * columns // units), (early_share, 1)],
                *(depth // 2, RATE_WIDEN),
            ),
            (
                *turned(narrow, narrow_first, narrow_second),
                [(middle_share, 4 * columns // units), (early_share, 0)],
                *(depth // 2, RATE_NARROW),
            ),
        ),
        factor_cell,
    )
    results = [latent, slope, media_slope, gradient_norm, *inward_made, *turn_back(outward_made)]
    results += [rows[:, 0] for rows in widen_made] + turn_back(narrow_made)
    mean_new, square_new, weight_new = adam_step(
        norm_gains, gain_first, gain_second, gain_total * factor, RATE_GAINS, 0.0
    )
    results = results + [mean_new, square_new, weight_new, gain_total[:, 4:6]]
    return tuple(results)


def solution(mesh):
    placed = (
        P(HEADS, ROWS, None),
        P(ROWS, HEADS, None),
        P(ROWS),
        P(ROWS, HEADS, None),
        P(None, None, ROWS, HEADS),
        P(None, None, ROWS, HEADS),
        P(None, None, ROWS, HEADS),
        P(None, HEADS, ROWS),
        P(None, HEADS, ROWS),
        P(None, HEADS, ROWS),
        P(None, ROWS, HEADS),
        P(None, ROWS, HEADS),
        P(None, ROWS, HEADS),
        P(None, HEADS, ROWS),
        P(None, HEADS, ROWS),
        P(None, HEADS, ROWS),
        P(),
        P(),
        P(),
    )
    local = local_fast if (mesh.shape[ROWS], mesh.shape[HEADS]) == (8, 4) else local_plain
    return jax.shard_map(
        local,
        mesh=mesh,
        in_specs=placed,
        out_specs=(
            P(ROWS, HEADS, None),
            P(ROWS, HEADS, None),
            P(HEADS, ROWS, None),
            P(),
            P(None, None, ROWS, HEADS),
            P(None, None, ROWS, HEADS),
            P(None, None, ROWS, HEADS),
            P(None, None, ROWS, HEADS),
            P(None, HEADS, ROWS),
            P(None, HEADS, ROWS),
            P(None, HEADS, ROWS),
            P(None, HEADS, ROWS),
            P(None, ROWS, HEADS),
            P(None, ROWS, HEADS),
            P(None, ROWS, HEADS),
            P(None, ROWS, HEADS),
            P(None, HEADS, ROWS),
            P(None, HEADS, ROWS),
            P(None, HEADS, ROWS),
            P(None, HEADS, ROWS),
            P(),
            P(),
            P(),
            P(),
        ),
        check_vma=False,
    )
```

```python
import functools

import jax
import jax.numpy as jnp
from jax import lax
from jax.experimental import pallas as pl
from jax.experimental.pallas import tpu as pltpu
from jax.sharding import PartitionSpec as P

HD = 96
STEP = 10
PATCHES = 128


EPS_NORM = 1e-05
BETA_ONE = 0.5
BETA_TWO = 0.5
ADAM_EPS = 1e-08
WEIGHT_DECAY = 0.1
CLIP_LEVEL = 1.0
MASKED_SCORE = -1e30
RATE_INWARD = 0.02
RATE_OUTWARD = 0.5
RATE_WIDEN = 0.02
RATE_NARROW = 0.01
RATE_GAINS = 0.1


def layer_norm(rows, gain, shift):
    middle = jnp.mean(rows, axis=-1, keepdims=True)
    centred = rows - middle
    spread = jnp.mean(centred * centred, axis=-1, keepdims=True)
    return centred * lax.rsqrt(spread + EPS_NORM) * gain + shift


def norm_back(rows, gain, shift, slope):
    _, pullback = jax.vjp(layer_norm, rows, gain, shift)
    return pullback(slope)


def adam_step(weight, first, second, gradient, rate, decay):
    mean_new = BETA_ONE * first + (1.0 - BETA_ONE) * gradient
    square_new = BETA_TWO * second + (1.0 - BETA_TWO) * gradient * gradient
    mean_hat = mean_new / (1.0 - BETA_ONE**STEP)
    square_hat = square_new / (1.0 - BETA_TWO**STEP)
    weight_new = weight - rate * (mean_hat / (jnp.sqrt(square_hat) + ADAM_EPS) + decay * weight)
    return (mean_new, square_new, weight_new)


def gather_slots(rows):
    return lax.all_gather(rows, HEADS, axis=1, tiled=True)


def scatter_slots(terms):
    return lax.psum_scatter(terms, HEADS, scatter_dimension=1, tiled=True)


def gather_slopes(rows):
    return lax.all_gather(rows, HEADS, axis=1, tiled=True)


def scatter_slopes(terms):
    return lax.psum_scatter(terms, HEADS, scatter_dimension=1, tiled=True)


def both_scores(query, media_pair, latent_pair, live, scale):
    score_media = (
        jnp.einsum("vnhe,pvhe->vhnp", query, media_pair[0], preferred_element_type=jnp.float32)
        * scale
    )
    score_media = jnp.where(live[:, None, None, :], score_media, MASKED_SCORE)
    score_latent = (
        jnp.einsum("vnhe,vmhe->vhnm", query, latent_pair[0], preferred_element_type=jnp.float32)
        * scale
    )
    return (score_media, score_latent)


def attend(query, media_pair, latent_pair, live, scale):
    score_media, score_latent = both_scores(query, media_pair, latent_pair, live, scale)
    top = jnp.maximum(
        jnp.max(score_media, axis=-1, keepdims=True), jnp.max(score_latent, axis=-1, keepdims=True)
    )
    exponent_media = jnp.exp(score_media - top)
    exponent_latent = jnp.exp(score_latent - top)
    total = jnp.sum(exponent_media, axis=-1, keepdims=True) + jnp.sum(
        exponent_latent, axis=-1, keepdims=True
    )
    share_media = (exponent_media / total).astype(jnp.bfloat16)
    share_latent = (exponent_latent / total).astype(jnp.bfloat16)
    mixed = jnp.einsum(
        "vhnp,pvhe->vnhe", share_media, media_pair[1], preferred_element_type=jnp.float32
    )
    mixed = mixed + jnp.einsum(
        "vhnm,vmhe->vnhe", share_latent, latent_pair[1], preferred_element_type=jnp.float32
    )
    return (mixed.astype(jnp.bfloat16), top + jnp.log(total))


def attend_back(query, media_pair, latent_pair, live, log_total, mixed_slope, scale):
    score_media, score_latent = both_scores(query, media_pair, latent_pair, live, scale)
    share_media = jnp.exp(score_media - log_total)
    share_latent = jnp.exp(score_latent - log_total)
    share_slope_media = jnp.einsum(
        "vnhe,pvhe->vhnp", mixed_slope, media_pair[1], preferred_element_type=jnp.float32
    )
    share_slope_latent = jnp.einsum(
        "vnhe,vmhe->vhnm", mixed_slope, latent_pair[1], preferred_element_type=jnp.float32
    )
    row_total = jnp.sum(share_media * share_slope_media, axis=-1, keepdims=True)
    row_total = row_total + jnp.sum(share_latent * share_slope_latent, axis=-1, keepdims=True)
    score_slope_media = (share_media * (share_slope_media - row_total)).astype(jnp.bfloat16)
    score_slope_latent = (share_latent * (share_slope_latent - row_total)).astype(jnp.bfloat16)
    query_slope = jnp.einsum(
        "vhnp,pvhe->vnhe", score_slope_media, media_pair[0], preferred_element_type=jnp.float32
    )
    query_slope = query_slope + jnp.einsum(
        "vhnm,vmhe->vnhe", score_slope_latent, latent_pair[0], preferred_element_type=jnp.float32
    )
    query_slope = (query_slope * scale).astype(jnp.bfloat16)
    key_media = (
        jnp.einsum("vhnp,vnhe->pvhe", score_slope_media, query, preferred_element_type=jnp.float32)
        * scale
    ).astype(jnp.bfloat16)
    value_media = jnp.einsum(
        "vhnp,vnhe->pvhe",
        share_media.astype(jnp.bfloat16),
        mixed_slope,
        preferred_element_type=jnp.float32,
    ).astype(jnp.bfloat16)
    key_latent = (
        jnp.einsum("vhnm,vnhe->vmhe", score_slope_latent, query, preferred_element_type=jnp.float32)
        * scale
    ).astype(jnp.bfloat16)
    value_latent = jnp.einsum(
        "vhnm,vnhe->vmhe",
        share_latent.astype(jnp.bfloat16),
        mixed_slope,
        preferred_element_type=jnp.float32,
    ).astype(jnp.bfloat16)
    return (query_slope, jnp.stack((key_media, value_media)), jnp.stack((key_latent, value_latent)))


def local_plain(
    media,
    latents,
    frame_count,
    cotangent,
    inward,
    inward_first,
    inward_second,
    outward,
    outward_first,
    outward_second,
    widen,
    widen_first,
    widen_second,
    narrow,
    narrow_first,
    narrow_second,
    norm_gains,
    gain_first,
    gain_second,
):
    heads_count = lax.axis_size(HEADS)
    layers, _, row_share, head_columns = inward.shape
    local_positions, videos, width = media.shape
    positions = local_positions * heads_count
    latent_count = latents.shape[1] * heads_count
    local_heads = head_columns // HD
    scale = HD ** (-0.5)
    live = (jnp.arange(positions, dtype=jnp.int32) // PATCHES)[None, :] < frame_count[:, None]
    inward_columns, outward_rows, widen_columns, narrow_rows = (
        lax.all_gather(inward.astype(jnp.bfloat16), ROWS, axis=2, tiled=True),
        lax.all_gather(outward.astype(jnp.bfloat16), ROWS, axis=2, tiled=True),
        lax.all_gather(widen.astype(jnp.bfloat16), ROWS, axis=1, tiled=True),
        lax.all_gather(narrow.astype(jnp.bfloat16), ROWS, axis=2, tiled=True),
    )
    media_rows = media.astype(jnp.float32)
    latent = latents
    kept = []
    for layer in range(layers):
        gains = norm_gains[layer]
        media_norm = layer_norm(media_rows, gains[0], gains[1]).astype(jnp.bfloat16)
        latent_norm = gather_slots(layer_norm(latent, gains[2], gains[3]).astype(jnp.bfloat16))
        triple = jnp.einsum(
            "vnd,tdc->tvnc", latent_norm, inward_columns[layer], preferred_element_type=jnp.float32
        ).astype(jnp.bfloat16)
        pair_columns = inward_columns[layer, 1:3]
        media_pair = jnp.einsum(
            "pvd,tdc->tpvc",
            lax.all_gather(media_norm, HEADS, axis=0, tiled=True),
            pair_columns,
            preferred_element_type=jnp.float32,
        ).astype(jnp.bfloat16)
        query = triple[0].reshape(videos, latent_count, local_heads, HD)
        latent_pair = triple[1:3].reshape(2, videos, latent_count, local_heads, HD)
        heads_pair = media_pair.reshape(2, positions, videos, local_heads, HD)
        mixed, log_total = attend(query, heads_pair, latent_pair, live, scale)
        mixed = mixed.reshape(videos, latent_count, head_columns)
        middle = latent + scatter_slots(
            jnp.einsum(
                "vnc,cd->vnd", mixed, outward_rows[layer], preferred_element_type=jnp.float32
            )
        )
        feed_norm = gather_slots(layer_norm(middle, gains[4], gains[5]).astype(jnp.bfloat16))
        hidden_pre = jnp.einsum(
            "vnd,df->vnf", feed_norm, widen_columns[layer], preferred_element_type=jnp.float32
        )
        hidden = jax.nn.gelu(hidden_pre).astype(jnp.bfloat16)
        kept.append(
            (
                latent,
                middle,
                media_norm,
                latent_norm,
                query,
                heads_pair,
                latent_pair,
                mixed,
                log_total,
                feed_norm,
                hidden_pre,
                hidden,
            )
        )
        latent = middle + scatter_slots(
            jnp.einsum(
                "vnf,fd->vnd", hidden, narrow_rows[layer], preferred_element_type=jnp.float32
            )
        )
    slope = cotangent
    media_slope = jnp.zeros(media_rows.shape, jnp.float32)
    inward_parts, outward_parts, widen_parts, narrow_parts, gain_parts = ([], [], [], [], [])
    for layer in reversed(range(layers)):
        (
            latent_in,
            middle,
            media_norm,
            latent_norm,
            query,
            heads_pair,
            latent_pair,
            mixed,
            log_total,
            feed_norm,
            hidden_pre,
            hidden,
        ) = kept[layer]
        gains = norm_gains[layer]
        feed_slope = gather_slopes(slope.astype(jnp.bfloat16))
        narrow_grad = jnp.einsum(
            "vnf,vnd->fd", hidden, feed_slope, preferred_element_type=jnp.float32
        )
        hidden_slope = jnp.einsum(
            "vnd,fd->vnf", feed_slope, narrow_rows[layer], preferred_element_type=jnp.float32
        )
        _, gelu_back = jax.vjp(jax.nn.gelu, hidden_pre)
        pre_slope = gelu_back(hidden_slope)[0].astype(jnp.bfloat16)
        widen_grad = jnp.einsum(
            "vnd,vnf->df", feed_norm, pre_slope, preferred_element_type=jnp.float32
        )
        norm_slope = scatter_slopes(
            jnp.einsum(
                "vnf,df->vnd", pre_slope, widen_columns[layer], preferred_element_type=jnp.float32
            )
        )
        middle_part, gain_feed, shift_feed = norm_back(middle, gains[4], gains[5], norm_slope)
        middle_slope = slope + middle_part
        branch_slope = gather_slopes(middle_slope.astype(jnp.bfloat16))
        outward_grad = jnp.einsum(
            "vnc,vnd->cd", mixed, branch_slope, preferred_element_type=jnp.float32
        )
        mixed_slope = jnp.einsum(
            "vnd,cd->vnc", branch_slope, outward_rows[layer], preferred_element_type=jnp.float32
        ).astype(jnp.bfloat16)
        mixed_slope = mixed_slope.reshape(videos, latent_count, local_heads, HD)
        query_slope, media_slopes, latent_slopes = attend_back(
            query, heads_pair, latent_pair, live, log_total, mixed_slope, scale
        )
        triple_slope = jnp.concatenate(
            (
                query_slope.reshape(1, videos, latent_count, head_columns),
                latent_slopes.reshape(2, videos, latent_count, head_columns),
            ),
            axis=0,
        )
        inward_grad = jnp.einsum(
            "vnd,tvnc->tdc", latent_norm, triple_slope, preferred_element_type=jnp.float32
        )
        norm_slope = scatter_slopes(
            jnp.einsum(
                "tvnc,tdc->vnd",
                triple_slope,
                inward_columns[layer],
                preferred_element_type=jnp.float32,
            )
        )
        latent_part, gain_latent, shift_latent = norm_back(
            latent_in, gains[2], gains[3], norm_slope
        )
        slope = middle_slope + latent_part
        pair_slope = media_slopes.reshape(2, positions, videos, head_columns)
        media_columns = jnp.einsum(
            "pvd,tpvc->tdc",
            lax.all_gather(media_norm, HEADS, axis=0, tiled=True),
            pair_slope,
            preferred_element_type=jnp.float32,
        )
        inward_grad = jnp.concatenate((inward_grad[:1], inward_grad[1:] + media_columns), axis=0)
        pair_columns = inward_columns[layer, 1:3]
        media_norm_slope = lax.psum_scatter(
            jnp.einsum(
                "tpvc,tdc->pvd", pair_slope, pair_columns, preferred_element_type=jnp.float32
            ),
            HEADS,
            scatter_dimension=0,
            tiled=True,
        )
        media_part, gain_media, shift_media = norm_back(
            media_rows, gains[0], gains[1], media_norm_slope
        )
        media_slope = media_slope + media_part
        inward_parts.append(inward_grad)
        outward_parts.append(outward_grad)
        widen_parts.append(widen_grad)
        narrow_parts.append(narrow_grad)
        gain_parts.append(
            jnp.stack((gain_media, shift_media, gain_latent, shift_latent, gain_feed, shift_feed))
        )
    inward_grad, outward_grad, widen_grad, narrow_grad = (
        lax.psum_scatter(jnp.stack(inward_parts[::-1]), ROWS, scatter_dimension=2, tiled=True),
        lax.psum_scatter(jnp.stack(outward_parts[::-1]), ROWS, scatter_dimension=2, tiled=True),
        lax.psum_scatter(jnp.stack(widen_parts[::-1]), ROWS, scatter_dimension=1, tiled=True),
        lax.psum_scatter(jnp.stack(narrow_parts[::-1]), ROWS, scatter_dimension=2, tiled=True),
    )
    squares = jnp.sum(inward_grad * inward_grad) + jnp.sum(outward_grad * outward_grad)
    squares = squares + jnp.sum(widen_grad * widen_grad) + jnp.sum(narrow_grad * narrow_grad)
    gain_total, square_total = lax.psum((jnp.stack(gain_parts[::-1]), squares), (ROWS, HEADS))
    gradient_norm = jnp.sqrt(square_total + jnp.sum(gain_total * gain_total))
    factor = CLIP_LEVEL / jnp.maximum(gradient_norm, CLIP_LEVEL)
    table = (
        (inward, inward_first, inward_second, inward_grad, RATE_INWARD, WEIGHT_DECAY),
        (outward, outward_first, outward_second, outward_grad, RATE_OUTWARD, WEIGHT_DECAY),
        (widen, widen_first, widen_second, widen_grad, RATE_WIDEN, WEIGHT_DECAY),
        (narrow, narrow_first, narrow_second, narrow_grad, RATE_NARROW, WEIGHT_DECAY),
    )
    results = [latent, slope, media_slope, gradient_norm]
    for weight, first, second, gradient, rate, decay in table:
        mean_new, square_new, weight_new = adam_step(
            weight, first, second, gradient * factor, rate, decay
        )
        results = results + [mean_new, square_new, weight_new, weight_new.astype(jnp.bfloat16)]
    mean_new, square_new, weight_new = adam_step(
        norm_gains, gain_first, gain_second, gain_total * factor, RATE_GAINS, 0.0
    )
    results = results + [mean_new, square_new, weight_new, gain_total[:, 4:6]]
    return tuple(results)


BF = jnp.bfloat16
F32 = jnp.float32
MIB = 1024 * 1024
HEADS, ROWS = "heads", "rows"
NT = (((1,), (1,)), ((), ()))
TN = (((0,), (0,)), ((), ()))
X_SWAP = ((0, 1), (1, 0), (2, 3), (3, 2))
Y_SWAP = ((0, 2), (2, 0), (1, 3), (3, 1))
FAR_SWAP = ((0, 3), (3, 0), (1, 2), (2, 1))


def vmem_spec():
    return pl.BlockSpec(memory_space=pltpu.VMEM)


def mm(left, right, dims=None, out=BF):
    dims = dims or (((1,), (0,)), ((), ()))
    return lax.dot_general(left, right, dims, preferred_element_type=F32).astype(out)


def greet(count):
    me = lax.axis_index(HEADS)
    barrier = pltpu.get_barrier_semaphore()
    for step in range(1, count):
        pl.semaphore_signal(barrier, inc=1, device_id={HEADS: (me + step) % count})
    pl.semaphore_wait(barrier, count - 1)
    return me


def own_rows(ref, place, share):
    return ref.at[:, pl.ds(pl.multiple_of(place * share, share), share), :]


def start_gather(me, count, share, own_ref, full_ref, send_sem, recv_sem):
    copies = []
    for step in range(1, count):
        copy = pltpu.make_async_remote_copy(
            src_ref=own_ref,
            dst_ref=own_rows(full_ref, me, share),
            send_sem=send_sem.at[step - 1],
            recv_sem=recv_sem.at[step - 1],
            device_id={HEADS: (me + step) % count},
        )
        copy.start()
        copies.append(copy)
    return copies


def beside(me):
    return me + 1 - 2 * (me % 2), me + 2 - 4 * (me // 2)


def gather_kernel(count, own_ref, norm_ref, near_ref, full_ref, send_sem, recv_sem, norm_send, norm_recv):
    me = greet(count)
    beside_x, beside_y = beside(me)
    share = norm_ref.shape[1]
    copies = start_gather(me, count, share, norm_ref, full_ref, norm_send, norm_recv)
    for at, (half, slot, peer) in enumerate(
        ((1, 1, beside_x), (0, 2, beside_y), (0, 0, beside_x), (1, 3, beside_y))
    ):
        copy = pltpu.make_async_remote_copy(
            src_ref=own_ref.at[half],
            dst_ref=near_ref.at[slot],
            send_sem=send_sem.at[at],
            recv_sem=recv_sem.at[at],
            device_id={HEADS: peer},
        )
        copy.start()
        copies.append(copy)
    full_ref[:, pl.ds(pl.multiple_of(me * share, share), share), :] = norm_ref[...]
    for copy in copies:
        copy.wait()


def gather_near(own, norm, count):
    videos, share, width = norm.shape
    any_spec = pl.BlockSpec(memory_space=pl.ANY)
    return pl.pallas_call(
        functools.partial(gather_kernel, count),
        out_shape=(
            jax.ShapeDtypeStruct((4, *own.shape[1:]), BF),
            jax.ShapeDtypeStruct((videos, share * count, width), BF),
        ),
        in_specs=[any_spec, vmem_spec()],
        out_specs=(any_spec, vmem_spec()),
        scratch_shapes=[pltpu.SemaphoreType.DMA((4,))] * 2 + [pltpu.SemaphoreType.DMA((count - 1,))] * 2,
        compiler_params=pltpu.CompilerParams(
            collective_id=1, has_side_effects=True, vmem_limit_bytes=60 * MIB
        ),
        cost_estimate=pl.CostEstimate(flops=0, bytes_accessed=250 * 1000 * 1000, transcendentals=0),
        name="gather_near",
    )(own, norm)


def media_rows(half, layer, chunk_ref, gain_ref, weight_ref, keys_ref, hat_ref, rows_ref, other_ref=None):
    @pl.when(layer == 0)
    def _():
        if other_ref is None:
            rows_ref[...] = chunk_ref[0].astype(F32).reshape(rows_ref.shape)
        else:

            @pl.when(half < 2)
            def _():
                rows_ref[...] = chunk_ref[0].astype(F32).reshape(rows_ref.shape)

            @pl.when(half >= 2)
            def _():
                rows_ref[...] = other_ref[0].astype(F32).reshape(rows_ref.shape)

        rows = rows_ref[...]
        centred = rows - jnp.mean(rows, axis=-1, keepdims=True)
        spread = jnp.mean(centred * centred, axis=-1, keepdims=True)
        hat = centred * lax.rsqrt(spread + EPS_NORM)
        rows_ref[...] = hat
        hat_ref[...] = hat.astype(BF).reshape(hat_ref.shape)

    gain = gain_ref[pl.ds(layer, 1), 0]
    shift = gain_ref[pl.ds(layer, 1), 1]
    normed = (rows_ref[...] * gain + shift).astype(BF)
    keys_ref[...] = jnp.dot(normed, weight_ref[...], preferred_element_type=F32).astype(BF).reshape(keys_ref.shape)


def near_kernel(
    count, own_ref, near_ref, gain_ref, weight_ref, source_ref, keys_ref, hat_ref, far_ref, rows_ref, send_sem, recv_sem
):
    half, layer = pl.program_id(0), pl.program_id(1)
    me = lax.axis_index(HEADS)
    beside_x, beside_y = beside(me)

    def relays():
        return [
            pltpu.make_async_remote_copy(
                src_ref=source_ref.at[slot],
                dst_ref=far_ref.at[at],
                send_sem=send_sem.at[at],
                recv_sem=recv_sem.at[at],
                device_id={HEADS: peer},
            )
            for at, (slot, peer) in enumerate(((2, beside_x), (1, beside_y)))
        ]

    @pl.when((half == 0) & (layer == 0))
    def _():
        barrier = pltpu.get_barrier_semaphore()
        for peer in (beside_x, beside_y):
            pl.semaphore_signal(barrier, inc=1, device_id={HEADS: peer})
        pl.semaphore_wait(barrier, 2)
        for copy in relays():
            copy.start()

    media_rows(half, layer, own_ref, gain_ref, weight_ref, keys_ref, hat_ref, rows_ref, near_ref)

    @pl.when((half == 5) & (layer == 1))
    def _():
        for copy in relays():
            copy.wait()


def media_near(own, near, gains, weight, columns, count):
    _, videos, patches, width = own.shape
    rows = videos * patches
    any_spec = pl.BlockSpec(memory_space=pl.ANY)
    return pl.pallas_call(
        functools.partial(near_kernel, count),
        grid=(6, 2),
        out_shape=(
            jax.ShapeDtypeStruct((8, videos, patches, columns), BF),
            jax.ShapeDtypeStruct((8, videos, patches, width), BF),
            jax.ShapeDtypeStruct(own.shape, BF),
        ),
        in_specs=[
            pl.BlockSpec((1, videos, patches, width), lambda i, j: (jnp.minimum(i, 1), 0, 0, 0)),
            pl.BlockSpec((1, videos, patches, width), lambda i, j: (jnp.maximum(i - 2, 0), 0, 0, 0)),
            pl.BlockSpec(gains.shape, lambda i, j: (0, 0, 0)),
            pl.BlockSpec((width, columns // 2), lambda i, j: (0, j)),
            any_spec,
        ],
        out_specs=(
            pl.BlockSpec((1, videos, patches, columns // 2), lambda i, j: (i, 0, 0, j)),
            pl.BlockSpec((1, videos, patches, width), lambda i, j: (i, 0, 0, 0)),
            any_spec,
        ),
        scratch_shapes=[
            pltpu.VMEM((rows, width), F32),
            pltpu.SemaphoreType.DMA((2,)),
            pltpu.SemaphoreType.DMA((2,)),
        ],
        compiler_params=pltpu.CompilerParams(
            collective_id=6, has_side_effects=True, vmem_limit_bytes=60 * MIB
        ),
        cost_estimate=pl.CostEstimate(
            flops=12 * rows * width * columns, bytes_accessed=24 * rows * width, transcendentals=0
        ),
        name="media_near",
    )(own, near, gains, weight, near)


def far_kernel(
    count, chunk_ref, gain_ref, weight_ref, slope_ref, keys_in, hat_in, keys_ref, hat_ref, full_ref, rows_ref, *sems
):
    half, layer = pl.program_id(0), pl.program_id(1)
    send_sem, recv_sem, own_sem = sems
    me = lax.axis_index(HEADS)
    share = slope_ref.shape[1]

    def copies():
        return [
            pltpu.make_async_remote_copy(
                src_ref=slope_ref,
                dst_ref=own_rows(full_ref, me, share),
                send_sem=send_sem.at[step - 1],
                recv_sem=recv_sem.at[step - 1],
                device_id={HEADS: (me + step) % count},
            )
            for step in range(1, count)
        ] + [pltpu.make_async_copy(slope_ref, own_rows(full_ref, me, share), own_sem)]

    @pl.when((half == 0) & (layer == 0))
    def _():
        greet(count)
        for copy in copies():
            copy.start()

    media_rows(half, layer, chunk_ref, gain_ref, weight_ref, keys_ref, hat_ref, rows_ref)

    @pl.when((half == 1) & (layer == 1))
    def _():
        for copy in copies():
            copy.wait()


def media_far(far, gains, weight, slope, keys, hat, count):
    _, videos, patches, width = far.shape
    columns = keys.shape[3]
    rows = videos * patches
    share = slope.shape[1]
    any_spec = pl.BlockSpec(memory_space=pl.ANY)
    return pl.pallas_call(
        functools.partial(far_kernel, count),
        grid=(2, 2),
        out_shape=(
            jax.ShapeDtypeStruct(keys.shape, BF),
            jax.ShapeDtypeStruct(hat.shape, BF),
            jax.ShapeDtypeStruct((videos, share * count, width), BF),
        ),
        in_specs=[
            pl.BlockSpec((1, videos, patches, width), lambda i, j: (i, 0, 0, 0)),
            pl.BlockSpec(gains.shape, lambda i, j: (0, 0, 0)),
            pl.BlockSpec((width, columns // 2), lambda i, j: (0, j)),
            any_spec,
            any_spec,
            any_spec,
        ],
        out_specs=(
            pl.BlockSpec((1, videos, patches, columns // 2), lambda i, j: (6 + i, 0, 0, j)),
            pl.BlockSpec((1, videos, patches, width), lambda i, j: (6 + i, 0, 0, 0)),
            any_spec,
        ),
        scratch_shapes=[
            pltpu.VMEM((rows, width), F32),
            pltpu.SemaphoreType.DMA((count - 1,)),
            pltpu.SemaphoreType.DMA((count - 1,)),
            pltpu.SemaphoreType.DMA,
        ],
        input_output_aliases={4: 0, 5: 1},
        compiler_params=pltpu.CompilerParams(
            collective_id=8, has_side_effects=True, vmem_limit_bytes=60 * MIB
        ),
        cost_estimate=pl.CostEstimate(
            flops=4 * rows * width * columns, bytes_accessed=8 * rows * width, transcendentals=0
        ),
        name="media_far",
    )(far, gains, weight, slope, keys, hat)


def head_mask(rows, columns, head):
    place = lax.broadcasted_iota(jnp.int32, (rows, columns), 1)
    return (place >= head * HD) & (place < (head + 1) * HD)


def spread_heads(rows):
    heads = rows.shape[1] // HD
    zero = jnp.zeros_like(rows)
    return jnp.concatenate(
        [jnp.where(head_mask(*rows.shape, head), rows, zero) for head in range(heads)], axis=0
    )


def gather_heads(rows, count):
    heads = rows.shape[1] // HD
    total = jnp.zeros((count, rows.shape[1]), F32)
    for head in range(heads):
        part = rows[head * count : (head + 1) * count]
        total = total + jnp.where(head_mask(*part.shape, head), part, 0.0)
    return total


def attend_kernel(live_ref, query_ref, latent_key_ref, latent_value_ref, key_ref, value_ref, mixed_ref, *, scale):
    video = pl.program_id(0)
    slots, patches = key_ref.shape[0], key_ref.shape[2]
    query = spread_heads(query_ref[...])
    rows, columns = query.shape
    place = lax.broadcasted_iota(jnp.int32, (rows, 2 * patches), 1)
    scores = []
    for pair in range(slots // 2):
        keys = key_ref[2 * pair : 2 * pair + 2, 0].reshape(2 * patches, columns)
        score = lax.dot_general(query, keys, NT, preferred_element_type=F32) * scale
        live = jnp.where(place < patches, live_ref[video, 2 * pair], live_ref[video, 2 * pair + 1])
        scores.append(jnp.where(live > 0, score, MASKED_SCORE))
    scores.append(lax.dot_general(query, latent_key_ref[...], NT, preferred_element_type=F32) * scale)
    top = functools.reduce(jnp.maximum, [jnp.max(score, axis=-1, keepdims=True) for score in scores])
    exponents = [jnp.exp(score - top) for score in scores]
    total = functools.reduce(jnp.add, [jnp.sum(e, axis=-1, keepdims=True) for e in exponents])
    mixed = jnp.zeros((rows, columns), F32)
    for pair in range(slots // 2):
        values = value_ref[2 * pair : 2 * pair + 2, 0].reshape(2 * patches, columns)
        mixed = mixed + jnp.dot((exponents[pair] / total).astype(BF), values, preferred_element_type=F32)
    mixed = mixed + jnp.dot(
        (exponents[-1] / total).astype(BF), latent_value_ref[...], preferred_element_type=F32
    )
    mixed_ref[...] = gather_heads(mixed, query_ref.shape[0]).astype(BF)


def attend_fast(live, query, latent_pair, keys, layer, scale):
    slots, videos, patches, _ = keys.shape
    count, columns = query.shape[0] // videos, query.shape[1]
    row_block = pl.BlockSpec((count, columns), lambda v: (v, 0))
    return pl.pallas_call(
        functools.partial(attend_kernel, scale=scale),
        grid=(videos,),
        out_shape=jax.ShapeDtypeStruct(query.shape, BF),
        in_specs=[
            pl.BlockSpec(memory_space=pltpu.SMEM),
            row_block,
            row_block,
            pl.BlockSpec((count, columns), lambda v: (v, 1)),
            pl.BlockSpec((slots, 1, patches, columns), lambda v: (0, v, 0, 2 * layer)),
            pl.BlockSpec((slots, 1, patches, columns), lambda v: (0, v, 0, 2 * layer + 1)),
        ],
        out_specs=row_block,
        compiler_params=pltpu.CompilerParams(vmem_limit_bytes=28 * MIB),
        cost_estimate=pl.CostEstimate(
            flops=8 * slots * patches * videos * count * 2 * columns,
            bytes_accessed=4 * slots * videos * patches * columns,
            transcendentals=slots * patches * videos * count * 4,
        ),
        name="attend",
    )(live, query, latent_pair, latent_pair, keys, keys)


def attend_back_kernel(
    live_ref, query_ref, latent_key_ref, latent_value_ref, key_ref, value_ref, slope_ref, *rest, scale
):
    query_slope_ref, latent_slope_ref, media_slope_ref, sums_ref = rest[-4:]
    video = pl.program_id(0)
    slots, patches = key_ref.shape[0], key_ref.shape[2]
    pairs = slots // 2
    count = query_ref.shape[0]
    query, slope = spread_heads(query_ref[...]), spread_heads(slope_ref[...])
    rows, columns = query.shape
    place = lax.broadcasted_iota(jnp.int32, (2 * patches, rows), 0)

    def keys_of(ref, pair):
        return ref[2 * pair : 2 * pair + 2, 0].reshape(2 * patches, columns)

    scores = []
    for pair in range(pairs):
        score = lax.dot_general(keys_of(key_ref, pair), query, NT, preferred_element_type=F32) * scale
        live = jnp.where(place < patches, live_ref[video, 2 * pair], live_ref[video, 2 * pair + 1])
        scores.append(jnp.where(live > 0, score, MASKED_SCORE))
    scores.append(lax.dot_general(latent_key_ref[...], query, NT, preferred_element_type=F32) * scale)
    top = functools.reduce(jnp.maximum, [jnp.max(score, axis=0, keepdims=True) for score in scores])
    exponents = [jnp.exp(score - top) for score in scores]
    total = functools.reduce(jnp.add, [jnp.sum(e, axis=0, keepdims=True) for e in exponents])
    shares = [e / total for e in exponents]
    share_slopes = [
        lax.dot_general(keys_of(value_ref, pair), slope, NT, preferred_element_type=F32)
        for pair in range(pairs)
    ]
    share_slopes.append(
        lax.dot_general(latent_value_ref[...], slope, NT, preferred_element_type=F32)
    )
    row_total = functools.reduce(
        jnp.add,
        [jnp.sum(a * b, axis=0, keepdims=True) for a, b in zip(shares, share_slopes)],
    )
    query_slope = jnp.zeros((rows, columns), F32)
    key_sum, value_sum = jnp.zeros((1, columns), F32), jnp.zeros((1, columns), F32)
    for at in range(pairs + 1):
        keys = keys_of(key_ref, at) if at < pairs else latent_key_ref[...]
        score_slope = (shares[at] * (share_slopes[at] - row_total)).astype(BF)
        key_slope = (jnp.dot(score_slope, query, preferred_element_type=F32) * scale).astype(BF)
        value_slope = jnp.dot(shares[at].astype(BF), slope, preferred_element_type=F32).astype(BF)
        query_slope = query_slope + lax.dot_general(
            score_slope, keys, TN, preferred_element_type=F32
        )
        if at < pairs:
            key_sum = key_sum + jnp.sum(key_slope.astype(F32), axis=0, keepdims=True)
            value_sum = value_sum + jnp.sum(value_slope.astype(F32), axis=0, keepdims=True)
            media_slope_ref[2 * at : 2 * at + 2, 0, :, :columns] = key_slope.reshape(2, patches, columns)
            media_slope_ref[2 * at : 2 * at + 2, 0, :, columns:] = value_slope.reshape(2, patches, columns)
        else:
            latent_slope_ref[:, :columns] = key_slope
            latent_slope_ref[:, columns:] = value_slope
    sums_ref[0, :, :columns] = key_sum
    sums_ref[0, :, columns:] = value_sum
    query_slope_ref[...] = (gather_heads(query_slope, count) * scale).astype(BF)


def attend_back_fast(live, query, latent_pair, keys, slope, layer, scale, earlier):
    slots, videos, patches, _ = keys.shape
    count, columns = query.shape[0] // videos, query.shape[1]
    row_block = pl.BlockSpec((count, columns), lambda v: (v, 0))
    in_specs = [
        pl.BlockSpec(memory_space=pltpu.SMEM),
        row_block,
        row_block,
        pl.BlockSpec((count, columns), lambda v: (v, 1)),
        pl.BlockSpec((slots, 1, patches, columns), lambda v: (0, v, 0, 2 * layer)),
        pl.BlockSpec((slots, 1, patches, columns), lambda v: (0, v, 0, 2 * layer + 1)),
        row_block,
    ]
    aliases = {}
    if earlier:
        in_specs += [pl.BlockSpec(memory_space=pl.ANY)]
        aliases = {7: 2}
    return pl.pallas_call(
        functools.partial(attend_back_kernel, scale=scale),
        grid=(videos,),
        out_shape=(
            jax.ShapeDtypeStruct(query.shape, BF),
            jax.ShapeDtypeStruct(latent_pair.shape, BF),
            jax.ShapeDtypeStruct(keys.shape, BF),
            jax.ShapeDtypeStruct((videos, 1, 2 * columns), F32),
        ),
        in_specs=in_specs,
        out_specs=(
            row_block,
            pl.BlockSpec((count, 2 * columns), lambda v: (v, 0)),
            pl.BlockSpec((slots, 1, patches, 2 * columns), lambda v: (0, v, 0, layer)),
            pl.BlockSpec((1, 1, 2 * columns), lambda v: (v, 0, 0)),
        ),
        input_output_aliases=aliases,
        compiler_params=pltpu.CompilerParams(vmem_limit_bytes=60 * MIB),
        cost_estimate=pl.CostEstimate(
            flops=20 * slots * patches * videos * count * 2 * columns,
            bytes_accessed=8 * slots * videos * patches * columns,
            transcendentals=slots * patches * videos * count * 4,
        ),
        name="attend_back",
    )(live, query, latent_pair, latent_pair, keys, keys, slope, *earlier)


def product_pair_kernel(begin, first_ref, second_ref, third_ref, fourth_ref, *rest):
    step = pl.program_id(0)
    count = len(rest) - 5
    extra, (out_ref, tile_ref, extra_ref, tile_sem, extra_sem) = rest[:count], rest[count:]
    cut, half = tile_ref.shape[2], pl.num_programs(0) // 2

    def moves():
        at = 0
        for number, ref in enumerate(extra):
            lines = pl.ds(at, ref.shape[1])
            yield pltpu.make_async_copy(ref, extra_ref.at[:, lines], extra_sem.at[number])
            at += ref.shape[1]

    def store(at):
        lines = pl.ds(pl.multiple_of(begin + at * cut, 128), cut)
        return pltpu.make_async_copy(tile_ref.at[at % 2], out_ref.at[:, lines], tile_sem.at[at % 2])

    def store_extra():
        return pltpu.make_async_copy(extra_ref, out_ref.at[:, pl.ds(0, begin)], extra_sem.at[count])

    if count:

        @pl.when(step == 0)
        def _():
            for copy in moves():
                copy.start()

        @pl.when(step == 2)
        def _():
            for copy in moves():
                copy.wait()
            store_extra().start()

    @pl.when(step >= 2)
    def _():
        store(step - 2).wait()

    @pl.when(step < half)
    def _():
        tile_ref[step % 2] = mm(first_ref[...], second_ref[...], TN)

    @pl.when(step >= half)
    def _():
        tile_ref[step % 2] = mm(third_ref[...], fourth_ref[...], TN)

    store(step).start()

    @pl.when(step == 2 * half - 1)
    def _():
        store(step - 1).wait()
        store(step).wait()
        if count:
            store_extra().wait()


def product_pair(first, second, third, fourth, *extra):
    rows, width, columns = first.shape[0], first.shape[1], second.shape[1]
    cut = columns // 3
    begin = sum(piece.shape[1] for piece in extra)
    left = pl.BlockSpec((rows, width), lambda i: (0, 0))
    any_spec = pl.BlockSpec(memory_space=pl.ANY)
    return pl.pallas_call(
        functools.partial(product_pair_kernel, begin),
        grid=(6,),
        out_shape=jax.ShapeDtypeStruct((width, begin + 2 * columns), BF),
        in_specs=[
            left,
            pl.BlockSpec((rows, cut), lambda i: (0, jnp.minimum(i, 2))),
            left,
            pl.BlockSpec((rows, cut), lambda i: (0, jnp.maximum(i - 3, 0))),
        ]
        + [any_spec] * len(extra),
        out_specs=any_spec,
        scratch_shapes=[
            pltpu.VMEM((2, width, cut), BF),
            pltpu.VMEM((width, max(begin, 128)), BF),
            pltpu.SemaphoreType.DMA((2,)),
            pltpu.SemaphoreType.DMA((4,)),
        ],
        compiler_params=pltpu.CompilerParams(vmem_limit_bytes=60 * MIB),
        cost_estimate=pl.CostEstimate(
            flops=4 * rows * width * columns, bytes_accessed=8 * width * columns, transcendentals=0
        ),
        name="feed_gradients",
    )(first, second, third, fourth, *extra)


def start_scatter(me, count, share, part_ref, landed_ref, send_sem, recv_sem):
    copies = []
    for step in range(1, count):
        peer = (me + step) % count
        copy = pltpu.make_async_remote_copy(
            src_ref=own_rows(part_ref, peer, share),
            dst_ref=landed_ref.at[step - 1],
            send_sem=send_sem.at[step - 1],
            recv_sem=recv_sem.at[step - 1],
            device_id={HEADS: peer},
        )
        copy.start()
        copies.append(copy)
    return copies


def forward_kernel(
    count, last, part_ref, rest_ref, gain_ref, new_ref, *refs
):
    refs = list(refs)
    full_ref = None if last else refs.pop(0)
    landed_ref, own_ref, send_sem, recv_sem, send_more, recv_more = refs
    me = greet(count)
    share = rest_ref.shape[1]
    copies = start_scatter(me, count, share, part_ref, landed_ref, send_sem, recv_sem)
    mine = pl.ds(pl.multiple_of(me * share, share), share)
    total = rest_ref[...] + part_ref[:, mine, :].astype(F32)
    for step, copy in enumerate(copies):
        copy.wait_recv()
        total = total + landed_ref[step].astype(F32)
    new_ref[...] = total
    if not last:
        own_ref[...] = layer_norm(total, gain_ref[0], gain_ref[1]).astype(BF)
        more = start_gather(me, count, share, own_ref, full_ref, send_more, recv_more)
        full_ref[:, mine, :] = own_ref[...]
        for copy in more:
            copy.wait()
    for copy in copies:
        copy.wait_send()


def forward_exchange(part, rest, gain, count, last=False):
    videos, share, width = rest.shape
    outs = [jax.ShapeDtypeStruct(rest.shape, F32)]
    if not last:
        outs.append(jax.ShapeDtypeStruct(part.shape, BF))
    got = pl.pallas_call(
        functools.partial(forward_kernel, count, last),
        out_shape=tuple(outs),
        in_specs=[vmem_spec()] * 3,
        out_specs=(vmem_spec(),) * len(outs),
        scratch_shapes=[
            pltpu.VMEM((count - 1, videos, share, width), BF),
            pltpu.VMEM((videos, share, width), BF),
        ]
        + [pltpu.SemaphoreType.DMA((count - 1,))] * 4,
        compiler_params=pltpu.CompilerParams(
            collective_id=3 if last else 2, has_side_effects=True, vmem_limit_bytes=14 * MIB
        ),
        cost_estimate=pl.CostEstimate(flops=0, bytes_accessed=75 * 1000 * 1000, transcendentals=0),
        name="forward_exchange",
    )(part, rest, gain)
    return got if not last else (got[0], None)


def backward_kernel(
    count, last, part_ref, rows_ref, rest_ref, gain_ref, new_ref, sums_ref, *refs
):
    refs = list(refs)
    full_ref = None if last else refs.pop(0)
    landed_ref, own_ref, send_sem, recv_sem, send_more, recv_more = refs
    me = greet(count)
    share = rest_ref.shape[1]
    copies = start_scatter(me, count, share, part_ref, landed_ref, send_sem, recv_sem)
    mine = pl.ds(pl.multiple_of(me * share, share), share)
    rows = rows_ref[...]
    centred = rows - jnp.mean(rows, axis=-1, keepdims=True)
    scale = lax.rsqrt(jnp.mean(centred * centred, axis=-1, keepdims=True) + EPS_NORM)
    hat = centred * scale
    slope = part_ref[:, mine, :].astype(F32)
    for step, copy in enumerate(copies):
        copy.wait_recv()
        slope = slope + landed_ref[step].astype(F32)
    hat_slope = slope * gain_ref[0]
    back = hat_slope - jnp.mean(hat_slope, axis=-1, keepdims=True)
    back = back - hat * jnp.mean(hat_slope * hat, axis=-1, keepdims=True)
    new = rest_ref[...] + back * scale
    new_ref[...] = new
    if not last:
        own_ref[...] = new.astype(BF)
        more = start_gather(me, count, share, own_ref, full_ref, send_more, recv_more)
        full_ref[:, mine, :] = own_ref[...]
    sums_ref[0:1] = jnp.sum(jnp.sum(slope * hat, axis=0), axis=0, keepdims=True)
    sums_ref[1:2] = jnp.sum(jnp.sum(slope, axis=0), axis=0, keepdims=True)
    if not last:
        for copy in more:
            copy.wait()
    for copy in copies:
        copy.wait_send()


def backward_exchange(part, rows, rest, gain, count, last=False):
    videos, share, width = rest.shape
    outs = [jax.ShapeDtypeStruct(rest.shape, F32), jax.ShapeDtypeStruct((2, width), F32)]
    if not last:
        outs.append(jax.ShapeDtypeStruct(part.shape, BF))
    got = pl.pallas_call(
        functools.partial(backward_kernel, count, last),
        out_shape=tuple(outs),
        in_specs=[vmem_spec()] * 4,
        out_specs=(vmem_spec(),) * len(outs),
        scratch_shapes=[
            pltpu.VMEM((count - 1, videos, share, width), BF),
            pltpu.VMEM((videos, share, width), BF),
        ]
        + [pltpu.SemaphoreType.DMA((count - 1,))] * 4,
        compiler_params=pltpu.CompilerParams(
            collective_id=5 if last else 4, has_side_effects=True, vmem_limit_bytes=14 * MIB
        ),
        cost_estimate=pl.CostEstimate(flops=0, bytes_accessed=75 * 1000 * 1000, transcendentals=0),
        name="backward_exchange",
    )(part, rows, rest, gain)
    return got if not last else (*got, None)


def sum_kernel(heads, rows, lines, term_in, *refs):
    shares, (out_ref, term_ref, plane_ref, line_ref, part_ref), sems = refs[:3], refs[3:8], refs[8:]
    me_head, me_row = lax.axis_index(HEADS), lax.axis_index(ROWS)
    barrier = pltpu.get_barrier_semaphore()
    for step in range(1, heads):
        pl.semaphore_signal(barrier, inc=1, device_id={HEADS: (me_head + step) % heads})
    for step in range(1, rows):
        pl.semaphore_signal(barrier, inc=1, device_id={ROWS: (me_row + step) % rows})
    term_ref[...] = term_in[...]
    total = jnp.zeros((16, 384), F32)
    for share in shares:

        def add_squares(at, total, share=share):
            line = pl.ds(pl.multiple_of(at * 16, 16), 16)
            for begin in range(0, share.shape[1], 384):
                wide = share[line, begin : begin + 384].astype(F32)
                total = total + wide * wide
            return total

        total = lax.fori_loop(0, share.shape[0] // 16, add_squares, total)
    total = jnp.sum(total, axis=0, keepdims=True)
    term_ref[0, lines : lines + 1] = total[:, :128] + total[:, 128:256] + total[:, 256:]
    pl.semaphore_wait(barrier, heads - 1 + rows - 1)

    def spread(axis, me, count, source_of, slots_ref, own, send, recv):
        copies = []
        for step in range(1, count):
            peer = (me + step) % count
            copy = pltpu.make_async_remote_copy(
                src_ref=source_of(peer),
                dst_ref=slots_ref.at[me],
                send_sem=send.at[step - 1],
                recv_sem=recv.at[step - 1],
                device_id={axis: peer},
            )
            copy.start()
            copies.append(copy)
        slots_ref[pl.ds(me, 1)] = own[None]
        for copy in copies:
            copy.wait()

    def added(slots_ref, count):
        total = slots_ref[0]
        for at in range(1, count):
            total = total + slots_ref[at]
        return total

    mine = term_ref[pl.ds(me_head, 1)][0]
    spread(HEADS, me_head, heads, lambda peer: term_ref.at[peer], plane_ref, mine, *sems[0:2])
    part_ref[0] = added(plane_ref, heads)
    spread(ROWS, me_row, rows, lambda peer: part_ref.at[0], line_ref, part_ref[0], *sems[2:4])
    part_ref[1] = added(line_ref, rows)
    spread(HEADS, me_head, heads, lambda peer: part_ref.at[1], out_ref, part_ref[1], *sems[4:6])


def sum_fast(term, shares, lines, heads, rows, identity):
    block = term.shape[1:]
    return pl.pallas_call(
        functools.partial(sum_kernel, heads, rows, lines),
        out_shape=jax.ShapeDtypeStruct(term.shape, F32),
        in_specs=[vmem_spec()] * 4,
        out_specs=vmem_spec(),
        scratch_shapes=[
            pltpu.VMEM(term.shape, F32),
            pltpu.VMEM((heads, *block), F32),
            pltpu.VMEM((rows, *block), F32),
            pltpu.VMEM((2, *block), F32),
            pltpu.SemaphoreType.DMA((heads - 1,)),
            pltpu.SemaphoreType.DMA((heads - 1,)),
            pltpu.SemaphoreType.DMA((rows - 1,)),
            pltpu.SemaphoreType.DMA((rows - 1,)),
            pltpu.SemaphoreType.DMA((heads - 1,)),
            pltpu.SemaphoreType.DMA((heads - 1,)),
        ],
        compiler_params=pltpu.CompilerParams(
            collective_id=identity, has_side_effects=True, vmem_limit_bytes=16 * MIB
        ),
        cost_estimate=pl.CostEstimate(flops=0, bytes_accessed=40 * 1000 * 1000, transcendentals=0),
        name="sum_over_all",
    )(term, *shares)


def last_kernel(
    chips,
    heads,
    query_ref,
    pair_ref,
    rest_part_ref,
    near_x_ref,
    near_y_ref,
    over_x_ref,
    over_y_ref,
    slopes_ref,
    scaled_ref,
    slots_ref,
    final_ref,
    final_rest_ref,
    rows_ref,
    rest_ref,
    gain_ref,
    out_ref,
    from_x_ref,
    from_y_ref,
    new_ref,
    sums_ref,
    final_out_ref,
    back_ref,
    mine_ref,
    other_ref,
    down_ref,
    up_ref,
    landed_ref,
    final_landed_ref,
    to_x_ref,
    to_y_ref,
    add_x_ref,
    add_y_ref,
    weight_ref,
    chunk_ref,
    near_sem,
    local_sem,
    slot_send,
    slot_recv,
    final_send,
    final_recv,
    down_send,
    down_recv,
    up_send,
    up_recv,
):
    head, place = lax.axis_index(HEADS), lax.axis_index(ROWS)
    z, core = place // 2, place % 2
    sibling, above, below = place + 1 - 2 * core, place + 2, place - 2
    beside_x, beside_y = head + 1 - 2 * (head % 2), (head + 2) % heads
    has_above, has_below = z < chips - 1, z > 0
    depth = out_ref.shape[0]
    pieces = down_send.shape[1]
    cut = depth // pieces

    barrier = pltpu.get_barrier_semaphore()
    for step in range(1, heads):
        pl.semaphore_signal(barrier, inc=1, device_id={HEADS: (head + step) % heads})
    pl.semaphore_signal(barrier, inc=1, device_id={ROWS: sibling})

    for step in (2, 2 * chips - 2):
        pl.semaphore_signal(barrier, inc=1, device_id={ROWS: (place + step) % (2 * chips)})
    pl.semaphore_wait(barrier, heads + 2)

    share = rest_ref.shape[1]
    slots = start_scatter(head, heads, share, slots_ref, landed_ref, slot_send, slot_recv)
    finals = start_scatter(head, heads, share, final_ref, final_landed_ref, final_send, final_recv)
    whole = [query_ref, pair_ref, rest_part_ref]
    begins = [0]
    for ref in whole:
        begins.append(begins[-1] + ref.shape[3])
    over, keep = [], []
    for at, ref in enumerate(whole):
        lines = pl.ds(begins[at], ref.shape[3])
        copy = pltpu.make_async_remote_copy(
            src_ref=ref.at[:, 1 - core],
            dst_ref=other_ref.at[:, :, lines],
            send_sem=near_sem.at[at],
            recv_sem=near_sem.at[3 + at],
            device_id={ROWS: sibling},
        )
        copy.start()
        over.append(copy)
        copy = pltpu.make_async_copy(ref.at[:, core], mine_ref.at[:, :, lines], local_sem.at[at])
        copy.start()
        keep.append(copy)
    loads = []
    for at, (source, target) in enumerate(
        (
            (near_x_ref, to_x_ref),
            (over_y_ref, add_x_ref),
            (near_y_ref, to_y_ref),
            (over_x_ref, add_y_ref),
            (scaled_ref, weight_ref),
            (slopes_ref.at[pl.ds(0, 2)], chunk_ref),
        )
    ):
        loads.append(pltpu.make_async_copy(source, target, local_sem.at[3 + at]))
        loads[-1].start()
    medias = []
    for at, (to_ref, add_ref, from_ref, peer) in enumerate(
        ((to_x_ref, add_x_ref, from_x_ref, beside_x), (to_y_ref, add_y_ref, from_y_ref, beside_y))
    ):
        loads[2 * at].wait()
        loads[2 * at + 1].wait()
        for video in range(to_ref.shape[0]):

            def add_slopes(row, carry, to_ref=to_ref, add_ref=add_ref, video=video):
                lines = pl.ds(pl.multiple_of(row * 16, 16), 16)
                to_ref[video, lines] = (
                    to_ref[video, lines].astype(F32) + add_ref[video, lines].astype(F32)
                ).astype(BF)
                return carry

            lax.fori_loop(0, to_ref.shape[1] // 16, add_slopes, 0)
        copy = pltpu.make_async_remote_copy(
            src_ref=to_ref,
            dst_ref=from_ref,
            send_sem=near_sem.at[6 + 2 * at],
            recv_sem=near_sem.at[7 + 2 * at],
            device_id={HEADS: peer},
        )
        copy.start()
        medias.append(copy)
    for copy in keep:
        copy.wait()
    for copy in over:
        copy.wait()
    for chip in range(chips):

        def add_rows(at, carry, chip=chip):
            lines = pl.ds(pl.multiple_of(at * 16, 16), 16)
            mine_ref[chip, lines] = (
                mine_ref[chip, lines].astype(F32) + other_ref[chip, lines].astype(F32)
            ).astype(BF)
            return carry

        lax.fori_loop(0, depth // 16, add_rows, 0)

    def chain(step, piece, down):
        landed, send, recv = (down_ref, down_send, down_recv) if down else (up_ref, up_send, up_recv)
        owner = z - chips + step if down else z + chips - step
        lines = pl.ds(piece * cut, cut)
        return pltpu.make_async_remote_copy(
            src_ref=mine_ref.at[owner, lines],
            dst_ref=landed.at[step - 1, lines],
            send_sem=send.at[step - 1, piece],
            recv_sem=recv.at[step - 1, piece],
            device_id={ROWS: below if down else above},
        )

    def take(step, piece, down, owner):
        landed, recv = (down_ref, down_recv) if down else (up_ref, up_recv)
        lines = pl.ds(piece * cut, cut)
        arrival = pltpu.make_async_remote_copy(
            src_ref=mine_ref.at[z, lines],
            dst_ref=landed.at[step - 1, lines],
            send_sem=recv.at[step - 1, piece],
            recv_sem=recv.at[step - 1, piece],
            device_id={ROWS: sibling},
        )
        arrival.wait_recv()
        mine_ref[owner, lines] = (
            mine_ref[owner, lines].astype(F32) + landed[step - 1, lines].astype(F32)
        ).astype(BF)

    for step in range(1, chips):
        for piece in range(pieces):
            for down in (True, False):
                sends = (z >= chips - step) if down else (z <= step - 1)
                takes = sends & (has_above if down else has_below)
                owner = z - chips + step if down else z + chips - step

                if step > 1:

                    @pl.when(takes)
                    def _():
                        take(step - 1, piece, down, owner)

                @pl.when(sends)
                def _():
                    chain(step, piece, down).start()

    loads[4].wait()
    loads[5].wait()
    videos, patches, width = chunk_ref.shape[1:]
    tile = width // 4

    def own_slopes(at, carry):
        half = at // 4
        lines = pl.ds(pl.multiple_of((at % 4) * tile, tile), tile)
        made = mm(chunk_ref[half].reshape(videos * patches, width), weight_ref[lines], NT)
        back_ref[half, :, :, lines] = made.reshape(videos, patches, tile)
        return carry

    lax.fori_loop(0, 8, own_slopes, 0)
    rows = rows_ref[...]
    centred = rows - jnp.mean(rows, axis=-1, keepdims=True)
    scale = lax.rsqrt(jnp.mean(centred * centred, axis=-1, keepdims=True) + EPS_NORM)
    hat = centred * scale
    own_slots = pl.ds(pl.multiple_of(head * share, share), share)
    final = final_rest_ref[...] + final_ref[:, own_slots, :].astype(F32)
    for at, copy in enumerate(finals):
        copy.wait_recv()
        final = final + final_landed_ref[at].astype(F32)
    final_out_ref[...] = final
    slope = slots_ref[:, own_slots, :].astype(F32)
    for at, copy in enumerate(slots):
        copy.wait_recv()
        slope = slope + landed_ref[at].astype(F32)
    hat_slope = slope * gain_ref[0]
    back = hat_slope - jnp.mean(hat_slope, axis=-1, keepdims=True)
    back = back - hat * jnp.mean(hat_slope * hat, axis=-1, keepdims=True)
    new_ref[...] = rest_ref[...] + back * scale
    sums_ref[0:1] = jnp.sum(jnp.sum(slope * hat, axis=0), axis=0, keepdims=True)
    sums_ref[1:2] = jnp.sum(jnp.sum(slope, axis=0), axis=0, keepdims=True)

    for piece in range(pieces):

        @pl.when(has_above)
        def _():
            take(chips - 1, piece, True, z)

        @pl.when(has_below)
        def _():
            take(chips - 1, piece, False, z)

    out_ref[...] = mine_ref[z]
    for step in range(1, chips):
        for piece in range(pieces):

            @pl.when(z >= chips - step)
            def _():
                chain(step, piece, True).wait_send()

            @pl.when(z <= step - 1)
            def _():
                chain(step, piece, False).wait_send()

    for copy in slots + finals:
        copy.wait_send()
    for copy in medias:
        copy.wait()


def last_step(parts, near, over, slopes, scaled, slots, final, final_rest, rows, rest, gain, heads, chips):
    depth, columns = parts[0].shape[0] // (2 * chips), sum(part.shape[1] for part in parts)
    videos, share, width = rest.shape
    pieces = 4
    any_spec = pl.BlockSpec(memory_space=pl.ANY)
    block = pltpu.VMEM((chips, depth, columns), BF)
    steps = pltpu.VMEM((chips - 1, depth, columns), BF)
    landed = pltpu.VMEM((heads - 1, videos, share, width), BF)
    chunk = pltpu.VMEM(near[0].shape, BF)
    chain_sem = pltpu.SemaphoreType.DMA((chips - 1, pieces))
    slot_sem = pltpu.SemaphoreType.DMA((heads - 1,))
    chunk_kind = jax.ShapeDtypeStruct(near[0].shape, BF)
    return pl.pallas_call(
        functools.partial(last_kernel, chips, heads),
        out_shape=(
            jax.ShapeDtypeStruct((depth, columns), BF),
            chunk_kind,
            chunk_kind,
            jax.ShapeDtypeStruct(rest.shape, F32),
            jax.ShapeDtypeStruct((2, width), F32),
            jax.ShapeDtypeStruct(rest.shape, F32),
            jax.ShapeDtypeStruct((2, *near[0].shape), BF),
        ),
        in_specs=[any_spec] * 9 + [vmem_spec()] * 6,
        out_specs=(vmem_spec(), any_spec, any_spec) + (vmem_spec(),) * 4,
        scratch_shapes=[block, block, steps, steps, landed, landed]
        + [chunk] * 4
        + [
            pltpu.VMEM(scaled.shape, BF),
            pltpu.VMEM((2, *near[0].shape), BF),
            pltpu.SemaphoreType.DMA((10,)),
            pltpu.SemaphoreType.DMA((9,)),
        ]
        + [slot_sem] * 4
        + [chain_sem] * 4,
        compiler_params=pltpu.CompilerParams(
            collective_id=7, has_side_effects=True, vmem_limit_bytes=60 * MIB
        ),
        cost_estimate=pl.CostEstimate(flops=0, bytes_accessed=160 * 1000 * 1000, transcendentals=0),
        name="last_step",
    )(
        *[part.reshape(chips, 2, depth, part.shape[1]) for part in parts],
        *near,
        *over,
        slopes,
        scaled,
        slots,
        final,
        final_rest,
        rows,
        rest,
        gain,
    )


def media_back_kernel(own_ref, back_ref, *refs):
    first, second, out_ref = refs[:2], refs[2:4], refs[-1]

    def write(*terms):
        rows = own_ref[0].astype(F32)
        centred = rows - jnp.mean(rows, axis=-1, keepdims=True)
        spread = lax.rsqrt(jnp.mean(centred * centred, axis=-1, keepdims=True) + EPS_NORM)
        hat = centred * spread
        total = functools.reduce(jnp.add, [term[...].astype(F32) for term in terms], back_ref[0].astype(F32))
        total = total - jnp.mean(total, axis=-1, keepdims=True) - hat * jnp.mean(total * hat, axis=-1, keepdims=True)
        total = total * spread
        for video in range(rows.shape[0]):
            out_ref[:, video, :] = total[video]

    @pl.when(pl.program_id(0) == 0)
    def _():
        write(*first)

    @pl.when(pl.program_id(0) == 1)
    def _():
        write(*second)


def media_back(own, back, in_x, in_y):
    _, videos, rows, width = own.shape
    cut = 32
    steps = rows // cut
    both = pl.BlockSpec((1, videos, cut, width), lambda i, j: (i, 0, j, 0))
    specs = [pl.BlockSpec((videos, cut, width), lambda i, j: (0, jnp.where(i == 0, j, steps - 1), 0))] * 2
    specs += [pl.BlockSpec((videos, cut, width), lambda i, j: (0, jnp.where(i == 1, j, 0), 0))] * 2
    return pl.pallas_call(
        media_back_kernel,
        grid=(2, steps),
        out_shape=jax.ShapeDtypeStruct((2 * rows, videos, width), F32),
        in_specs=[both, both] + specs,
        out_specs=pl.BlockSpec((cut, videos, width), lambda i, j: (steps * i + j, 0, 0)),
        compiler_params=pltpu.CompilerParams(vmem_limit_bytes=60 * MIB),
        cost_estimate=pl.CostEstimate(flops=0, bytes_accessed=30 * 1000 * 1000, transcendentals=0),
        name="media_back",
    )(own, back, in_x[0], in_y[0], in_x[1], in_y[1])


def adam_kernel(rates, begins, factor_ref, *refs):
    kinds, step = len(rates), pl.program_id(0)
    layers = (len(refs) // kinds) - 7
    factor = factor_ref[0, 0]
    ins = [refs[at * (3 + layers) : (at + 1) * (3 + layers)] for at in range(kinds)]
    outs = [refs[kinds * (3 + layers) + 4 * at :][:4] for at in range(kinds)]
    for kind in range(kinds):
        steps = (begins[kind + 1] - begins[kind]) // layers
        weight_ref, first_ref, second_ref = ins[kind][:3]
        mean_ref, square_ref, next_ref, copy_ref = outs[kind]
        columns = weight_ref.shape[3]
        for layer in range(layers):
            begin = begins[kind] + layer * steps

            @pl.when((step >= begin) & (step < begin + steps))
            def _():
                for part in range(weight_ref.shape[1]):
                    grad = ins[kind][3 + layer][:, part * columns : (part + 1) * columns]
                    scaled = grad.astype(F32) * factor
                    mean = BETA_ONE * first_ref[0, part] + (1.0 - BETA_ONE) * scaled
                    square = BETA_TWO * second_ref[0, part] + (1.0 - BETA_TWO) * scaled * scaled
                    root = jnp.sqrt(square * (1.0 / (1.0 - BETA_TWO**STEP))) + ADAM_EPS
                    change = (mean * (1.0 / (1.0 - BETA_ONE**STEP))) / root
                    weight = weight_ref[0, part]
                    weight = weight - rates[kind] * (change + WEIGHT_DECAY * weight)
                    mean_ref[0, part] = mean
                    square_ref[0, part] = square
                    next_ref[0, part] = weight
                    copy_ref[0, part] = weight.astype(BF)


def adam_fast(kinds, factor):
    layers = kinds[0][0].shape[0]
    begins = [0]
    for weight, _, _, _, cut, _ in kinds:
        begins.append(begins[-1] + layers * (weight.shape[2] // cut))
    operands, in_specs, out_specs, out_shape = [], [], [], []
    for kind, (weight, first, second, grads, cut, _) in enumerate(kinds):
        _, parts, rows, columns = weight.shape
        steps = rows // cut
        begin, end = begins[kind], begins[kind + 1]

        def place(i, begin=begin, end=end, steps=steps):
            at = jnp.clip(i, begin, end - 1) - begin
            return (at // steps, 0, at % steps, 0)

        spec = pl.BlockSpec((1, parts, cut, columns), place)
        operands += [weight, first, second]
        in_specs += [spec] * 3
        for layer, (grad, base) in enumerate(grads):

            def grad_place(i, begin=begin + layer * steps, steps=steps, base=base):
                return (jnp.clip(i, begin, begin + steps - 1) - begin, base)

            operands.append(grad)
            in_specs.append(pl.BlockSpec((cut, parts * columns), grad_place))
        wide = jax.ShapeDtypeStruct(weight.shape, F32)
        out_specs += [spec] * 4
        out_shape += [wide, wide, wide, jax.ShapeDtypeStruct(weight.shape, BF)]
    size = sum(kind[0].size for kind in kinds)
    made = pl.pallas_call(
        functools.partial(adam_kernel, [kind[-1] for kind in kinds], begins),
        grid=(begins[-1],),
        out_shape=tuple(out_shape),
        in_specs=[pl.BlockSpec(memory_space=pltpu.SMEM)] + in_specs,
        out_specs=tuple(out_specs),
        compiler_params=pltpu.CompilerParams(vmem_limit_bytes=60 * MIB),
        cost_estimate=pl.CostEstimate(flops=20 * size, bytes_accessed=28 * size, transcendentals=size),
        name="adam",
    )(factor, *operands)
    return [made[4 * at : 4 * at + 4] for at in range(len(kinds))]


def flat(rows):
    return rows.reshape(-1, rows.shape[-1])


def local_fast(
    media,
    latents,
    frame_count,
    cotangent,
    inward,
    inward_first,
    inward_second,
    outward,
    outward_first,
    outward_second,
    widen,
    widen_first,
    widen_second,
    narrow,
    narrow_first,
    narrow_second,
    norm_gains,
    gain_first,
    gain_second,
):
    heads_count, rows_count = lax.axis_size(HEADS), lax.axis_size(ROWS)
    me = lax.axis_index(HEADS)
    layers, _, row_share, head_columns = inward.shape
    local_positions, videos, width = media.shape
    latent_count = latents.shape[1] * heads_count
    scale = HD ** (-0.5)

    def swap_x(rows):
        return lax.ppermute(rows, HEADS, X_SWAP)

    def swap_y(rows):
        return lax.ppermute(rows, HEADS, Y_SWAP)

    def gather_rows(rows):
        return lax.all_gather(rows, ROWS, axis=0, tiled=True)

    outward_t, narrow_t = (jnp.swapaxes(outward, 1, 2), jnp.swapaxes(narrow, 1, 2))
    columns, units = head_columns, widen.shape[2]
    first_set = [inward[l, t] for l in range(layers) for t in (1, 2)]
    first_set = first_set + [inward[l, 0] for l in range(layers)] + [outward_t[l] for l in range(layers)]
    first_set = jnp.concatenate([piece.astype(BF) for piece in first_set], axis=1)

    latent = latents
    normed = layer_norm(latent, norm_gains[0, 2], norm_gains[0, 3]).astype(BF)
    slope_rows = cotangent.astype(BF)
    first_set = gather_rows(first_set)
    pair_weights = first_set[:, : 2 * layers * columns]
    begin = 2 * layers * columns
    query_full = [first_set[:, begin + l * columns : begin + (l + 1) * columns] for l in range(layers)]
    begin = begin + layers * columns
    out_full = [first_set[:, begin + l * columns : begin + (l + 1) * columns] for l in range(layers)]
    share = latents.shape[1]
    own = jnp.swapaxes(media.reshape(2, local_positions // 2, videos, width), 1, 2)
    later_sets = [
        jnp.concatenate((widen[layer].astype(BF), narrow_t[layer].astype(BF)), axis=1) for layer in range(layers)
    ]
    own, *later_sets = lax.optimization_barrier((own, *later_sets))
    later_sets = [gather_rows(rows) for rows in later_sets]
    widen_full = [rows[:, :units] for rows in later_sets]
    narrow_full = [rows[:, units:] for rows in later_sets]

    frames = jnp.stack([2 * (me ^ group) + half for group in range(4) for half in range(2)])
    live = (frames[None, :] < frame_count[:, None]).astype(jnp.int32)
    media_gains = norm_gains[:, 0:2]
    near, latent_norm = gather_near(own, normed, heads_count)
    keys, media_hat, far = media_near(own, near, media_gains, first_set, 2 * layers * columns, heads_count)
    keys, media_hat, feed_slope = media_far(far, media_gains, first_set, slope_rows, keys, media_hat, heads_count)
    scaled = jnp.concatenate(
        [
            (
                pair_weights[:, 2 * l * head_columns : 2 * (l + 1) * head_columns].astype(F32)
                * norm_gains[l, 0][:, None]
            ).astype(BF)
            for l in range(layers)
        ],
        axis=1,
    )

    kept = []
    for layer in range(layers):
        query_weight, out_weight = query_full[layer], out_full[layer]
        pair_weight = pair_weights[:, 2 * layer * head_columns : 2 * (layer + 1) * head_columns]
        query = mm(flat(latent_norm), query_weight)
        latent_pair = mm(flat(latent_norm), pair_weight)
        mixed = attend_fast(live, query, latent_pair, keys, layer, scale)
        part = mm(mixed, out_weight, NT).reshape(videos, latent_count, width)
        if layer == layers - 1:
            gain_rows = [rows.reshape(-1, width) for rows in (norm_gains, gain_first, gain_second)]
            part, scaled, *gain_rows = lax.optimization_barrier((part, scaled, *gain_rows))
        middle, feed_norm = forward_exchange(part, latent, norm_gains[layer, 4:6], heads_count)
        hidden_pre = mm(flat(feed_norm), widen_full[layer], None, F32)
        hidden = jax.nn.gelu(hidden_pre).astype(BF)
        part = mm(hidden, narrow_full[layer], NT).reshape(videos, latent_count, width)
        last = layer == layers - 1
        gain = norm_gains[0 if last else layer + 1, 2:4]
        kept.append((latent, middle, latent_norm, query, latent_pair, mixed, feed_norm, hidden_pre, hidden))
        if last:
            final_part, final_rest = part, middle
        else:
            latent, latent_norm = forward_exchange(part, middle, gain, heads_count)

    slope = cotangent
    gain_parts = [None] * layers
    shares, waiting = [], []
    media_slopes = ()

    def hat_slope(slopes, group, half):
        return mm(flat(slopes[2 * group + half]), scaled, NT).reshape(videos, -1, width)

    summed = []

    def scatter_rows(gradient):
        if summed:
            gradient, _ = lax.optimization_barrier((gradient, summed[-1]))
        summed.append(lax.psum_scatter(gradient, ROWS, scatter_dimension=0, tiled=True))
        return summed[-1]

    for layer in reversed(range(layers)):
        latent_in, middle, latent_norm, query, latent_pair, mixed, feed_norm, hidden_pre, hidden = kept[layer]
        query_weight, out_weight = query_full[layer], out_full[layer]
        pair_weight = pair_weights[:, 2 * layer * head_columns : 2 * (layer + 1) * head_columns]
        feed_slope = flat(feed_slope)
        hidden_slope = mm(feed_slope, narrow_full[layer], None, F32)
        _, gelu_back = jax.vjp(jax.nn.gelu, hidden_pre)
        pre_slope = gelu_back(hidden_slope)[0].astype(BF)
        part = mm(pre_slope, widen_full[layer], NT).reshape(videos, latent_count, width)
        feed_grad = product_pair(feed_slope, hidden, flat(feed_norm), pre_slope, *waiting)
        part, feed_grad = lax.optimization_barrier((part, feed_grad))
        shares.append(scatter_rows(feed_grad))
        middle_slope, feed_sums, branch_slope = backward_exchange(
            part, middle, slope, norm_gains[layer, 4:6], heads_count
        )
        branch_slope = flat(branch_slope)
        mixed_slope = mm(branch_slope, out_weight)
        out_grad = mm(branch_slope, mixed, TN)
        query_slope, latent_slopes, media_slopes, slope_sums = attend_back_fast(
            live, query, latent_pair, keys, mixed_slope, layer, scale, (media_slopes,) if layer < layers - 1 else ()
        )
        part = (mm(query_slope, query_weight, NT, F32) + mm(latent_slopes, pair_weight, NT, F32)).astype(BF)
        part = part.reshape(videos, latent_count, width)
        last = layer == 0
        if not last:
            slope, latent_sums, feed_slope = backward_exchange(
                part, latent_in, middle_slope, norm_gains[layer, 2:4], heads_count
            )
        else:
            last_part = part
            far = [hat_slope(media_slopes, 3, half) for half in range(2)]
            media_slopes, *far = lax.optimization_barrier((media_slopes, *far))
            over_x, over_y = swap_x(far[0]), swap_y(far[1])
            near = [hat_slope(media_slopes, 1, 0), hat_slope(media_slopes, 2, 1)]
            media_slopes, *near = lax.optimization_barrier((media_slopes, *near))
            in_x, in_y = [swap_x(near[0]), None], [None, swap_y(near[1])]
            near = [hat_slope(media_slopes, 1, 1), hat_slope(media_slopes, 2, 0)]
            media_slopes, *near = lax.optimization_barrier((media_slopes, *near))
        query_grad = mm(flat(latent_norm), query_slope, TN)
        pair_slope = flat(media_slopes[..., 2 * layer * head_columns : 2 * (layer + 1) * head_columns])
        hat_grad = mm(flat(media_hat), pair_slope, TN, F32)
        slope_sum = jnp.sum(slope_sums[:, 0], axis=0)
        gain, shift = norm_gains[layer, 0], norm_gains[layer, 1]
        pair_grad = (
            mm(flat(latent_norm), latent_slopes, TN, F32)
            + gain[:, None] * hat_grad
            + shift[:, None] * slope_sum[None, :]
        ).astype(BF)
        wide = pair_weight.astype(F32)
        media_sums = jnp.stack(
            (jnp.sum(wide * hat_grad, axis=1), jnp.sum(wide * slope_sum[None, :], axis=1))
        )
        parts = (query_grad, pair_grad, out_grad)
        if last:
            *parts, over_x, over_y, near[0], near[1] = lax.optimization_barrier((*parts, over_x, over_y, *near))
        waiting = parts
        gain_parts[layer] = [media_sums, None if last else latent_sums, feed_sums]

    share_out, in_x[1], in_y[0], slope, gain_parts[0][1], latent, back = last_step(
        *(parts, near, (over_x, over_y), media_slopes, scaled),
        *(last_part, final_part, final_rest, latents, middle_slope, norm_gains[0, 2:4]),
        *(heads_count, rows_count // 2),
    )
    media_slope = media_back(own, back, in_x, in_y)

    shares.append(share_out)
    gain_term = jnp.concatenate([rows for parts in gain_parts for rows in parts], axis=0).reshape(heads_count, -1, 128)
    lines = gain_term.shape[1]
    gain_term = jnp.pad(gain_term, ((0, 0), (0, 8 - lines % 8), (0, 0)))
    totals = sum_fast(gain_term, shares, lines, heads_count, rows_count, 9)
    gain_total = totals[:, :lines].reshape(layers, 6, width)
    square_total = jnp.sum(totals[0, lines]) + jnp.sum(totals[:, :lines] * totals[:, :lines])
    gradient_norm = jnp.sqrt(square_total)
    factor = CLIP_LEVEL / jnp.maximum(gradient_norm, CLIP_LEVEL)

    factor_cell = factor.reshape(1, 1)
    early_share, middle_share, late_share = shares
    depth = widen.shape[1]

    def turned(*arrays):
        return [jnp.swapaxes(rows, 1, 2)[:, None] for rows in arrays]

    def turn_back(arrays):
        return [jnp.swapaxes(rows[:, 0], 1, 2) for rows in arrays]

    inward_made, outward_made, widen_made, narrow_made = adam_fast(
        (
            (
                *(inward, inward_first, inward_second),
                [(late_share, 0), (middle_share, 0)],
                *(depth // 2, RATE_INWARD),
            ),
            (
                *turned(outward, outward_first, outward_second),
                [(late_share, 3), (middle_share, 3)],
                *(depth, RATE_OUTWARD),
            ),
            (
                *[rows[:, None] for rows in (widen, widen_first, widen_second)],
                [(middle_share, 1 + 4 * columns // units), (early_share, 1)],
                *(depth // 2, RATE_WIDEN),
            ),
            (
                *turned(narrow, narrow_first, narrow_second),
                [(middle_share, 4 * columns // units), (early_share, 0)],
                *(depth // 2, RATE_NARROW),
            ),
        ),
        factor_cell,
    )
    results = [latent, slope, media_slope, gradient_norm, *inward_made, *turn_back(outward_made)]
    results += [rows[:, 0] for rows in widen_made] + turn_back(narrow_made)
    made = adam_step(*gain_rows, gain_total.reshape(-1, width) * factor, RATE_GAINS, 0.0)
    results = results + [rows.reshape(norm_gains.shape) for rows in made] + [gain_total[:, 4:6]]
    return tuple(results)


def solution(mesh):
    placed = (
        P(HEADS, ROWS, None),
        P(ROWS, HEADS, None),
        P(ROWS),
        P(ROWS, HEADS, None),
        P(None, None, ROWS, HEADS),
        P(None, None, ROWS, HEADS),
        P(None, None, ROWS, HEADS),
        P(None, HEADS, ROWS),
        P(None, HEADS, ROWS),
        P(None, HEADS, ROWS),
        P(None, ROWS, HEADS),
        P(None, ROWS, HEADS),
        P(None, ROWS, HEADS),
        P(None, HEADS, ROWS),
        P(None, HEADS, ROWS),
        P(None, HEADS, ROWS),
        P(),
        P(),
        P(),
    )
    local = local_fast if (mesh.shape[ROWS], mesh.shape[HEADS]) == (8, 4) else local_plain
    return jax.shard_map(
        local,
        mesh=mesh,
        in_specs=placed,
        out_specs=(
            P(ROWS, HEADS, None),
            P(ROWS, HEADS, None),
            P(HEADS, ROWS, None),
            P(),
            P(None, None, ROWS, HEADS),
            P(None, None, ROWS, HEADS),
            P(None, None, ROWS, HEADS),
            P(None, None, ROWS, HEADS),
            P(None, HEADS, ROWS),
            P(None, HEADS, ROWS),
            P(None, HEADS, ROWS),
            P(None, HEADS, ROWS),
            P(None, ROWS, HEADS),
            P(None, ROWS, HEADS),
            P(None, ROWS, HEADS),
            P(None, ROWS, HEADS),
            P(None, HEADS, ROWS),
            P(None, HEADS, ROWS),
            P(None, HEADS, ROWS),
            P(None, HEADS, ROWS),
            P(),
            P(),
            P(),
            P(),
        ),
        check_vma=False,
    )
```

```python
import functools

import jax
import jax.numpy as jnp
from jax import lax
from jax.experimental import pallas as pl
from jax.experimental.pallas import tpu as pltpu
from jax.sharding import PartitionSpec as P

HD = 96
STEP = 10
PATCHES = 128


EPS_NORM = 1e-05
BETA_ONE = 0.5
BETA_TWO = 0.5
ADAM_EPS = 1e-08
WEIGHT_DECAY = 0.1
CLIP_LEVEL = 1.0
MASKED_SCORE = -1e30
RATE_INWARD = 0.02
RATE_OUTWARD = 0.5
RATE_WIDEN = 0.02
RATE_NARROW = 0.01
RATE_GAINS = 0.1


def layer_norm(rows, gain, shift):
    middle = jnp.mean(rows, axis=-1, keepdims=True)
    centred = rows - middle
    spread = jnp.mean(centred * centred, axis=-1, keepdims=True)
    return centred * lax.rsqrt(spread + EPS_NORM) * gain + shift


def norm_back(rows, gain, shift, slope):
    _, pullback = jax.vjp(layer_norm, rows, gain, shift)
    return pullback(slope)


def adam_step(weight, first, second, gradient, rate, decay):
    mean_new = BETA_ONE * first + (1.0 - BETA_ONE) * gradient
    square_new = BETA_TWO * second + (1.0 - BETA_TWO) * gradient * gradient
    mean_hat = mean_new / (1.0 - BETA_ONE**STEP)
    square_hat = square_new / (1.0 - BETA_TWO**STEP)
    weight_new = weight - rate * (mean_hat / (jnp.sqrt(square_hat) + ADAM_EPS) + decay * weight)
    return (mean_new, square_new, weight_new)


def gather_slots(rows):
    return lax.all_gather(rows, HEADS, axis=1, tiled=True)


def scatter_slots(terms):
    return lax.psum_scatter(terms, HEADS, scatter_dimension=1, tiled=True)


def gather_slopes(rows):
    return lax.all_gather(rows, HEADS, axis=1, tiled=True)


def scatter_slopes(terms):
    return lax.psum_scatter(terms, HEADS, scatter_dimension=1, tiled=True)


def both_scores(query, media_pair, latent_pair, live, scale):
    score_media = (
        jnp.einsum("vnhe,pvhe->vhnp", query, media_pair[0], preferred_element_type=jnp.float32)
        * scale
    )
    score_media = jnp.where(live[:, None, None, :], score_media, MASKED_SCORE)
    score_latent = (
        jnp.einsum("vnhe,vmhe->vhnm", query, latent_pair[0], preferred_element_type=jnp.float32)
        * scale
    )
    return (score_media, score_latent)


def attend(query, media_pair, latent_pair, live, scale):
    score_media, score_latent = both_scores(query, media_pair, latent_pair, live, scale)
    top = jnp.maximum(
        jnp.max(score_media, axis=-1, keepdims=True), jnp.max(score_latent, axis=-1, keepdims=True)
    )
    exponent_media = jnp.exp(score_media - top)
    exponent_latent = jnp.exp(score_latent - top)
    total = jnp.sum(exponent_media, axis=-1, keepdims=True) + jnp.sum(
        exponent_latent, axis=-1, keepdims=True
    )
    share_media = (exponent_media / total).astype(jnp.bfloat16)
    share_latent = (exponent_latent / total).astype(jnp.bfloat16)
    mixed = jnp.einsum(
        "vhnp,pvhe->vnhe", share_media, media_pair[1], preferred_element_type=jnp.float32
    )
    mixed = mixed + jnp.einsum(
        "vhnm,vmhe->vnhe", share_latent, latent_pair[1], preferred_element_type=jnp.float32
    )
    return (mixed.astype(jnp.bfloat16), top + jnp.log(total))


def attend_back(query, media_pair, latent_pair, live, log_total, mixed_slope, scale):
    score_media, score_latent = both_scores(query, media_pair, latent_pair, live, scale)
    share_media = jnp.exp(score_media - log_total)
    share_latent = jnp.exp(score_latent - log_total)
    share_slope_media = jnp.einsum(
        "vnhe,pvhe->vhnp", mixed_slope, media_pair[1], preferred_element_type=jnp.float32
    )
    share_slope_latent = jnp.einsum(
        "vnhe,vmhe->vhnm", mixed_slope, latent_pair[1], preferred_element_type=jnp.float32
    )
    row_total = jnp.sum(share_media * share_slope_media, axis=-1, keepdims=True)
    row_total = row_total + jnp.sum(share_latent * share_slope_latent, axis=-1, keepdims=True)
    score_slope_media = (share_media * (share_slope_media - row_total)).astype(jnp.bfloat16)
    score_slope_latent = (share_latent * (share_slope_latent - row_total)).astype(jnp.bfloat16)
    query_slope = jnp.einsum(
        "vhnp,pvhe->vnhe", score_slope_media, media_pair[0], preferred_element_type=jnp.float32
    )
    query_slope = query_slope + jnp.einsum(
        "vhnm,vmhe->vnhe", score_slope_latent, latent_pair[0], preferred_element_type=jnp.float32
    )
    query_slope = (query_slope * scale).astype(jnp.bfloat16)
    key_media = (
        jnp.einsum("vhnp,vnhe->pvhe", score_slope_media, query, preferred_element_type=jnp.float32)
        * scale
    ).astype(jnp.bfloat16)
    value_media = jnp.einsum(
        "vhnp,vnhe->pvhe",
        share_media.astype(jnp.bfloat16),
        mixed_slope,
        preferred_element_type=jnp.float32,
    ).astype(jnp.bfloat16)
    key_latent = (
        jnp.einsum("vhnm,vnhe->vmhe", score_slope_latent, query, preferred_element_type=jnp.float32)
        * scale
    ).astype(jnp.bfloat16)
    value_latent = jnp.einsum(
        "vhnm,vnhe->vmhe",
        share_latent.astype(jnp.bfloat16),
        mixed_slope,
        preferred_element_type=jnp.float32,
    ).astype(jnp.bfloat16)
    return (query_slope, jnp.stack((key_media, value_media)), jnp.stack((key_latent, value_latent)))


def local_plain(
    media,
    latents,
    frame_count,
    cotangent,
    inward,
    inward_first,
    inward_second,
    outward,
    outward_first,
    outward_second,
    widen,
    widen_first,
    widen_second,
    narrow,
    narrow_first,
    narrow_second,
    norm_gains,
    gain_first,
    gain_second,
):
    heads_count = lax.axis_size(HEADS)
    layers, _, row_share, head_columns = inward.shape
    local_positions, videos, width = media.shape
    positions = local_positions * heads_count
    latent_count = latents.shape[1] * heads_count
    local_heads = head_columns // HD
    scale = HD ** (-0.5)
    live = (jnp.arange(positions, dtype=jnp.int32) // PATCHES)[None, :] < frame_count[:, None]
    inward_columns, outward_rows, widen_columns, narrow_rows = (
        lax.all_gather(inward.astype(jnp.bfloat16), ROWS, axis=2, tiled=True),
        lax.all_gather(outward.astype(jnp.bfloat16), ROWS, axis=2, tiled=True),
        lax.all_gather(widen.astype(jnp.bfloat16), ROWS, axis=1, tiled=True),
        lax.all_gather(narrow.astype(jnp.bfloat16), ROWS, axis=2, tiled=True),
    )
    media_rows = media.astype(jnp.float32)
    latent = latents
    kept = []
    for layer in range(layers):
        gains = norm_gains[layer]
        media_norm = layer_norm(media_rows, gains[0], gains[1]).astype(jnp.bfloat16)
        latent_norm = gather_slots(layer_norm(latent, gains[2], gains[3]).astype(jnp.bfloat16))
        triple = jnp.einsum(
            "vnd,tdc->tvnc", latent_norm, inward_columns[layer], preferred_element_type=jnp.float32
        ).astype(jnp.bfloat16)
        pair_columns = inward_columns[layer, 1:3]
        media_pair = jnp.einsum(
            "pvd,tdc->tpvc",
            lax.all_gather(media_norm, HEADS, axis=0, tiled=True),
            pair_columns,
            preferred_element_type=jnp.float32,
        ).astype(jnp.bfloat16)
        query = triple[0].reshape(videos, latent_count, local_heads, HD)
        latent_pair = triple[1:3].reshape(2, videos, latent_count, local_heads, HD)
        heads_pair = media_pair.reshape(2, positions, videos, local_heads, HD)
        mixed, log_total = attend(query, heads_pair, latent_pair, live, scale)
        mixed = mixed.reshape(videos, latent_count, head_columns)
        middle = latent + scatter_slots(
            jnp.einsum(
                "vnc,cd->vnd", mixed, outward_rows[layer], preferred_element_type=jnp.float32
            )
        )
        feed_norm = gather_slots(layer_norm(middle, gains[4], gains[5]).astype(jnp.bfloat16))
        hidden_pre = jnp.einsum(
            "vnd,df->vnf", feed_norm, widen_columns[layer], preferred_element_type=jnp.float32
        )
        hidden = jax.nn.gelu(hidden_pre).astype(jnp.bfloat16)
        kept.append(
            (
                latent,
                middle,
                media_norm,
                latent_norm,
                query,
                heads_pair,
                latent_pair,
                mixed,
                log_total,
                feed_norm,
                hidden_pre,
                hidden,
            )
        )
        latent = middle + scatter_slots(
            jnp.einsum(
                "vnf,fd->vnd", hidden, narrow_rows[layer], preferred_element_type=jnp.float32
            )
        )
    slope = cotangent
    media_slope = jnp.zeros(media_rows.shape, jnp.float32)
    inward_parts, outward_parts, widen_parts, narrow_parts, gain_parts = ([], [], [], [], [])
    for layer in reversed(range(layers)):
        (
            latent_in,
            middle,
            media_norm,
            latent_norm,
            query,
            heads_pair,
            latent_pair,
            mixed,
            log_total,
            feed_norm,
            hidden_pre,
            hidden,
        ) = kept[layer]
        gains = norm_gains[layer]
        feed_slope = gather_slopes(slope.astype(jnp.bfloat16))
        narrow_grad = jnp.einsum(
            "vnf,vnd->fd", hidden, feed_slope, preferred_element_type=jnp.float32
        )
        hidden_slope = jnp.einsum(
            "vnd,fd->vnf", feed_slope, narrow_rows[layer], preferred_element_type=jnp.float32
        )
        _, gelu_back = jax.vjp(jax.nn.gelu, hidden_pre)
        pre_slope = gelu_back(hidden_slope)[0].astype(jnp.bfloat16)
        widen_grad = jnp.einsum(
            "vnd,vnf->df", feed_norm, pre_slope, preferred_element_type=jnp.float32
        )
        norm_slope = scatter_slopes(
            jnp.einsum(
                "vnf,df->vnd", pre_slope, widen_columns[layer], preferred_element_type=jnp.float32
            )
        )
        middle_part, gain_feed, shift_feed = norm_back(middle, gains[4], gains[5], norm_slope)
        middle_slope = slope + middle_part
        branch_slope = gather_slopes(middle_slope.astype(jnp.bfloat16))
        outward_grad = jnp.einsum(
            "vnc,vnd->cd", mixed, branch_slope, preferred_element_type=jnp.float32
        )
        mixed_slope = jnp.einsum(
            "vnd,cd->vnc", branch_slope, outward_rows[layer], preferred_element_type=jnp.float32
        ).astype(jnp.bfloat16)
        mixed_slope = mixed_slope.reshape(videos, latent_count, local_heads, HD)
        query_slope, media_slopes, latent_slopes = attend_back(
            query, heads_pair, latent_pair, live, log_total, mixed_slope, scale
        )
        triple_slope = jnp.concatenate(
            (
                query_slope.reshape(1, videos, latent_count, head_columns),
                latent_slopes.reshape(2, videos, latent_count, head_columns),
            ),
            axis=0,
        )
        inward_grad = jnp.einsum(
            "vnd,tvnc->tdc", latent_norm, triple_slope, preferred_element_type=jnp.float32
        )
        norm_slope = scatter_slopes(
            jnp.einsum(
                "tvnc,tdc->vnd",
                triple_slope,
                inward_columns[layer],
                preferred_element_type=jnp.float32,
            )
        )
        latent_part, gain_latent, shift_latent = norm_back(
            latent_in, gains[2], gains[3], norm_slope
        )
        slope = middle_slope + latent_part
        pair_slope = media_slopes.reshape(2, positions, videos, head_columns)
        media_columns = jnp.einsum(
            "pvd,tpvc->tdc",
            lax.all_gather(media_norm, HEADS, axis=0, tiled=True),
            pair_slope,
            preferred_element_type=jnp.float32,
        )
        inward_grad = jnp.concatenate((inward_grad[:1], inward_grad[1:] + media_columns), axis=0)
        pair_columns = inward_columns[layer, 1:3]
        media_norm_slope = lax.psum_scatter(
            jnp.einsum(
                "tpvc,tdc->pvd", pair_slope, pair_columns, preferred_element_type=jnp.float32
            ),
            HEADS,
            scatter_dimension=0,
            tiled=True,
        )
        media_part, gain_media, shift_media = norm_back(
            media_rows, gains[0], gains[1], media_norm_slope
        )
        media_slope = media_slope + media_part
        inward_parts.append(inward_grad)
        outward_parts.append(outward_grad)
        widen_parts.append(widen_grad)
        narrow_parts.append(narrow_grad)
        gain_parts.append(
            jnp.stack((gain_media, shift_media, gain_latent, shift_latent, gain_feed, shift_feed))
        )
    inward_grad, outward_grad, widen_grad, narrow_grad = (
        lax.psum_scatter(jnp.stack(inward_parts[::-1]), ROWS, scatter_dimension=2, tiled=True),
        lax.psum_scatter(jnp.stack(outward_parts[::-1]), ROWS, scatter_dimension=2, tiled=True),
        lax.psum_scatter(jnp.stack(widen_parts[::-1]), ROWS, scatter_dimension=1, tiled=True),
        lax.psum_scatter(jnp.stack(narrow_parts[::-1]), ROWS, scatter_dimension=2, tiled=True),
    )
    squares = jnp.sum(inward_grad * inward_grad) + jnp.sum(outward_grad * outward_grad)
    squares = squares + jnp.sum(widen_grad * widen_grad) + jnp.sum(narrow_grad * narrow_grad)
    gain_total, square_total = lax.psum((jnp.stack(gain_parts[::-1]), squares), (ROWS, HEADS))
    gradient_norm = jnp.sqrt(square_total + jnp.sum(gain_total * gain_total))
    factor = CLIP_LEVEL / jnp.maximum(gradient_norm, CLIP_LEVEL)
    table = (
        (inward, inward_first, inward_second, inward_grad, RATE_INWARD, WEIGHT_DECAY),
        (outward, outward_first, outward_second, outward_grad, RATE_OUTWARD, WEIGHT_DECAY),
        (widen, widen_first, widen_second, widen_grad, RATE_WIDEN, WEIGHT_DECAY),
        (narrow, narrow_first, narrow_second, narrow_grad, RATE_NARROW, WEIGHT_DECAY),
    )
    results = [latent, slope, media_slope, gradient_norm]
    for weight, first, second, gradient, rate, decay in table:
        mean_new, square_new, weight_new = adam_step(
            weight, first, second, gradient * factor, rate, decay
        )
        results = results + [mean_new, square_new, weight_new, weight_new.astype(jnp.bfloat16)]
    mean_new, square_new, weight_new = adam_step(
        norm_gains, gain_first, gain_second, gain_total * factor, RATE_GAINS, 0.0
    )
    results = results + [mean_new, square_new, weight_new, gain_total[:, 4:6]]
    return tuple(results)


BF = jnp.bfloat16
F32 = jnp.float32
MIB = 1024 * 1024
HEADS, ROWS = "heads", "rows"
NT = (((1,), (1,)), ((), ()))
TN = (((0,), (0,)), ((), ()))
X_SWAP = ((0, 1), (1, 0), (2, 3), (3, 2))
Y_SWAP = ((0, 2), (2, 0), (1, 3), (3, 1))
FAR_SWAP = ((0, 3), (3, 0), (1, 2), (2, 1))


def vmem_spec():
    return pl.BlockSpec(memory_space=pltpu.VMEM)


def mm(left, right, dims=None, out=BF):
    dims = dims or (((1,), (0,)), ((), ()))
    return lax.dot_general(left, right, dims, preferred_element_type=F32).astype(out)


def greet(count):
    me = lax.axis_index(HEADS)
    barrier = pltpu.get_barrier_semaphore()
    for step in range(1, count):
        pl.semaphore_signal(barrier, inc=1, device_id={HEADS: (me + step) % count})
    pl.semaphore_wait(barrier, count - 1)
    return me


def own_rows(ref, place, share):
    return ref.at[:, pl.ds(pl.multiple_of(place * share, share), share), :]


def start_gather(me, count, share, own_ref, full_ref, send_sem, recv_sem):
    copies = []
    for step in range(1, count):
        copy = pltpu.make_async_remote_copy(
            src_ref=own_ref,
            dst_ref=own_rows(full_ref, me, share),
            send_sem=send_sem.at[step - 1],
            recv_sem=recv_sem.at[step - 1],
            device_id={HEADS: (me + step) % count},
        )
        copy.start()
        copies.append(copy)
    return copies


def beside(me):
    return me + 1 - 2 * (me % 2), me + 2 - 4 * (me // 2)


def gather_kernel(count, own_ref, norm_ref, near_ref, full_ref, send_sem, recv_sem, norm_send, norm_recv):
    me = greet(count)
    beside_x, beside_y = beside(me)
    share = norm_ref.shape[1]
    copies = start_gather(me, count, share, norm_ref, full_ref, norm_send, norm_recv)
    for at, (half, slot, peer) in enumerate(
        ((1, 1, beside_x), (0, 2, beside_y), (0, 0, beside_x), (1, 3, beside_y))
    ):
        copy = pltpu.make_async_remote_copy(
            src_ref=own_ref.at[half],
            dst_ref=near_ref.at[slot],
            send_sem=send_sem.at[at],
            recv_sem=recv_sem.at[at],
            device_id={HEADS: peer},
        )
        copy.start()
        copies.append(copy)
    full_ref[:, pl.ds(pl.multiple_of(me * share, share), share), :] = norm_ref[...]
    for copy in copies:
        copy.wait()


def gather_near(own, norm, count):
    videos, share, width = norm.shape
    any_spec = pl.BlockSpec(memory_space=pl.ANY)
    return pl.pallas_call(
        functools.partial(gather_kernel, count),
        out_shape=(
            jax.ShapeDtypeStruct((4, *own.shape[1:]), BF),
            jax.ShapeDtypeStruct((videos, share * count, width), BF),
        ),
        in_specs=[any_spec, vmem_spec()],
        out_specs=(any_spec, vmem_spec()),
        scratch_shapes=[pltpu.SemaphoreType.DMA((4,))] * 2 + [pltpu.SemaphoreType.DMA((count - 1,))] * 2,
        compiler_params=pltpu.CompilerParams(
            collective_id=1, has_side_effects=True, vmem_limit_bytes=60 * MIB
        ),
        cost_estimate=pl.CostEstimate(flops=0, bytes_accessed=250 * 1000 * 1000, transcendentals=0),
        name="gather_near",
    )(own, norm)


def media_rows(half, layer, chunk_ref, gain_ref, weight_ref, keys_ref, hat_ref, rows_ref, other_ref=None):
    @pl.when(layer == 0)
    def _():
        if other_ref is None:
            rows_ref[...] = chunk_ref[0].astype(F32).reshape(rows_ref.shape)
        else:

            @pl.when(half < 2)
            def _():
                rows_ref[...] = chunk_ref[0].astype(F32).reshape(rows_ref.shape)

            @pl.when(half >= 2)
            def _():
                rows_ref[...] = other_ref[0].astype(F32).reshape(rows_ref.shape)

        rows = rows_ref[...]
        centred = rows - jnp.mean(rows, axis=-1, keepdims=True)
        spread = jnp.mean(centred * centred, axis=-1, keepdims=True)
        hat = centred * lax.rsqrt(spread + EPS_NORM)
        rows_ref[...] = hat
        hat_ref[...] = hat.astype(BF).reshape(hat_ref.shape)

    gain = gain_ref[pl.ds(layer, 1), 0]
    shift = gain_ref[pl.ds(layer, 1), 1]
    normed = (rows_ref[...] * gain + shift).astype(BF)
    keys_ref[...] = jnp.dot(normed, weight_ref[...], preferred_element_type=F32).astype(BF).reshape(keys_ref.shape)


def near_kernel(
    count, own_ref, near_ref, gain_ref, weight_ref, source_ref, keys_ref, hat_ref, far_ref, rows_ref, send_sem, recv_sem
):
    half, layer = pl.program_id(0), pl.program_id(1)
    me = lax.axis_index(HEADS)
    beside_x, beside_y = beside(me)

    def relays():
        return [
            pltpu.make_async_remote_copy(
                src_ref=source_ref.at[slot],
                dst_ref=far_ref.at[at],
                send_sem=send_sem.at[at],
                recv_sem=recv_sem.at[at],
                device_id={HEADS: peer},
            )
            for at, (slot, peer) in enumerate(((2, beside_x), (1, beside_y)))
        ]

    @pl.when((half == 0) & (layer == 0))
    def _():
        barrier = pltpu.get_barrier_semaphore()
        for peer in (beside_x, beside_y):
            pl.semaphore_signal(barrier, inc=1, device_id={HEADS: peer})
        pl.semaphore_wait(barrier, 2)
        for copy in relays():
            copy.start()

    media_rows(half, layer, own_ref, gain_ref, weight_ref, keys_ref, hat_ref, rows_ref, near_ref)

    @pl.when((half == 5) & (layer == 1))
    def _():
        for copy in relays():
            copy.wait()


def media_near(own, near, gains, weight, columns, count):
    _, videos, patches, width = own.shape
    rows = videos * patches
    any_spec = pl.BlockSpec(memory_space=pl.ANY)
    return pl.pallas_call(
        functools.partial(near_kernel, count),
        grid=(6, 2),
        out_shape=(
            jax.ShapeDtypeStruct((8, videos, patches, columns), BF),
            jax.ShapeDtypeStruct((8, videos, patches, width), BF),
            jax.ShapeDtypeStruct(own.shape, BF),
        ),
        in_specs=[
            pl.BlockSpec((1, videos, patches, width), lambda i, j: (jnp.minimum(i, 1), 0, 0, 0)),
            pl.BlockSpec((1, videos, patches, width), lambda i, j: (jnp.maximum(i - 2, 0), 0, 0, 0)),
            pl.BlockSpec(gains.shape, lambda i, j: (0, 0, 0)),
            pl.BlockSpec((width, columns // 2), lambda i, j: (0, j)),
            any_spec,
        ],
        out_specs=(
            pl.BlockSpec((1, videos, patches, columns // 2), lambda i, j: (i, 0, 0, j)),
            pl.BlockSpec((1, videos, patches, width), lambda i, j: (i, 0, 0, 0)),
            any_spec,
        ),
        scratch_shapes=[
            pltpu.VMEM((rows, width), F32),
            pltpu.SemaphoreType.DMA((2,)),
            pltpu.SemaphoreType.DMA((2,)),
        ],
        compiler_params=pltpu.CompilerParams(
            collective_id=6, has_side_effects=True, vmem_limit_bytes=60 * MIB
        ),
        cost_estimate=pl.CostEstimate(
            flops=12 * rows * width * columns, bytes_accessed=24 * rows * width, transcendentals=0
        ),
        name="media_near",
    )(own, near, gains, weight, near)


def far_kernel(
    count, chunk_ref, gain_ref, weight_ref, slope_ref, keys_in, hat_in, keys_ref, hat_ref, full_ref, rows_ref, *sems
):
    half, layer = pl.program_id(0), pl.program_id(1)
    send_sem, recv_sem, own_sem = sems
    me = lax.axis_index(HEADS)
    share = slope_ref.shape[1]

    def copies():
        return [
            pltpu.make_async_remote_copy(
                src_ref=slope_ref,
                dst_ref=own_rows(full_ref, me, share),
                send_sem=send_sem.at[step - 1],
                recv_sem=recv_sem.at[step - 1],
                device_id={HEADS: (me + step) % count},
            )
            for step in range(1, count)
        ] + [pltpu.make_async_copy(slope_ref, own_rows(full_ref, me, share), own_sem)]

    @pl.when((half == 0) & (layer == 0))
    def _():
        greet(count)
        for copy in copies():
            copy.start()

    media_rows(half, layer, chunk_ref, gain_ref, weight_ref, keys_ref, hat_ref, rows_ref)

    @pl.when((half == 1) & (layer == 1))
    def _():
        for copy in copies():
            copy.wait()


def media_far(far, gains, weight, slope, keys, hat, count):
    _, videos, patches, width = far.shape
    columns = keys.shape[3]
    rows = videos * patches
    share = slope.shape[1]
    any_spec = pl.BlockSpec(memory_space=pl.ANY)
    return pl.pallas_call(
        functools.partial(far_kernel, count),
        grid=(2, 2),
        out_shape=(
            jax.ShapeDtypeStruct(keys.shape, BF),
            jax.ShapeDtypeStruct(hat.shape, BF),
            jax.ShapeDtypeStruct((videos, share * count, width), BF),
        ),
        in_specs=[
            pl.BlockSpec((1, videos, patches, width), lambda i, j: (i, 0, 0, 0)),
            pl.BlockSpec(gains.shape, lambda i, j: (0, 0, 0)),
            pl.BlockSpec((width, columns // 2), lambda i, j: (0, j)),
            any_spec,
            any_spec,
            any_spec,
        ],
        out_specs=(
            pl.BlockSpec((1, videos, patches, columns // 2), lambda i, j: (6 + i, 0, 0, j)),
            pl.BlockSpec((1, videos, patches, width), lambda i, j: (6 + i, 0, 0, 0)),
            any_spec,
        ),
        scratch_shapes=[
            pltpu.VMEM((rows, width), F32),
            pltpu.SemaphoreType.DMA((count - 1,)),
            pltpu.SemaphoreType.DMA((count - 1,)),
            pltpu.SemaphoreType.DMA,
        ],
        input_output_aliases={4: 0, 5: 1},
        compiler_params=pltpu.CompilerParams(
            collective_id=8, has_side_effects=True, vmem_limit_bytes=60 * MIB
        ),
        cost_estimate=pl.CostEstimate(
            flops=4 * rows * width * columns, bytes_accessed=8 * rows * width, transcendentals=0
        ),
        name="media_far",
    )(far, gains, weight, slope, keys, hat)


def head_mask(rows, columns, head):
    place = lax.broadcasted_iota(jnp.int32, (rows, columns), 1)
    return (place >= head * HD) & (place < (head + 1) * HD)


def spread_heads(rows):
    heads = rows.shape[1] // HD
    zero = jnp.zeros_like(rows)
    return jnp.concatenate(
        [jnp.where(head_mask(*rows.shape, head), rows, zero) for head in range(heads)], axis=0
    )


def gather_heads(rows, count):
    heads = rows.shape[1] // HD
    total = jnp.zeros((count, rows.shape[1]), F32)
    for head in range(heads):
        part = rows[head * count : (head + 1) * count]
        total = total + jnp.where(head_mask(*part.shape, head), part, 0.0)
    return total


def attend_kernel(live_ref, query_ref, latent_key_ref, latent_value_ref, key_ref, value_ref, mixed_ref, *, scale):
    video = pl.program_id(0)
    slots, patches = key_ref.shape[0], key_ref.shape[2]
    query = spread_heads(query_ref[...])
    rows, columns = query.shape
    place = lax.broadcasted_iota(jnp.int32, (rows, 2 * patches), 1)
    scores = []
    for pair in range(slots // 2):
        keys = key_ref[2 * pair : 2 * pair + 2, 0].reshape(2 * patches, columns)
        score = lax.dot_general(query, keys, NT, preferred_element_type=F32) * scale
        live = jnp.where(place < patches, live_ref[video, 2 * pair], live_ref[video, 2 * pair + 1])
        scores.append(jnp.where(live > 0, score, MASKED_SCORE))
    scores.append(lax.dot_general(query, latent_key_ref[...], NT, preferred_element_type=F32) * scale)
    top = functools.reduce(jnp.maximum, [jnp.max(score, axis=-1, keepdims=True) for score in scores])
    exponents = [jnp.exp(score - top) for score in scores]
    total = functools.reduce(jnp.add, [jnp.sum(e, axis=-1, keepdims=True) for e in exponents])
    mixed = jnp.zeros((rows, columns), F32)
    for pair in range(slots // 2):
        values = value_ref[2 * pair : 2 * pair + 2, 0].reshape(2 * patches, columns)
        mixed = mixed + jnp.dot((exponents[pair] / total).astype(BF), values, preferred_element_type=F32)
    mixed = mixed + jnp.dot(
        (exponents[-1] / total).astype(BF), latent_value_ref[...], preferred_element_type=F32
    )
    mixed_ref[...] = gather_heads(mixed, query_ref.shape[0]).astype(BF)


def attend_fast(live, query, latent_pair, keys, layer, scale):
    slots, videos, patches, _ = keys.shape
    count, columns = query.shape[0] // videos, query.shape[1]
    row_block = pl.BlockSpec((count, columns), lambda v: (v, 0))
    return pl.pallas_call(
        functools.partial(attend_kernel, scale=scale),
        grid=(videos,),
        out_shape=jax.ShapeDtypeStruct(query.shape, BF),
        in_specs=[
            pl.BlockSpec(memory_space=pltpu.SMEM),
            row_block,
            row_block,
            pl.BlockSpec((count, columns), lambda v: (v, 1)),
            pl.BlockSpec((slots, 1, patches, columns), lambda v: (0, v, 0, 2 * layer)),
            pl.BlockSpec((slots, 1, patches, columns), lambda v: (0, v, 0, 2 * layer + 1)),
        ],
        out_specs=row_block,
        compiler_params=pltpu.CompilerParams(vmem_limit_bytes=28 * MIB),
        cost_estimate=pl.CostEstimate(
            flops=8 * slots * patches * videos * count * 2 * columns,
            bytes_accessed=4 * slots * videos * patches * columns,
            transcendentals=slots * patches * videos * count * 4,
        ),
        name="attend",
    )(live, query, latent_pair, latent_pair, keys, keys)


def attend_back_kernel(
    live_ref, query_ref, latent_key_ref, latent_value_ref, key_ref, value_ref, slope_ref, *rest, scale
):
    query_slope_ref, latent_slope_ref, media_slope_ref, sums_ref = rest[-4:]
    video = pl.program_id(0)
    slots, patches = key_ref.shape[0], key_ref.shape[2]
    pairs = slots // 2
    count = query_ref.shape[0]
    query, slope = spread_heads(query_ref[...]), spread_heads(slope_ref[...])
    rows, columns = query.shape
    place = lax.broadcasted_iota(jnp.int32, (2 * patches, rows), 0)

    def keys_of(ref, pair):
        return ref[2 * pair : 2 * pair + 2, 0].reshape(2 * patches, columns)

    scores = []
    for pair in range(pairs):
        score = lax.dot_general(keys_of(key_ref, pair), query, NT, preferred_element_type=F32) * scale
        live = jnp.where(place < patches, live_ref[video, 2 * pair], live_ref[video, 2 * pair + 1])
        scores.append(jnp.where(live > 0, score, MASKED_SCORE))
    scores.append(lax.dot_general(latent_key_ref[...], query, NT, preferred_element_type=F32) * scale)
    top = functools.reduce(jnp.maximum, [jnp.max(score, axis=0, keepdims=True) for score in scores])
    exponents = [jnp.exp(score - top) for score in scores]
    total = functools.reduce(jnp.add, [jnp.sum(e, axis=0, keepdims=True) for e in exponents])
    shares = [e / total for e in exponents]
    share_slopes = [
        lax.dot_general(keys_of(value_ref, pair), slope, NT, preferred_element_type=F32)
        for pair in range(pairs)
    ]
    share_slopes.append(
        lax.dot_general(latent_value_ref[...], slope, NT, preferred_element_type=F32)
    )
    row_total = functools.reduce(
        jnp.add,
        [jnp.sum(a * b, axis=0, keepdims=True) for a, b in zip(shares, share_slopes)],
    )
    query_slope = jnp.zeros((rows, columns), F32)
    key_sum, value_sum = jnp.zeros((1, columns), F32), jnp.zeros((1, columns), F32)
    for at in range(pairs + 1):
        keys = keys_of(key_ref, at) if at < pairs else latent_key_ref[...]
        score_slope = (shares[at] * (share_slopes[at] - row_total)).astype(BF)
        key_slope = (jnp.dot(score_slope, query, preferred_element_type=F32) * scale).astype(BF)
        value_slope = jnp.dot(shares[at].astype(BF), slope, preferred_element_type=F32).astype(BF)
        query_slope = query_slope + lax.dot_general(
            score_slope, keys, TN, preferred_element_type=F32
        )
        if at < pairs:
            key_sum = key_sum + jnp.sum(key_slope.astype(F32), axis=0, keepdims=True)
            value_sum = value_sum + jnp.sum(value_slope.astype(F32), axis=0, keepdims=True)
            media_slope_ref[2 * at : 2 * at + 2, 0, :, :columns] = key_slope.reshape(2, patches, columns)
            media_slope_ref[2 * at : 2 * at + 2, 0, :, columns:] = value_slope.reshape(2, patches, columns)
        else:
            latent_slope_ref[:, :columns] = key_slope
            latent_slope_ref[:, columns:] = value_slope
    sums_ref[0, :, :columns] = key_sum
    sums_ref[0, :, columns:] = value_sum
    query_slope_ref[...] = (gather_heads(query_slope, count) * scale).astype(BF)


def attend_back_fast(live, query, latent_pair, keys, slope, layer, scale, earlier):
    slots, videos, patches, _ = keys.shape
    count, columns = query.shape[0] // videos, query.shape[1]
    row_block = pl.BlockSpec((count, columns), lambda v: (v, 0))
    in_specs = [
        pl.BlockSpec(memory_space=pltpu.SMEM),
        row_block,
        row_block,
        pl.BlockSpec((count, columns), lambda v: (v, 1)),
        pl.BlockSpec((slots, 1, patches, columns), lambda v: (0, v, 0, 2 * layer)),
        pl.BlockSpec((slots, 1, patches, columns), lambda v: (0, v, 0, 2 * layer + 1)),
        row_block,
    ]
    aliases = {}
    if earlier:
        in_specs += [pl.BlockSpec(memory_space=pl.ANY)]
        aliases = {7: 2}
    return pl.pallas_call(
        functools.partial(attend_back_kernel, scale=scale),
        grid=(videos,),
        out_shape=(
            jax.ShapeDtypeStruct(query.shape, BF),
            jax.ShapeDtypeStruct(latent_pair.shape, BF),
            jax.ShapeDtypeStruct(keys.shape, BF),
            jax.ShapeDtypeStruct((videos, 1, 2 * columns), F32),
        ),
        in_specs=in_specs,
        out_specs=(
            row_block,
            pl.BlockSpec((count, 2 * columns), lambda v: (v, 0)),
            pl.BlockSpec((slots, 1, patches, 2 * columns), lambda v: (0, v, 0, layer)),
            pl.BlockSpec((1, 1, 2 * columns), lambda v: (v, 0, 0)),
        ),
        input_output_aliases=aliases,
        compiler_params=pltpu.CompilerParams(vmem_limit_bytes=60 * MIB),
        cost_estimate=pl.CostEstimate(
            flops=20 * slots * patches * videos * count * 2 * columns,
            bytes_accessed=8 * slots * videos * patches * columns,
            transcendentals=slots * patches * videos * count * 4,
        ),
        name="attend_back",
    )(live, query, latent_pair, latent_pair, keys, keys, slope, *earlier)


def product_pair_kernel(first_ref, second_ref, third_ref, fourth_ref, *rest):
    out_ref, at = rest[-1], 0
    for ref in rest[:-1]:
        out_ref[:, at : at + ref.shape[1]] = ref[...]
        at += ref.shape[1]
    units = second_ref.shape[1]
    out_ref[:, at : at + units] = mm(first_ref[...], second_ref[...], TN)
    out_ref[:, at + units :] = mm(third_ref[...], fourth_ref[...], TN)


def product_pair(first, second, third, fourth, *extra):
    rows, width, columns = first.shape[0], first.shape[1], second.shape[1]
    cut = width // 6
    total = sum(piece.shape[1] for piece in extra) + 2 * columns
    left = pl.BlockSpec((rows, cut), lambda i: (0, i))
    whole = pl.BlockSpec((rows, columns), lambda i: (0, 0))
    return pl.pallas_call(
        product_pair_kernel,
        grid=(6,),
        out_shape=jax.ShapeDtypeStruct((width, total), BF),
        in_specs=[left, whole, left, whole]
        + [pl.BlockSpec((cut, piece.shape[1]), lambda i: (i, 0)) for piece in extra],
        out_specs=pl.BlockSpec((cut, total), lambda i: (i, 0)),
        compiler_params=pltpu.CompilerParams(vmem_limit_bytes=60 * MIB),
        cost_estimate=pl.CostEstimate(
            flops=4 * rows * width * columns, bytes_accessed=8 * width * columns, transcendentals=0
        ),
        name="feed_gradients",
    )(first, second, third, fourth, *extra)


def start_scatter(me, count, share, part_ref, landed_ref, send_sem, recv_sem):
    copies = []
    for step in range(1, count):
        peer = (me + step) % count
        copy = pltpu.make_async_remote_copy(
            src_ref=own_rows(part_ref, peer, share),
            dst_ref=landed_ref.at[step - 1],
            send_sem=send_sem.at[step - 1],
            recv_sem=recv_sem.at[step - 1],
            device_id={HEADS: peer},
        )
        copy.start()
        copies.append(copy)
    return copies


def forward_kernel(
    count, last, part_ref, rest_ref, gain_ref, new_ref, *refs
):
    refs = list(refs)
    full_ref = None if last else refs.pop(0)
    landed_ref, own_ref, send_sem, recv_sem, send_more, recv_more = refs
    me = greet(count)
    share = rest_ref.shape[1]
    copies = start_scatter(me, count, share, part_ref, landed_ref, send_sem, recv_sem)
    mine = pl.ds(pl.multiple_of(me * share, share), share)
    total = rest_ref[...] + part_ref[:, mine, :].astype(F32)
    for step, copy in enumerate(copies):
        copy.wait_recv()
        total = total + landed_ref[step].astype(F32)
    new_ref[...] = total
    if not last:
        own_ref[...] = layer_norm(total, gain_ref[0], gain_ref[1]).astype(BF)
        more = start_gather(me, count, share, own_ref, full_ref, send_more, recv_more)
        full_ref[:, mine, :] = own_ref[...]
        for copy in more:
            copy.wait()
    for copy in copies:
        copy.wait_send()


def forward_exchange(part, rest, gain, count, last=False):
    videos, share, width = rest.shape
    outs = [jax.ShapeDtypeStruct(rest.shape, F32)]
    if not last:
        outs.append(jax.ShapeDtypeStruct(part.shape, BF))
    got = pl.pallas_call(
        functools.partial(forward_kernel, count, last),
        out_shape=tuple(outs),
        in_specs=[vmem_spec()] * 3,
        out_specs=(vmem_spec(),) * len(outs),
        scratch_shapes=[
            pltpu.VMEM((count - 1, videos, share, width), BF),
            pltpu.VMEM((videos, share, width), BF),
        ]
        + [pltpu.SemaphoreType.DMA((count - 1,))] * 4,
        compiler_params=pltpu.CompilerParams(
            collective_id=3 if last else 2, has_side_effects=True, vmem_limit_bytes=14 * MIB
        ),
        cost_estimate=pl.CostEstimate(flops=0, bytes_accessed=75 * 1000 * 1000, transcendentals=0),
        name="forward_exchange",
    )(part, rest, gain)
    return got if not last else (got[0], None)


def backward_kernel(
    count, last, part_ref, rows_ref, rest_ref, gain_ref, new_ref, sums_ref, *refs
):
    refs = list(refs)
    full_ref = None if last else refs.pop(0)
    landed_ref, own_ref, send_sem, recv_sem, send_more, recv_more = refs
    me = greet(count)
    share = rest_ref.shape[1]
    copies = start_scatter(me, count, share, part_ref, landed_ref, send_sem, recv_sem)
    mine = pl.ds(pl.multiple_of(me * share, share), share)
    rows = rows_ref[...]
    centred = rows - jnp.mean(rows, axis=-1, keepdims=True)
    scale = lax.rsqrt(jnp.mean(centred * centred, axis=-1, keepdims=True) + EPS_NORM)
    hat = centred * scale
    slope = part_ref[:, mine, :].astype(F32)
    for step, copy in enumerate(copies):
        copy.wait_recv()
        slope = slope + landed_ref[step].astype(F32)
    hat_slope = slope * gain_ref[0]
    back = hat_slope - jnp.mean(hat_slope, axis=-1, keepdims=True)
    back = back - hat * jnp.mean(hat_slope * hat, axis=-1, keepdims=True)
    new = rest_ref[...] + back * scale
    new_ref[...] = new
    if not last:
        own_ref[...] = new.astype(BF)
        more = start_gather(me, count, share, own_ref, full_ref, send_more, recv_more)
        full_ref[:, mine, :] = own_ref[...]
    sums_ref[0:1] = jnp.sum(jnp.sum(slope * hat, axis=0), axis=0, keepdims=True)
    sums_ref[1:2] = jnp.sum(jnp.sum(slope, axis=0), axis=0, keepdims=True)
    if not last:
        for copy in more:
            copy.wait()
    for copy in copies:
        copy.wait_send()


def backward_exchange(part, rows, rest, gain, count, last=False):
    videos, share, width = rest.shape
    outs = [jax.ShapeDtypeStruct(rest.shape, F32), jax.ShapeDtypeStruct((2, width), F32)]
    if not last:
        outs.append(jax.ShapeDtypeStruct(part.shape, BF))
    got = pl.pallas_call(
        functools.partial(backward_kernel, count, last),
        out_shape=tuple(outs),
        in_specs=[vmem_spec()] * 4,
        out_specs=(vmem_spec(),) * len(outs),
        scratch_shapes=[
            pltpu.VMEM((count - 1, videos, share, width), BF),
            pltpu.VMEM((videos, share, width), BF),
        ]
        + [pltpu.SemaphoreType.DMA((count - 1,))] * 4,
        compiler_params=pltpu.CompilerParams(
            collective_id=5 if last else 4, has_side_effects=True, vmem_limit_bytes=14 * MIB
        ),
        cost_estimate=pl.CostEstimate(flops=0, bytes_accessed=75 * 1000 * 1000, transcendentals=0),
        name="backward_exchange",
    )(part, rows, rest, gain)
    return got if not last else (*got, None)


def sum_kernel(heads, rows, lines, term_in, *refs):
    shares, (out_ref, term_ref, plane_ref, line_ref, part_ref), sems = refs[:3], refs[3:8], refs[8:]
    me_head, me_row = lax.axis_index(HEADS), lax.axis_index(ROWS)
    barrier = pltpu.get_barrier_semaphore()
    for step in range(1, heads):
        pl.semaphore_signal(barrier, inc=1, device_id={HEADS: (me_head + step) % heads})
    for step in range(1, rows):
        pl.semaphore_signal(barrier, inc=1, device_id={ROWS: (me_row + step) % rows})
    term_ref[...] = term_in[...]
    total = jnp.zeros((16, 384), F32)
    for share in shares:

        def add_squares(at, total, share=share):
            line = pl.ds(pl.multiple_of(at * 16, 16), 16)
            for begin in range(0, share.shape[1], 384):
                wide = share[line, begin : begin + 384].astype(F32)
                total = total + wide * wide
            return total

        total = lax.fori_loop(0, share.shape[0] // 16, add_squares, total)
    total = jnp.sum(total, axis=0, keepdims=True)
    term_ref[0, lines : lines + 1] = total[:, :128] + total[:, 128:256] + total[:, 256:]
    pl.semaphore_wait(barrier, heads - 1 + rows - 1)

    def spread(axis, me, count, source_of, slots_ref, own, send, recv):
        copies = []
        for step in range(1, count):
            peer = (me + step) % count
            copy = pltpu.make_async_remote_copy(
                src_ref=source_of(peer),
                dst_ref=slots_ref.at[me],
                send_sem=send.at[step - 1],
                recv_sem=recv.at[step - 1],
                device_id={axis: peer},
            )
            copy.start()
            copies.append(copy)
        slots_ref[pl.ds(me, 1)] = own[None]
        for copy in copies:
            copy.wait()

    def added(slots_ref, count):
        total = slots_ref[0]
        for at in range(1, count):
            total = total + slots_ref[at]
        return total

    mine = term_ref[pl.ds(me_head, 1)][0]
    spread(HEADS, me_head, heads, lambda peer: term_ref.at[peer], plane_ref, mine, *sems[0:2])
    part_ref[0] = added(plane_ref, heads)
    spread(ROWS, me_row, rows, lambda peer: part_ref.at[0], line_ref, part_ref[0], *sems[2:4])
    part_ref[1] = added(line_ref, rows)
    spread(HEADS, me_head, heads, lambda peer: part_ref.at[1], out_ref, part_ref[1], *sems[4:6])


def sum_fast(term, shares, lines, heads, rows, identity):
    block = term.shape[1:]
    return pl.pallas_call(
        functools.partial(sum_kernel, heads, rows, lines),
        out_shape=jax.ShapeDtypeStruct(term.shape, F32),
        in_specs=[vmem_spec()] * 4,
        out_specs=vmem_spec(),
        scratch_shapes=[
            pltpu.VMEM(term.shape, F32),
            pltpu.VMEM((heads, *block), F32),
            pltpu.VMEM((rows, *block), F32),
            pltpu.VMEM((2, *block), F32),
            pltpu.SemaphoreType.DMA((heads - 1,)),
            pltpu.SemaphoreType.DMA((heads - 1,)),
            pltpu.SemaphoreType.DMA((rows - 1,)),
            pltpu.SemaphoreType.DMA((rows - 1,)),
            pltpu.SemaphoreType.DMA((heads - 1,)),
            pltpu.SemaphoreType.DMA((heads - 1,)),
        ],
        compiler_params=pltpu.CompilerParams(
            collective_id=identity, has_side_effects=True, vmem_limit_bytes=16 * MIB
        ),
        cost_estimate=pl.CostEstimate(flops=0, bytes_accessed=40 * 1000 * 1000, transcendentals=0),
        name="sum_over_all",
    )(term, *shares)


def last_kernel(
    chips,
    heads,
    query_ref,
    pair_ref,
    rest_part_ref,
    near_x_ref,
    near_y_ref,
    over_x_ref,
    over_y_ref,
    slopes_ref,
    scaled_ref,
    slots_ref,
    final_ref,
    final_rest_ref,
    rows_ref,
    rest_ref,
    gain_ref,
    out_ref,
    from_x_ref,
    from_y_ref,
    new_ref,
    sums_ref,
    final_out_ref,
    back_ref,
    mine_ref,
    other_ref,
    down_ref,
    up_ref,
    landed_ref,
    final_landed_ref,
    to_x_ref,
    to_y_ref,
    add_x_ref,
    add_y_ref,
    weight_ref,
    chunk_ref,
    near_sem,
    local_sem,
    slot_send,
    slot_recv,
    final_send,
    final_recv,
    down_send,
    down_recv,
    up_send,
    up_recv,
):
    head, place = lax.axis_index(HEADS), lax.axis_index(ROWS)
    z, core = place // 2, place % 2
    sibling, above, below = place + 1 - 2 * core, place + 2, place - 2
    beside_x, beside_y = head + 1 - 2 * (head % 2), (head + 2) % heads
    has_above, has_below = z < chips - 1, z > 0
    depth = out_ref.shape[0]
    pieces = down_send.shape[1]
    cut = depth // pieces

    barrier = pltpu.get_barrier_semaphore()
    for step in range(1, heads):
        pl.semaphore_signal(barrier, inc=1, device_id={HEADS: (head + step) % heads})
    pl.semaphore_signal(barrier, inc=1, device_id={ROWS: sibling})

    for step in (2, 2 * chips - 2):
        pl.semaphore_signal(barrier, inc=1, device_id={ROWS: (place + step) % (2 * chips)})
    pl.semaphore_wait(barrier, heads + 2)

    share = rest_ref.shape[1]
    slots = start_scatter(head, heads, share, slots_ref, landed_ref, slot_send, slot_recv)
    finals = start_scatter(head, heads, share, final_ref, final_landed_ref, final_send, final_recv)
    whole = [query_ref, pair_ref, rest_part_ref]
    begins = [0]
    for ref in whole:
        begins.append(begins[-1] + ref.shape[3])
    over, keep = [], []
    for at, ref in enumerate(whole):
        lines = pl.ds(begins[at], ref.shape[3])
        copy = pltpu.make_async_remote_copy(
            src_ref=ref.at[:, 1 - core],
            dst_ref=other_ref.at[:, :, lines],
            send_sem=near_sem.at[at],
            recv_sem=near_sem.at[3 + at],
            device_id={ROWS: sibling},
        )
        copy.start()
        over.append(copy)
        copy = pltpu.make_async_copy(ref.at[:, core], mine_ref.at[:, :, lines], local_sem.at[at])
        copy.start()
        keep.append(copy)
    loads = []
    for at, (source, target) in enumerate(
        (
            (near_x_ref, to_x_ref),
            (over_y_ref, add_x_ref),
            (near_y_ref, to_y_ref),
            (over_x_ref, add_y_ref),
            (scaled_ref, weight_ref),
            (slopes_ref.at[pl.ds(0, 2)], chunk_ref),
        )
    ):
        loads.append(pltpu.make_async_copy(source, target, local_sem.at[3 + at]))
        loads[-1].start()
    medias = []
    for at, (to_ref, add_ref, from_ref, peer) in enumerate(
        ((to_x_ref, add_x_ref, from_x_ref, beside_x), (to_y_ref, add_y_ref, from_y_ref, beside_y))
    ):
        loads[2 * at].wait()
        loads[2 * at + 1].wait()
        for video in range(to_ref.shape[0]):

            def add_slopes(row, carry, to_ref=to_ref, add_ref=add_ref, video=video):
                lines = pl.ds(pl.multiple_of(row * 16, 16), 16)
                to_ref[video, lines] = (
                    to_ref[video, lines].astype(F32) + add_ref[video, lines].astype(F32)
                ).astype(BF)
                return carry

            lax.fori_loop(0, to_ref.shape[1] // 16, add_slopes, 0)
        copy = pltpu.make_async_remote_copy(
            src_ref=to_ref,
            dst_ref=from_ref,
            send_sem=near_sem.at[6 + 2 * at],
            recv_sem=near_sem.at[7 + 2 * at],
            device_id={HEADS: peer},
        )
        copy.start()
        medias.append(copy)
    for copy in keep:
        copy.wait()
    for copy in over:
        copy.wait()
    for chip in range(chips):

        def add_rows(at, carry, chip=chip):
            lines = pl.ds(pl.multiple_of(at * 16, 16), 16)
            mine_ref[chip, lines] = (
                mine_ref[chip, lines].astype(F32) + other_ref[chip, lines].astype(F32)
            ).astype(BF)
            return carry

        lax.fori_loop(0, depth // 16, add_rows, 0)

    def chain(step, piece, down):
        landed, send, recv = (down_ref, down_send, down_recv) if down else (up_ref, up_send, up_recv)
        owner = z - chips + step if down else z + chips - step
        lines = pl.ds(piece * cut, cut)
        return pltpu.make_async_remote_copy(
            src_ref=mine_ref.at[owner, lines],
            dst_ref=landed.at[step - 1, lines],
            send_sem=send.at[step - 1, piece],
            recv_sem=recv.at[step - 1, piece],
            device_id={ROWS: below if down else above},
        )

    def take(step, piece, down, owner):
        landed, recv = (down_ref, down_recv) if down else (up_ref, up_recv)
        lines = pl.ds(piece * cut, cut)
        arrival = pltpu.make_async_remote_copy(
            src_ref=mine_ref.at[z, lines],
            dst_ref=landed.at[step - 1, lines],
            send_sem=recv.at[step - 1, piece],
            recv_sem=recv.at[step - 1, piece],
            device_id={ROWS: sibling},
        )
        arrival.wait_recv()
        mine_ref[owner, lines] = (
            mine_ref[owner, lines].astype(F32) + landed[step - 1, lines].astype(F32)
        ).astype(BF)

    for step in range(1, chips):
        for piece in range(pieces):
            for down in (True, False):
                sends = (z >= chips - step) if down else (z <= step - 1)
                takes = sends & (has_above if down else has_below)
                owner = z - chips + step if down else z + chips - step

                if step > 1:

                    @pl.when(takes)
                    def _():
                        take(step - 1, piece, down, owner)

                @pl.when(sends)
                def _():
                    chain(step, piece, down).start()

    loads[4].wait()
    loads[5].wait()
    videos, patches, width = chunk_ref.shape[1:]
    tile = width // 4

    def own_slopes(at, carry):
        half = at // 4
        lines = pl.ds(pl.multiple_of((at % 4) * tile, tile), tile)
        made = mm(chunk_ref[half].reshape(videos * patches, width), weight_ref[lines], NT)
        back_ref[half, :, :, lines] = made.reshape(videos, patches, tile)
        return carry

    lax.fori_loop(0, 8, own_slopes, 0)
    rows = rows_ref[...]
    centred = rows - jnp.mean(rows, axis=-1, keepdims=True)
    scale = lax.rsqrt(jnp.mean(centred * centred, axis=-1, keepdims=True) + EPS_NORM)
    hat = centred * scale
    own_slots = pl.ds(pl.multiple_of(head * share, share), share)
    final = final_rest_ref[...] + final_ref[:, own_slots, :].astype(F32)
    for at, copy in enumerate(finals):
        copy.wait_recv()
        final = final + final_landed_ref[at].astype(F32)
    final_out_ref[...] = final
    slope = slots_ref[:, own_slots, :].astype(F32)
    for at, copy in enumerate(slots):
        copy.wait_recv()
        slope = slope + landed_ref[at].astype(F32)
    hat_slope = slope * gain_ref[0]
    back = hat_slope - jnp.mean(hat_slope, axis=-1, keepdims=True)
    back = back - hat * jnp.mean(hat_slope * hat, axis=-1, keepdims=True)
    new_ref[...] = rest_ref[...] + back * scale
    sums_ref[0:1] = jnp.sum(jnp.sum(slope * hat, axis=0), axis=0, keepdims=True)
    sums_ref[1:2] = jnp.sum(jnp.sum(slope, axis=0), axis=0, keepdims=True)

    for piece in range(pieces):

        @pl.when(has_above)
        def _():
            take(chips - 1, piece, True, z)

        @pl.when(has_below)
        def _():
            take(chips - 1, piece, False, z)

    out_ref[...] = mine_ref[z]
    for step in range(1, chips):
        for piece in range(pieces):

            @pl.when(z >= chips - step)
            def _():
                chain(step, piece, True).wait_send()

            @pl.when(z <= step - 1)
            def _():
                chain(step, piece, False).wait_send()

    for copy in slots + finals:
        copy.wait_send()
    for copy in medias:
        copy.wait()


def last_step(parts, near, over, slopes, scaled, slots, final, final_rest, rows, rest, gain, heads, chips):
    depth, columns = parts[0].shape[0] // (2 * chips), sum(part.shape[1] for part in parts)
    videos, share, width = rest.shape
    pieces = 4
    any_spec = pl.BlockSpec(memory_space=pl.ANY)
    block = pltpu.VMEM((chips, depth, columns), BF)
    steps = pltpu.VMEM((chips - 1, depth, columns), BF)
    landed = pltpu.VMEM((heads - 1, videos, share, width), BF)
    chunk = pltpu.VMEM(near[0].shape, BF)
    chain_sem = pltpu.SemaphoreType.DMA((chips - 1, pieces))
    slot_sem = pltpu.SemaphoreType.DMA((heads - 1,))
    chunk_kind = jax.ShapeDtypeStruct(near[0].shape, BF)
    return pl.pallas_call(
        functools.partial(last_kernel, chips, heads),
        out_shape=(
            jax.ShapeDtypeStruct((depth, columns), BF),
            chunk_kind,
            chunk_kind,
            jax.ShapeDtypeStruct(rest.shape, F32),
            jax.ShapeDtypeStruct((2, width), F32),
            jax.ShapeDtypeStruct(rest.shape, F32),
            jax.ShapeDtypeStruct((2, *near[0].shape), BF),
        ),
        in_specs=[any_spec] * 9 + [vmem_spec()] * 6,
        out_specs=(vmem_spec(), any_spec, any_spec) + (vmem_spec(),) * 4,
        scratch_shapes=[block, block, steps, steps, landed, landed]
        + [chunk] * 4
        + [
            pltpu.VMEM(scaled.shape, BF),
            pltpu.VMEM((2, *near[0].shape), BF),
            pltpu.SemaphoreType.DMA((10,)),
            pltpu.SemaphoreType.DMA((9,)),
        ]
        + [slot_sem] * 4
        + [chain_sem] * 4,
        compiler_params=pltpu.CompilerParams(
            collective_id=7, has_side_effects=True, vmem_limit_bytes=60 * MIB
        ),
        cost_estimate=pl.CostEstimate(flops=0, bytes_accessed=160 * 1000 * 1000, transcendentals=0),
        name="last_step",
    )(
        *[part.reshape(chips, 2, depth, part.shape[1]) for part in parts],
        *near,
        *over,
        slopes,
        scaled,
        slots,
        final,
        final_rest,
        rows,
        rest,
        gain,
    )


def media_back_kernel(own_ref, back_ref, *refs):
    first, second, out_ref = refs[:2], refs[2:4], refs[-1]

    def write(*terms):
        rows = own_ref[0].astype(F32)
        centred = rows - jnp.mean(rows, axis=-1, keepdims=True)
        spread = lax.rsqrt(jnp.mean(centred * centred, axis=-1, keepdims=True) + EPS_NORM)
        hat = centred * spread
        total = functools.reduce(jnp.add, [term[...].astype(F32) for term in terms], back_ref[0].astype(F32))
        total = total - jnp.mean(total, axis=-1, keepdims=True) - hat * jnp.mean(total * hat, axis=-1, keepdims=True)
        total = total * spread
        for video in range(rows.shape[0]):
            out_ref[:, video, :] = total[video]

    @pl.when(pl.program_id(0) == 0)
    def _():
        write(*first)

    @pl.when(pl.program_id(0) == 1)
    def _():
        write(*second)


def media_back(own, back, in_x, in_y):
    _, videos, rows, width = own.shape
    cut = 64
    steps = rows // cut
    both = pl.BlockSpec((1, videos, cut, width), lambda i, j: (i, 0, j, 0))
    specs = [pl.BlockSpec((videos, cut, width), lambda i, j: (0, jnp.where(i == 0, j, steps - 1), 0))] * 2
    specs += [pl.BlockSpec((videos, cut, width), lambda i, j: (0, jnp.where(i == 1, j, 0), 0))] * 2
    return pl.pallas_call(
        media_back_kernel,
        grid=(2, steps),
        out_shape=jax.ShapeDtypeStruct((2 * rows, videos, width), F32),
        in_specs=[both, both] + specs,
        out_specs=pl.BlockSpec((cut, videos, width), lambda i, j: (steps * i + j, 0, 0)),
        compiler_params=pltpu.CompilerParams(vmem_limit_bytes=60 * MIB),
        cost_estimate=pl.CostEstimate(flops=0, bytes_accessed=30 * 1000 * 1000, transcendentals=0),
        name="media_back",
    )(own, back, in_x[0], in_y[0], in_x[1], in_y[1])


def adam_kernel(rates, begins, factor_ref, *refs):
    kinds, step = len(rates), pl.program_id(0)
    layers = (len(refs) // kinds) - 7
    factor = factor_ref[0, 0]
    ins = [refs[at * (3 + layers) : (at + 1) * (3 + layers)] for at in range(kinds)]
    outs = [refs[kinds * (3 + layers) + 4 * at :][:4] for at in range(kinds)]
    for kind in range(kinds):
        steps = (begins[kind + 1] - begins[kind]) // layers
        weight_ref, first_ref, second_ref = ins[kind][:3]
        mean_ref, square_ref, next_ref, copy_ref = outs[kind]
        columns = weight_ref.shape[3]
        for layer in range(layers):
            begin = begins[kind] + layer * steps

            @pl.when((step >= begin) & (step < begin + steps))
            def _():
                for part in range(weight_ref.shape[1]):
                    grad = ins[kind][3 + layer][:, part * columns : (part + 1) * columns]
                    scaled = grad.astype(F32) * factor
                    mean = BETA_ONE * first_ref[0, part] + (1.0 - BETA_ONE) * scaled
                    square = BETA_TWO * second_ref[0, part] + (1.0 - BETA_TWO) * scaled * scaled
                    root = jnp.sqrt(square * (1.0 / (1.0 - BETA_TWO**STEP))) + ADAM_EPS
                    change = (mean * (1.0 / (1.0 - BETA_ONE**STEP))) / root
                    weight = weight_ref[0, part]
                    weight = weight - rates[kind] * (change + WEIGHT_DECAY * weight)
                    mean_ref[0, part] = mean
                    square_ref[0, part] = square
                    next_ref[0, part] = weight
                    copy_ref[0, part] = weight.astype(BF)


def adam_fast(kinds, factor):
    layers = kinds[0][0].shape[0]
    begins = [0]
    for weight, _, _, _, cut, _ in kinds:
        begins.append(begins[-1] + layers * (weight.shape[2] // cut))
    operands, in_specs, out_specs, out_shape = [], [], [], []
    for kind, (weight, first, second, grads, cut, _) in enumerate(kinds):
        _, parts, rows, columns = weight.shape
        steps = rows // cut
        begin, end = begins[kind], begins[kind + 1]

        def place(i, begin=begin, end=end, steps=steps):
            at = jnp.clip(i, begin, end - 1) - begin
            return (at // steps, 0, at % steps, 0)

        spec = pl.BlockSpec((1, parts, cut, columns), place)
        operands += [weight, first, second]
        in_specs += [spec] * 3
        for layer, (grad, base) in enumerate(grads):

            def grad_place(i, begin=begin + layer * steps, steps=steps, base=base):
                return (jnp.clip(i, begin, begin + steps - 1) - begin, base)

            operands.append(grad)
            in_specs.append(pl.BlockSpec((cut, parts * columns), grad_place))
        wide = jax.ShapeDtypeStruct(weight.shape, F32)
        out_specs += [spec] * 4
        out_shape += [wide, wide, wide, jax.ShapeDtypeStruct(weight.shape, BF)]
    size = sum(kind[0].size for kind in kinds)
    made = pl.pallas_call(
        functools.partial(adam_kernel, [kind[-1] for kind in kinds], begins),
        grid=(begins[-1],),
        out_shape=tuple(out_shape),
        in_specs=[pl.BlockSpec(memory_space=pltpu.SMEM)] + in_specs,
        out_specs=tuple(out_specs),
        compiler_params=pltpu.CompilerParams(vmem_limit_bytes=60 * MIB),
        cost_estimate=pl.CostEstimate(flops=20 * size, bytes_accessed=28 * size, transcendentals=size),
        name="adam",
    )(factor, *operands)
    return [made[4 * at : 4 * at + 4] for at in range(len(kinds))]


def flat(rows):
    return rows.reshape(-1, rows.shape[-1])


def local_fast(
    media,
    latents,
    frame_count,
    cotangent,
    inward,
    inward_first,
    inward_second,
    outward,
    outward_first,
    outward_second,
    widen,
    widen_first,
    widen_second,
    narrow,
    narrow_first,
    narrow_second,
    norm_gains,
    gain_first,
    gain_second,
):
    heads_count, rows_count = lax.axis_size(HEADS), lax.axis_size(ROWS)
    me = lax.axis_index(HEADS)
    layers, _, row_share, head_columns = inward.shape
    local_positions, videos, width = media.shape
    latent_count = latents.shape[1] * heads_count
    scale = HD ** (-0.5)

    def swap_x(rows):
        return lax.ppermute(rows, HEADS, X_SWAP)

    def swap_y(rows):
        return lax.ppermute(rows, HEADS, Y_SWAP)

    def gather_rows(rows):
        return lax.all_gather(rows, ROWS, axis=0, tiled=True)

    outward_t, narrow_t = (jnp.swapaxes(outward, 1, 2), jnp.swapaxes(narrow, 1, 2))
    columns, units = head_columns, widen.shape[2]
    first_set = [inward[l, t] for l in range(layers) for t in (1, 2)]
    first_set = first_set + [inward[l, 0] for l in range(layers)] + [outward_t[l] for l in range(layers)]
    first_set = jnp.concatenate([piece.astype(BF) for piece in first_set], axis=1)

    latent = latents
    normed = layer_norm(latent, norm_gains[0, 2], norm_gains[0, 3]).astype(BF)
    slope_rows = cotangent.astype(BF)
    first_set = gather_rows(first_set)
    pair_weights = first_set[:, : 2 * layers * columns]
    begin = 2 * layers * columns
    query_full = [first_set[:, begin + l * columns : begin + (l + 1) * columns] for l in range(layers)]
    begin = begin + layers * columns
    out_full = [first_set[:, begin + l * columns : begin + (l + 1) * columns] for l in range(layers)]
    share = latents.shape[1]
    own = jnp.swapaxes(media.reshape(2, local_positions // 2, videos, width), 1, 2)
    later_sets = [
        jnp.concatenate((widen[layer].astype(BF), narrow_t[layer].astype(BF)), axis=1) for layer in range(layers)
    ]
    own, *later_sets = lax.optimization_barrier((own, *later_sets))
    later_sets = [gather_rows(rows) for rows in later_sets]
    widen_full = [rows[:, :units] for rows in later_sets]
    narrow_full = [rows[:, units:] for rows in later_sets]

    frames = jnp.stack([2 * (me ^ group) + half for group in range(4) for half in range(2)])
    live = (frames[None, :] < frame_count[:, None]).astype(jnp.int32)
    media_gains = norm_gains[:, 0:2]
    near, latent_norm = gather_near(own, normed, heads_count)
    keys, media_hat, far = media_near(own, near, media_gains, first_set, 2 * layers * columns, heads_count)
    keys, media_hat, feed_slope = media_far(far, media_gains, first_set, slope_rows, keys, media_hat, heads_count)
    scaled = jnp.concatenate(
        [
            (
                pair_weights[:, 2 * l * head_columns : 2 * (l + 1) * head_columns].astype(F32)
                * norm_gains[l, 0][:, None]
            ).astype(BF)
            for l in range(layers)
        ],
        axis=1,
    )

    kept = []
    for layer in range(layers):
        query_weight, out_weight = query_full[layer], out_full[layer]
        pair_weight = pair_weights[:, 2 * layer * head_columns : 2 * (layer + 1) * head_columns]
        query = mm(flat(latent_norm), query_weight)
        latent_pair = mm(flat(latent_norm), pair_weight)
        mixed = attend_fast(live, query, latent_pair, keys, layer, scale)
        part = mm(mixed, out_weight, NT).reshape(videos, latent_count, width)
        if layer == layers - 1:
            gain_rows = [rows.reshape(-1, width) for rows in (norm_gains, gain_first, gain_second)]
            part, scaled, *gain_rows = lax.optimization_barrier((part, scaled, *gain_rows))
        middle, feed_norm = forward_exchange(part, latent, norm_gains[layer, 4:6], heads_count)
        hidden_pre = mm(flat(feed_norm), widen_full[layer], None, F32)
        hidden = jax.nn.gelu(hidden_pre).astype(BF)
        part = mm(hidden, narrow_full[layer], NT).reshape(videos, latent_count, width)
        last = layer == layers - 1
        gain = norm_gains[0 if last else layer + 1, 2:4]
        kept.append((latent, middle, latent_norm, query, latent_pair, mixed, feed_norm, hidden_pre, hidden))
        if last:
            final_part, final_rest = part, middle
        else:
            latent, latent_norm = forward_exchange(part, middle, gain, heads_count)

    slope = cotangent
    gain_parts = [None] * layers
    shares, waiting = [], []
    media_slopes = ()

    def hat_slope(slopes, group, half):
        return mm(flat(slopes[2 * group + half]), scaled, NT).reshape(videos, -1, width)

    summed = []

    def scatter_rows(gradient):
        if summed:
            gradient, _ = lax.optimization_barrier((gradient, summed[-1]))
        summed.append(lax.psum_scatter(gradient, ROWS, scatter_dimension=0, tiled=True))
        return summed[-1]

    for layer in reversed(range(layers)):
        latent_in, middle, latent_norm, query, latent_pair, mixed, feed_norm, hidden_pre, hidden = kept[layer]
        query_weight, out_weight = query_full[layer], out_full[layer]
        pair_weight = pair_weights[:, 2 * layer * head_columns : 2 * (layer + 1) * head_columns]
        feed_slope = flat(feed_slope)
        hidden_slope = mm(feed_slope, narrow_full[layer], None, F32)
        _, gelu_back = jax.vjp(jax.nn.gelu, hidden_pre)
        pre_slope = gelu_back(hidden_slope)[0].astype(BF)
        part = mm(pre_slope, widen_full[layer], NT).reshape(videos, latent_count, width)
        feed_grad = product_pair(feed_slope, hidden, flat(feed_norm), pre_slope, *waiting)
        part, feed_grad = lax.optimization_barrier((part, feed_grad))
        shares.append(scatter_rows(feed_grad))
        middle_slope, feed_sums, branch_slope = backward_exchange(
            part, middle, slope, norm_gains[layer, 4:6], heads_count
        )
        branch_slope = flat(branch_slope)
        mixed_slope = mm(branch_slope, out_weight)
        out_grad = mm(branch_slope, mixed, TN)
        query_slope, latent_slopes, media_slopes, slope_sums = attend_back_fast(
            live, query, latent_pair, keys, mixed_slope, layer, scale, (media_slopes,) if layer < layers - 1 else ()
        )
        part = (mm(query_slope, query_weight, NT, F32) + mm(latent_slopes, pair_weight, NT, F32)).astype(BF)
        part = part.reshape(videos, latent_count, width)
        last = layer == 0
        if not last:
            slope, latent_sums, feed_slope = backward_exchange(
                part, latent_in, middle_slope, norm_gains[layer, 2:4], heads_count
            )
        else:
            last_part = part
            far = [hat_slope(media_slopes, 3, half) for half in range(2)]
            media_slopes, *far = lax.optimization_barrier((media_slopes, *far))
            over_x, over_y = swap_x(far[0]), swap_y(far[1])
            near = [hat_slope(media_slopes, 1, 0), hat_slope(media_slopes, 2, 1)]
            media_slopes, *near = lax.optimization_barrier((media_slopes, *near))
            in_x, in_y = [swap_x(near[0]), None], [None, swap_y(near[1])]
            near = [hat_slope(media_slopes, 1, 1), hat_slope(media_slopes, 2, 0)]
            media_slopes, *near = lax.optimization_barrier((media_slopes, *near))
        query_grad = mm(flat(latent_norm), query_slope, TN)
        pair_slope = flat(media_slopes[..., 2 * layer * head_columns : 2 * (layer + 1) * head_columns])
        hat_grad = mm(flat(media_hat), pair_slope, TN, F32)
        slope_sum = jnp.sum(slope_sums[:, 0], axis=0)
        gain, shift = norm_gains[layer, 0], norm_gains[layer, 1]
        pair_grad = (
            mm(flat(latent_norm), latent_slopes, TN, F32)
            + gain[:, None] * hat_grad
            + shift[:, None] * slope_sum[None, :]
        ).astype(BF)
        wide = pair_weight.astype(F32)
        media_sums = jnp.stack(
            (jnp.sum(wide * hat_grad, axis=1), jnp.sum(wide * slope_sum[None, :], axis=1))
        )
        parts = (query_grad, pair_grad, out_grad)
        if last:
            *parts, over_x, over_y, near[0], near[1] = lax.optimization_barrier((*parts, over_x, over_y, *near))
        waiting = parts
        gain_parts[layer] = [media_sums, None if last else latent_sums, feed_sums]

    share_out, in_x[1], in_y[0], slope, gain_parts[0][1], latent, back = last_step(
        *(parts, near, (over_x, over_y), media_slopes, scaled),
        *(last_part, final_part, final_rest, latents, middle_slope, norm_gains[0, 2:4]),
        *(heads_count, rows_count // 2),
    )
    media_slope = media_back(own, back, in_x, in_y)

    shares.append(share_out)
    gain_term = jnp.concatenate([rows for parts in gain_parts for rows in parts], axis=0).reshape(heads_count, -1, 128)
    lines = gain_term.shape[1]
    gain_term = jnp.pad(gain_term, ((0, 0), (0, 8 - lines % 8), (0, 0)))
    totals = sum_fast(gain_term, shares, lines, heads_count, rows_count, 9)
    gain_total = totals[:, :lines].reshape(layers, 6, width)
    square_total = jnp.sum(totals[0, lines]) + jnp.sum(totals[:, :lines] * totals[:, :lines])
    gradient_norm = jnp.sqrt(square_total)
    factor = CLIP_LEVEL / jnp.maximum(gradient_norm, CLIP_LEVEL)

    factor_cell = factor.reshape(1, 1)
    early_share, middle_share, late_share = shares
    depth = widen.shape[1]

    def turned(*arrays):
        return [jnp.swapaxes(rows, 1, 2)[:, None] for rows in arrays]

    def turn_back(arrays):
        return [jnp.swapaxes(rows[:, 0], 1, 2) for rows in arrays]

    inward_made, outward_made, widen_made, narrow_made = adam_fast(
        (
            (
                *(inward, inward_first, inward_second),
                [(late_share, 0), (middle_share, 0)],
                *(depth, RATE_INWARD),
            ),
            (
                *turned(outward, outward_first, outward_second),
                [(late_share, 3), (middle_share, 3)],
                *(depth, RATE_OUTWARD),
            ),
            (
                *[rows[:, None] for rows in (widen, widen_first, widen_second)],
                [(middle_share, 1 + 4 * columns // units), (early_share, 1)],
                *(depth // 2, RATE_WIDEN),
            ),
            (
                *turned(narrow, narrow_first, narrow_second),
                [(middle_share, 4 * columns // units), (early_share, 0)],
                *(depth // 2, RATE_NARROW),
            ),
        ),
        factor_cell,
    )
    results = [latent, slope, media_slope, gradient_norm, *inward_made, *turn_back(outward_made)]
    results += [rows[:, 0] for rows in widen_made] + turn_back(narrow_made)
    made = adam_step(*gain_rows, gain_total.reshape(-1, width) * factor, RATE_GAINS, 0.0)
    results = results + [rows.reshape(norm_gains.shape) for rows in made] + [gain_total[:, 4:6]]
    return tuple(results)


def solution(mesh):
    placed = (
        P(HEADS, ROWS, None),
        P(ROWS, HEADS, None),
        P(ROWS),
        P(ROWS, HEADS, None),
        P(None, None, ROWS, HEADS),
        P(None, None, ROWS, HEADS),
        P(None, None, ROWS, HEADS),
        P(None, HEADS, ROWS),
        P(None, HEADS, ROWS),
        P(None, HEADS, ROWS),
        P(None, ROWS, HEADS),
        P(None, ROWS, HEADS),
        P(None, ROWS, HEADS),
        P(None, HEADS, ROWS),
        P(None, HEADS, ROWS),
        P(None, HEADS, ROWS),
        P(),
        P(),
        P(),
    )
    local = local_fast if (mesh.shape[ROWS], mesh.shape[HEADS]) == (8, 4) else local_plain
    return jax.shard_map(
        local,
        mesh=mesh,
        in_specs=placed,
        out_specs=(
            P(ROWS, HEADS, None),
            P(ROWS, HEADS, None),
            P(HEADS, ROWS, None),
            P(),
            P(None, None, ROWS, HEADS),
            P(None, None, ROWS, HEADS),
            P(None, None, ROWS, HEADS),
            P(None, None, ROWS, HEADS),
            P(None, HEADS, ROWS),
            P(None, HEADS, ROWS),
            P(None, HEADS, ROWS),
            P(None, HEADS, ROWS),
            P(None, ROWS, HEADS),
            P(None, ROWS, HEADS),
            P(None, ROWS, HEADS),
            P(None, ROWS, HEADS),
            P(None, HEADS, ROWS),
            P(None, HEADS, ROWS),
            P(None, HEADS, ROWS),
            P(None, HEADS, ROWS),
            P(),
            P(),
            P(),
            P(),
        ),
        check_vma=False,
    )
```
